32 devices in a mesh: row: 8 (over z, y), col: 4 (over x, core).
Axes of the slice: x: 2, y: 2, z: 4, core: 2. Of those that a mesh axis runs over, the one named last changes fastest.
Arguments:
- right_sides: bfloat16 [32768, 256], P(('row', 'col')), may hold values from -6 to 6
- tree_order: int32 [32768], P(('row', 'col')), may hold values from 0 to 32767, as said below
- leaf_inverse: bfloat16 [32, 2, 1024, 1024], P(('row', 'col'))
- leaf_basis: bfloat16 [32, 2, 1024, 256], P(('row', 'col')), may hold values from -0.125 to 0.125
- leaf_lift: bfloat16 [32, 2, 1024, 256], P(('row', 'col')), may hold values from -0.1875 to 0.1875
- node_inverse: bfloat16 [32, 5, 2, 512, 512], P(('row', 'col')), as said below
- node_basis: bfloat16 [32, 4, 2, 512, 256], P(('row', 'col')), as said below
- node_lift: bfloat16 [32, 4, 2, 512, 256], P(('row', 'col')), as said below
Outputs:
- solution: float32 [32768, 256], P(('row', 'col'))
The draws below stay inside these ranges and needn't reach their ends.
Inputs may be any that keep to these rules, and one draw needn't show every extreme that they name: tree_order is a permutation. Initial row i lies on device i div 1024 and goes to device tree_order[i] div 1024; the number of rows that a device sends to the device o places further along row+col (cyclically) depends only on o, is at most 64, and reaches 64 for some o. node_inverse[d, k - 1] is the same for all d with the same d div 2^k. node_basis[d, k - 1] is the same for all d with the same d div 2^k. node_lift[d, k - 1] is the same for all d with the same d div 2^k.
All inputs are finite; a program needn't handle non-finite values.
Results may differ from the reference program's by a relative error of at most 0.0003.
Values may be sent and summed in bfloat16 or wider, within the bound.
No kernel may reach another device: no remote copies, remote signals or barrier semaphores. Data moves between devices by JAX's collectives and lax.ppermute only.
A program may use at most 128 MiB of HBM per device.

```python
import jax
import jax.numpy as jnp
from jax import lax

LEAF = 1024
RANK = 256
RHS = 128
LEVELS = 5
UNKNOWNS = 32768
SPREAD = 32
DEVICES = 32


def noise_block(key, shape, fan_in):
    values = jax.random.normal(key, shape, jnp.float32)
    return values * fan_in ** (-0.5)


def inverse_block(key, leading, order_size):
    values = 0.6 * noise_block(key, leading + (2, order_size, order_size), 2 * order_size)
    identity = 0.8 * jnp.eye(order_size, dtype=jnp.float32)
    return jnp.stack([values[..., 0, :, :] + identity, values[..., 1, :, :]], axis=-3)


def make_inverse(sub_key, leading):
    return inverse_block(sub_key, leading, 2 * RANK)


def make_factor(sub_key, leading):
    return noise_block(sub_key, leading + (2, 2 * RANK, RANK), 4 * RANK)


def ancestor_copies(key, height_total, maker):
    copies = []
    owners_base = jnp.arange(DEVICES, dtype=jnp.int32)
    for height in range(1, height_total + 1):
        blocks = maker(jax.random.fold_in(key, height), (DEVICES // 2 ** height,))
        copies.append(blocks[owners_base // 2 ** height])
    return jnp.stack(copies, axis=1)


def draw_leaf_inverse(key, part):
    return inverse_block(jax.random.fold_in(key, 3), (DEVICES,), LEAF).astype(jnp.bfloat16)


def draw_node_inverse(key, part):
    return ancestor_copies(jax.random.fold_in(key, 5), LEVELS, make_inverse).astype(jnp.bfloat16)


def draw_node_basis(key, part):
    return ancestor_copies(jax.random.fold_in(key, 9), LEVELS - 1, make_factor).astype(jnp.bfloat16)


def draw_node_lift(key, part):
    return ancestor_copies(jax.random.fold_in(key, 13), LEVELS - 1, make_factor).astype(jnp.bfloat16)


def shuffle_rows(sub_key):
    return jax.random.permutation(sub_key, LEAF).astype(jnp.int32)


def draw_tree_order(key, part):
    first_key, second_key, third_key = jax.random.split(jax.random.fold_in(key, 7), 3)
    unit_rows = LEAF // (2 * SPREAD)
    pattern = jnp.array([4, 0, 3, 1], jnp.int32) * unit_rows
    spread_counts = jnp.tile(pattern, SPREAD // 4)
    shuffled = jax.random.permutation(first_key, DEVICES).astype(jnp.int32)
    rank_of = jnp.zeros((DEVICES,), jnp.int32).at[shuffled].set(jnp.arange(DEVICES, dtype=jnp.int32))
    every_offset = jnp.arange(DEVICES, dtype=jnp.int32)
    scores = rank_of + 3
    scores = jnp.where(every_offset == DEVICES // 2, 0, scores)
    scores = jnp.where(every_offset == 1, 1, scores)
    scores = jnp.where(every_offset == DEVICES - 1, 2, scores)
    chosen = jnp.argsort(scores, stable=True).astype(jnp.int32)[:SPREAD]
    arranged = jnp.concatenate([chosen[0:1], chosen[3:4], chosen[1:3], chosen[4:]])
    counts = jnp.zeros((DEVICES,), jnp.int32).at[arranged].set(spread_counts)
    offset_of_rank = jnp.repeat(jnp.arange(DEVICES, dtype=jnp.int32), counts, total_repeat_length=LEAF)
    source_ranks = jax.vmap(shuffle_rows)(jax.random.split(second_key, DEVICES))
    target_places = jax.vmap(shuffle_rows)(jax.random.split(third_key, DEVICES))
    sources = jnp.arange(DEVICES, dtype=jnp.int32)[:, None]
    targets = (sources + offset_of_rank[source_ranks]) % DEVICES
    places = target_places[targets, source_ranks]
    return (targets * LEAF + places).reshape(DEVICES * LEAF).astype(jnp.int32)


def level_of(own_key, extent, pieces, low, top_value):
    level = 1.0
    for axis_at, shards_of in pieces:
        draws = jax.random.uniform(jax.random.fold_in(jax.random.fold_in(own_key, 6), axis_at), (shards_of,), jnp.float32, low / len(pieces), top_value / len(pieces))
        level = level * jnp.repeat(jnp.exp(draws), extent[axis_at] // shards_of).reshape((-1,) + (1,) * (len(extent) - 1 - axis_at))
    return level


def gaussian(stream_key, dims, width, limit, cuts=(), held_as=jnp.bfloat16):
    gain = level_of(stream_key, dims, cuts, -0.22, 0.18) if cuts else 1.0
    entries = jax.random.normal(stream_key, dims, jnp.float32) * width * gain
    return jnp.minimum(jnp.maximum(entries, -limit), limit).astype(held_as)


def setup_inputs(seed: int = 0) -> dict:
    streams_of = jax.random.split(jax.random.key(seed), 9)
    right_sides = gaussian(streams_of[0], (UNKNOWNS, 2 * RHS), 1.0, 6.0, ((0, 32),))
    tree_order = draw_tree_order(jax.random.fold_in(streams_of[8], 71), 0)
    leaf_inverse = draw_leaf_inverse(jax.random.fold_in(streams_of[8], 71), 0)
    leaf_basis = gaussian(streams_of[3], (DEVICES, 2, LEAF, RANK), (2 * LEAF) ** -0.5, 0.125, ((0, 32),))
    leaf_lift = gaussian(streams_of[4], (DEVICES, 2, LEAF, RANK), (4 * RANK) ** -0.5, 0.1875, ((0, 32),))
    node_inverse = draw_node_inverse(jax.random.fold_in(streams_of[8], 71), 0)
    node_basis = draw_node_basis(jax.random.fold_in(streams_of[8], 71), 0)
    node_lift = draw_node_lift(jax.random.fold_in(streams_of[8], 71), 0)
    return dict(right_sides=right_sides, tree_order=tree_order, leaf_inverse=leaf_inverse, leaf_basis=leaf_basis, leaf_lift=leaf_lift, node_inverse=node_inverse, node_basis=node_basis, node_lift=node_lift)


exactness = lax.Precision.HIGHEST


def rotated(vectors):
    middle = vectors.shape[-1] // 2
    return jnp.concatenate([-vectors[..., middle:], vectors[..., :middle]], axis=-1)


def apply_complex(matrix, vectors):
    real_part = matrix[..., 0, :, :].astype(jnp.float32)
    imag_part = matrix[..., 1, :, :].astype(jnp.float32)
    plain = jnp.einsum("...ab,...bc->...ac", real_part, vectors, precision=exactness)
    return plain + jnp.einsum("...ab,...bc->...ac", imag_part, rotated(vectors), precision=exactness)


def apply_transposed(matrix, vectors):
    real_part = matrix[..., 0, :, :].astype(jnp.float32)
    imag_part = matrix[..., 1, :, :].astype(jnp.float32)
    plain = jnp.einsum("...ba,...bc->...ac", real_part, vectors, precision=exactness)
    return plain + jnp.einsum("...ba,...bc->...ac", imag_part, rotated(vectors), precision=exactness)


def leaf_phase(inputs):
    inverse_matrix, basis_matrix, leaf_rows = inputs
    leaf_sol = apply_complex(inverse_matrix, leaf_rows)
    return leaf_sol, apply_transposed(basis_matrix, leaf_sol)


def leaf_finish(inputs):
    lift_block, leaf_sol, leaf_coef, own_half = inputs
    return leaf_sol - apply_complex(lift_block, leaf_coef - own_half)


def reference(right_sides, tree_order, leaf_inverse, leaf_basis, leaf_lift, node_inverse, node_basis, node_lift):
    devices = leaf_inverse.shape[0]
    vector_width = right_sides.shape[1]
    levels = node_inverse.shape[1]
    placed = jnp.zeros(right_sides.shape, jnp.float32).at[tree_order].set(right_sides.astype(jnp.float32))
    leaf_rows = placed.reshape(devices, LEAF, vector_width)
    leaf_sol, leaf_coef = lax.map(leaf_phase, (leaf_inverse, leaf_basis, leaf_rows))
    upward = leaf_coef
    solutions = []
    coefficients = []
    for height in range(1, levels + 1):
        node_count = devices // (2 ** height)
        owners = jnp.arange(node_count, dtype=jnp.int32) * (2 ** height)
        node_rhs = upward.reshape(node_count, 2 * RANK, vector_width)
        node_sol = apply_complex(node_inverse[owners, height - 1], node_rhs)
        solutions.append(node_sol)
        if height < levels:
            upward = apply_transposed(node_basis[owners, height - 1], node_sol)
            coefficients.append(upward)
    top_down = solutions[levels - 1]
    for height in range(levels - 1, 0, -1):
        node_count = devices // (2 ** height)
        owners = jnp.arange(node_count, dtype=jnp.int32) * (2 ** height)
        halves = top_down.reshape(node_count, RANK, vector_width)
        top_down = solutions[height - 1] - apply_complex(node_lift[owners, height - 1], coefficients[height - 1] - halves)
    halves = top_down.reshape(devices, RANK, vector_width)
    tree_solution = lax.map(leaf_finish, (leaf_lift, leaf_sol, leaf_coef, halves))
    return tree_solution.reshape(devices * LEAF, vector_width)[tree_order]
```

```python
import functools

import jax
import jax.numpy as jnp
from jax import lax
from jax.experimental import pallas as pl
from jax.experimental.pallas import tpu as pltpu
from jax.sharding import PartitionSpec as P

LANES = 128
EXTRA = 16
CODE_BASE = 32
SCALE_STEPS = 64
BF16 = jnp.bfloat16
F32 = jnp.float32


def matmul(a, b):
    return lax.dot_general(a, b, (((1,), (0,)), ((), ())), preferred_element_type=F32)


def matmul_t(a, b):
    return lax.dot_general(a, b, (((0,), (0,)), ((), ())), preferred_element_type=F32)


def matmul_nt(a, b):
    return lax.dot_general(a, b, (((1,), (1,)), ((), ())), preferred_element_type=F32)


def iota(shape, dim):
    return lax.broadcasted_iota(jnp.int32, shape, dim)


def rotated(half):
    low = iota(half.shape, 1) < LANES // 2
    turned = pltpu.roll(half, LANES // 2, 1)
    return jnp.where(low, -turned, turned)


def rotated_all(x):
    return jnp.concatenate(
        [rotated(x[:, at : at + LANES]) for at in range(0, x.shape[1], LANES)], axis=1
    )


def swapped(first, second):
    low = iota(first.shape, 1) < LANES // 2
    return (
        jnp.where(low, first, pltpu.roll(second, LANES // 2, 1)),
        jnp.where(low, pltpu.roll(first, LANES // 2, 1), second),
    )


def two_parts(x):
    high = x.astype(BF16)
    low = (x - high.astype(F32)).astype(BF16)
    return jnp.concatenate([high, low], axis=1)


def folded(both):
    width = both.shape[1] // 2
    return both[:, :width] + both[:, width:]


def apply_complex(real, imag, x):
    turned = rotated_all(x)
    return folded(matmul(real, two_parts(x)) + matmul(imag, two_parts(turned)))


def apply_transposed(real, imag, x):
    turned = rotated_all(x)
    return folded(matmul_t(real, two_parts(x)) + matmul_t(imag, two_parts(turned)))


def unit_of(code):
    return jnp.exp2(code * (1.0 / SCALE_STEPS) - 15.0)


def inverse_unit_of(code):
    return jnp.exp2(15.0 - code * (1.0 / SCALE_STEPS))


def scale_code(x):
    largest = jnp.max(jnp.abs(x), axis=0, keepdims=True)
    return jnp.ceil(jnp.log2(jnp.maximum(largest, 2.0**-110)) * SCALE_STEPS)


def pack_kernel(me_ref, order_ref, rows_ref, send_ref, slot_ref, *, devices, capacity):
    leaf_rows = rows_ref.shape[0]
    order = order_ref[...]
    target = order // leaf_rows
    position = order - target * leaf_rows
    hits = (iota((devices, leaf_rows), 0) == target).astype(F32)
    upper = (iota((leaf_rows, leaf_rows), 0) < iota((leaf_rows, leaf_rows), 1)).astype(F32)
    before = matmul(hits.astype(BF16), upper.astype(BF16))
    rank = jnp.sum(hits * before, axis=0, keepdims=True).astype(jnp.int32)
    slot = target * capacity + rank
    slot_ref[...] = slot
    rows = rows_ref[...].astype(F32)
    first, second = swapped(rows[:, :LANES], rows[:, LANES:])
    rows = jnp.concatenate([first, second], axis=1).astype(BF16)
    chosen = (iota((devices * capacity, leaf_rows), 0) == slot).astype(F32).astype(BF16)
    sent = matmul(chosen, rows).astype(BF16)
    send_ref[:, :capacity, :] = sent[:, :LANES].reshape(devices, capacity, LANES)
    send_ref[:, capacity : 2 * capacity, :] = sent[:, LANES:].reshape(devices, capacity, LANES)
    group = LANES // capacity
    lane = rank + lax.rem(me_ref[0], group) * capacity
    code = position + 1
    high = code // CODE_BASE
    low = code - high * CODE_BASE
    codes = jnp.concatenate([hits * high.astype(F32), hits * low.astype(F32)], axis=0)
    places = (iota((LANES, leaf_rows), 0) == lane).astype(F32).astype(BF16)
    spread = matmul_nt(codes.astype(BF16), places)
    eight = (devices, EXTRA // 2, LANES)
    send_ref[:, 2 * capacity :, :] = jnp.concatenate(
        [
            jnp.broadcast_to(spread[:devices].reshape(devices, 1, LANES), eight),
            jnp.broadcast_to(spread[devices:].reshape(devices, 1, LANES), eight),
        ],
        axis=1,
    ).astype(BF16)


def positions(got_ref, devices, capacity):
    group = LANES // capacity
    extra = got_ref[:, 2 * capacity :, :].astype(F32)
    code = extra[:, 0, :] * CODE_BASE + extra[:, EXTRA // 2, :]
    return jnp.sum(code.reshape(devices // group, group, LANES), axis=1) - 1.0


def leaf_kernel(got_ref, inverse_ref, basis_ref, sol_ref, coef_ref, place_ref, *, devices, capacity):
    leaf_rows = sol_ref.shape[0]
    place = positions(got_ref, devices, capacity)
    place_ref[...] = place
    where_to = iota((leaf_rows, LANES), 0).astype(F32)
    chosen = jnp.concatenate(
        [
            (where_to == place[k : k + 1, :]).astype(F32).astype(BF16)
            for k in range(place.shape[0])
        ],
        axis=1,
    )
    slots = devices * capacity
    got = jnp.concatenate(
        [
            got_ref[:, :capacity, :].reshape(slots, LANES),
            got_ref[:, capacity : 2 * capacity, :].reshape(slots, LANES),
        ],
        axis=1,
    )
    placed = matmul(chosen, got)
    turned = rotated_all(placed)
    sol = matmul(inverse_ref[0], placed.astype(BF16)) + matmul(inverse_ref[1], turned.astype(BF16))
    sol_ref[...] = sol
    coef_ref[...] = apply_transposed(basis_ref[0], basis_ref[1], sol)


def node_rhs(upper, own, partner):
    is_upper = upper == 1
    return jnp.concatenate(
        [jnp.where(is_upper, partner, own), jnp.where(is_upper, own, partner)], axis=0
    )


def node_kernel(bit_ref, own_ref, partner_ref, inverse_ref, basis_ref, sol_ref, coef_ref):
    rhs = node_rhs(bit_ref[0], own_ref[...], partner_ref[...])
    sol = apply_complex(inverse_ref[0], inverse_ref[1], rhs)
    sol_ref[...] = sol
    coef_ref[...] = apply_transposed(basis_ref[0], basis_ref[1], sol)


def half_of(bit, x):
    rank = x.shape[0] // 2
    return jnp.where(bit == 1, x[rank:], x[:rank])


def descent_kernel(bits_ref, own_ref, partner_ref, inverse_ref, lift_ref, *refs):
    levels = bits_ref.shape[0]
    sols = refs[: levels - 1]
    coefs = refs[levels - 1 : 2 * levels - 2]
    mine_ref, other_ref = refs[2 * levels - 2 :]
    rhs = node_rhs(bits_ref[levels - 1], own_ref[...], partner_ref[...])
    down = apply_complex(inverse_ref[0], inverse_ref[1], rhs)
    for height in range(levels - 1, 0, -1):
        gap = coefs[height - 1][...] - half_of(bits_ref[height], down)
        down = sols[height - 1][...] - apply_complex(
            lift_ref[height - 1, 0], lift_ref[height - 1, 1], gap
        )
    mine_ref[...] = half_of(bits_ref[0], down)
    other_ref[...] = half_of(1 - bits_ref[0], down)


def finish_kernel(
    bit_ref, mine_ref, other_ref, coef_ref, sol_ref, lift_ref, place_ref, send_ref, *, devices, capacity
):
    leaf_rows = sol_ref.shape[0]
    swap = bit_ref[0] == 1
    mine, other = mine_ref[...], other_ref[...]
    h = jnp.concatenate([jnp.where(swap, other, mine), jnp.where(swap, mine, other)], axis=1)
    sol = sol_ref[...] - apply_complex(lift_ref[0], lift_ref[1], coef_ref[...] - h)
    code = scale_code(sol)
    level = jnp.clip(jnp.round(sol * inverse_unit_of(code)), -32767.0, 32767.0)
    high = jnp.round(level * (1.0 / 256.0))
    low = level - high * 256.0
    parts = jnp.concatenate([high.astype(BF16), low.astype(BF16)], axis=1)
    place = place_ref[...]
    place = jnp.transpose(place)
    where_from = iota((LANES, leaf_rows), 1).astype(F32)
    chosen = jnp.concatenate(
        [
            (where_from == place[:, k : k + 1]).astype(F32).astype(BF16)
            for k in range(place.shape[1])
        ],
        axis=0,
    )
    both = matmul(chosen, parts)
    width = sol.shape[1]
    level = (both[:, :width] * 256.0 + both[:, width:]).astype(jnp.int32).astype(jnp.int16)
    send_ref[:, :capacity, :] = level[:, :LANES].reshape(devices, capacity, LANES)
    send_ref[:, capacity : 2 * capacity, :] = level[:, LANES:].reshape(devices, capacity, LANES)
    eight = (EXTRA // 2, LANES)
    extra = jnp.concatenate(
        [jnp.broadcast_to(code[:, :LANES], eight), jnp.broadcast_to(code[:, LANES:], eight)], axis=0
    )
    extra = extra.astype(jnp.int32).astype(jnp.int16)
    send_ref[:, 2 * capacity :, :] = jnp.broadcast_to(
        extra.reshape(1, EXTRA, LANES), (devices, EXTRA, LANES)
    )


def unpack_kernel(got_ref, slot_ref, out_ref, *, devices, capacity):
    leaf_rows = out_ref.shape[0]
    slots = devices * capacity
    extra = got_ref[:, 2 * capacity :, :].astype(jnp.int32).astype(F32)
    halves = []
    for half in range(2):
        level = got_ref[:, half * capacity : (half + 1) * capacity, :]
        level = level.astype(jnp.int32).astype(F32)
        unit = unit_of(extra[:, half * (EXTRA // 2) : half * (EXTRA // 2) + 1, :])
        halves.append((level * unit).reshape(slots, LANES))
    both = two_parts(jnp.concatenate(halves, axis=1))
    slot = jnp.transpose(jnp.broadcast_to(slot_ref[...].astype(F32), (LANES, leaf_rows)))[:, :1]
    chosen = (iota((leaf_rows, slots), 1).astype(F32) == slot).astype(F32).astype(BF16)
    result = folded(matmul(chosen, both))
    first, second = swapped(result[:, :LANES], result[:, LANES:])
    out_ref[:, :LANES] = first
    out_ref[:, LANES:] = second


def call(kernel, out_shapes, operands, smem=0, flops=0, moved=0):
    vmem = pl.BlockSpec(memory_space=pltpu.VMEM)
    scalar = pl.BlockSpec(memory_space=pltpu.SMEM)
    return pl.pallas_call(
        kernel,
        out_shape=out_shapes,
        in_specs=[scalar] * smem + [vmem] * (len(operands) - smem),
        out_specs=jax.tree.map(lambda _: vmem, out_shapes),
        compiler_params=pltpu.CompilerParams(vmem_limit_bytes=48 * 2**20),
        cost_estimate=pl.CostEstimate(flops=flops, bytes_accessed=moved, transcendentals=0),
    )(*operands)


def shape(dims, dtype=F32):
    return jax.ShapeDtypeStruct(dims, dtype)


def from_partner(shard, axis, apart):
    return lax.ppermute(shard, axis, [(i, i ^ 1 << apart) for i in range(lax.axis_size(axis))])


def tree_bit(height, col_levels):
    if height < col_levels:
        return lax.axis_index("col") >> height & 1
    return lax.axis_index("row") >> height - col_levels & 1


def per_device(
    right_sides, tree_order, leaf_inverse, leaf_basis, leaf_lift, node_inverse, node_basis, node_lift
):
    row_count = lax.axis_size("row")
    col_count = lax.axis_size("col")
    devices = row_count * col_count
    col_levels = col_count.bit_length() - 1
    levels = col_levels + row_count.bit_length() - 1
    leaf_rows, width = right_sides.shape
    rank = leaf_basis.shape[3]
    capacity = 2 * leaf_rows // min(devices, leaf_rows // 8)
    block = (devices, 2 * capacity + EXTRA, LANES)
    sizes = dict(devices=devices, capacity=capacity)
    me = (lax.axis_index("row") * col_count + lax.axis_index("col")).astype(jnp.int32)
    bits = [tree_bit(height, col_levels).astype(jnp.int32) for height in range(levels)]

    def exchange(blocks):
        return lax.all_to_all(blocks, ("row", "col"), split_axis=0, concat_axis=0, tiled=True)

    def partner_of(shard, height):
        if height < col_levels:
            return from_partner(shard, "col", height)
        return from_partner(shard, "row", height - col_levels)

    send, slot = call(
        functools.partial(pack_kernel, **sizes),
        (shape(block, BF16), shape((1, leaf_rows), jnp.int32)),
        (me.reshape(1), tree_order.reshape(1, leaf_rows), right_sides),
        smem=1,
    )
    got = exchange(send)
    leaf_sol, leaf_coef, place = call(
        functools.partial(leaf_kernel, **sizes),
        (
            shape((leaf_rows, width)),
            shape((rank, width)),
            shape((devices * capacity // LANES, LANES)),
        ),
        (got, leaf_inverse[0], leaf_basis[0]),
    )
    odd = bits[0] == 1
    own = jnp.where(odd, leaf_coef[:, LANES:], leaf_coef[:, :LANES])
    other = jnp.where(odd, leaf_coef[:, :LANES], leaf_coef[:, LANES:])
    sols, coefs = [], []
    for height in range(1, levels):
        partner = partner_of(other if height == 1 else own, height - 1)
        sol, own = call(
            node_kernel,
            (shape((2 * rank, LANES)), shape((rank, LANES))),
            (
                bits[height - 1].reshape(1),
                own,
                partner,
                node_inverse[0, height - 1],
                node_basis[0, height - 1],
            ),
            smem=1,
        )
        sols.append(sol)
        coefs.append(own)
    partner = partner_of(own, levels - 1)
    mine, other = call(
        descent_kernel,
        (shape((rank, LANES)), shape((rank, LANES))),
        (jnp.stack(bits), own, partner, node_inverse[0, levels - 1], node_lift[0], *sols, *coefs),
        smem=1,
    )
    other = partner_of(other, 0)
    back = call(
        functools.partial(finish_kernel, **sizes),
        shape(block, jnp.int16),
        (bits[0].reshape(1), mine, other, leaf_coef, leaf_sol, leaf_lift[0], place),
        smem=1,
    )
    returned = exchange(back)
    return call(
        functools.partial(unpack_kernel, **sizes),
        shape((leaf_rows, width)),
        (returned, slot),
    )


def solution(mesh):
    in_specs = (
        P(("row", "col"), None),
        P(("row", "col")),
        P(("row", "col"), None, None, None),
        P(("row", "col"), None, None, None),
        P(("row", "col"), None, None, None),
        P(("row", "col"), None, None, None, None),
        P(("row", "col"), None, None, None, None),
        P(("row", "col"), None, None, None, None),
    )
    out_specs = P(("row", "col"), None)
    return jax.shard_map(
        per_device, mesh=mesh, in_specs=in_specs, out_specs=out_specs, check_vma=False
    )
```

```python
import functools

import jax
import jax.numpy as jnp
from jax import lax
from jax.experimental import pallas as pl
from jax.experimental.pallas import tpu as pltpu
from jax.sharding import PartitionSpec as P

LANES = 128
EXTRA = 16
CODE_BASE = 32
SCALE_STEPS = 64
BF16 = jnp.bfloat16
F32 = jnp.float32


def matmul(a, b):
    return lax.dot_general(a, b, (((1,), (0,)), ((), ())), preferred_element_type=F32)


def matmul_t(a, b):
    return lax.dot_general(a, b, (((0,), (0,)), ((), ())), preferred_element_type=F32)


def matmul_nt(a, b):
    return lax.dot_general(a, b, (((1,), (1,)), ((), ())), preferred_element_type=F32)


def iota(shape, dim):
    return lax.broadcasted_iota(jnp.int32, shape, dim)


def rotated(half):
    low = iota(half.shape, 1) < LANES // 2
    turned = pltpu.roll(half, LANES // 2, 1)
    return jnp.where(low, -turned, turned)


def rotated_all(x):
    return jnp.concatenate(
        [rotated(x[:, at : at + LANES]) for at in range(0, x.shape[1], LANES)], axis=1
    )


def swapped(first, second):
    low = iota(first.shape, 1) < LANES // 2
    return (
        jnp.where(low, first, pltpu.roll(second, LANES // 2, 1)),
        jnp.where(low, pltpu.roll(first, LANES // 2, 1), second),
    )


def two_parts(x):
    high = x.astype(BF16)
    low = (x - high.astype(F32)).astype(BF16)
    return jnp.concatenate([high, low], axis=1)


def folded(both):
    width = both.shape[1] // 2
    return both[:, :width] + both[:, width:]


def apply_complex(real, imag, x):
    turned = rotated_all(x)
    return folded(matmul(real, two_parts(x)) + matmul(imag, two_parts(turned)))


def apply_transposed(real, imag, x):
    turned = rotated_all(x)
    return folded(matmul_t(real, two_parts(x)) + matmul_t(imag, two_parts(turned)))


def unit_of(code):
    return jnp.exp2(code * (1.0 / SCALE_STEPS) - 15.0)


def inverse_unit_of(code):
    return jnp.exp2(15.0 - code * (1.0 / SCALE_STEPS))


def scale_code(x):
    largest = jnp.max(jnp.abs(x), axis=0, keepdims=True)
    return jnp.ceil(jnp.log2(jnp.maximum(largest, 2.0**-110)) * SCALE_STEPS)


def fetch(source, target, sem):
    copy = pltpu.make_async_copy(source, target, sem)
    copy.start()
    return copy


def pack_kernel(me_ref, order_ref, rows_hbm, send_ref, slot_ref, rows_ref, sem, *, devices, capacity):
    rows_copy = fetch(rows_hbm, rows_ref, sem.at[0])
    leaf_rows = rows_ref.shape[0]
    order = order_ref[...]
    target = order // leaf_rows
    position = order - target * leaf_rows
    hits = (iota((devices, leaf_rows), 0) == target).astype(F32)
    upper = (iota((leaf_rows, leaf_rows), 0) < iota((leaf_rows, leaf_rows), 1)).astype(F32)
    before = matmul(hits.astype(BF16), upper.astype(BF16))
    rank = jnp.sum(hits * before, axis=0, keepdims=True).astype(jnp.int32)
    slot = target * capacity + rank
    slot_ref[...] = slot
    group = LANES // capacity
    lane = rank + lax.rem(me_ref[0], group) * capacity
    code = position + 1
    high = code // CODE_BASE
    low = code - high * CODE_BASE
    codes = jnp.concatenate([hits * high.astype(F32), hits * low.astype(F32)], axis=0)
    places = (iota((LANES, leaf_rows), 0) == lane).astype(F32).astype(BF16)
    spread = matmul_nt(codes.astype(BF16), places)
    eight = (devices, EXTRA // 2, LANES)
    send_ref[:, 2 * capacity :, :] = jnp.concatenate(
        [
            jnp.broadcast_to(spread[:devices].reshape(devices, 1, LANES), eight),
            jnp.broadcast_to(spread[devices:].reshape(devices, 1, LANES), eight),
        ],
        axis=1,
    ).astype(BF16)
    chosen = (iota((devices * capacity, leaf_rows), 0) == slot).astype(F32).astype(BF16)
    rows_copy.wait()
    rows = rows_ref[...].astype(F32)
    first, second = swapped(rows[:, :LANES], rows[:, LANES:])
    rows = jnp.concatenate([first, second], axis=1).astype(BF16)
    sent = matmul(chosen, rows).astype(BF16)
    send_ref[:, :capacity, :] = sent[:, :LANES].reshape(devices, capacity, LANES)
    send_ref[:, capacity : 2 * capacity, :] = sent[:, LANES:].reshape(devices, capacity, LANES)


def positions(got_ref, devices, capacity):
    group = LANES // capacity
    extra = got_ref[:, 2 * capacity :, :].astype(F32)
    code = extra[:, 0, :] * CODE_BASE + extra[:, EXTRA // 2, :]
    return jnp.sum(code.reshape(devices // group, group, LANES), axis=1) - 1.0


def leaf_kernel(
    bit_ref, got_ref, inverse_hbm, basis_hbm, sol_hbm, own_ref, other_ref, place_ref,
    inverse_ref, basis_ref, sol_ref, sem, *, devices, capacity,
):
    inverse_copies = [fetch(inverse_hbm.at[k], inverse_ref.at[k], sem.at[k]) for k in range(2)]
    basis_copy = fetch(basis_hbm, basis_ref, sem.at[2])
    leaf_rows = sol_ref.shape[0]
    place = positions(got_ref, devices, capacity)
    place_ref[...] = place
    where_to = iota((leaf_rows, LANES), 0).astype(F32)
    chosen = jnp.concatenate(
        [
            (where_to == place[k : k + 1, :]).astype(F32).astype(BF16)
            for k in range(place.shape[0])
        ],
        axis=1,
    )
    slots = devices * capacity
    got = jnp.concatenate(
        [
            got_ref[:, :capacity, :].reshape(slots, LANES),
            got_ref[:, capacity : 2 * capacity, :].reshape(slots, LANES),
        ],
        axis=1,
    )
    placed = matmul(chosen, got)
    turned = rotated_all(placed)
    inverse_copies[0].wait()
    sol = matmul(inverse_ref[0], placed.astype(BF16))
    inverse_copies[1].wait()
    sol = sol + matmul(inverse_ref[1], turned.astype(BF16))
    sol_ref[...] = sol
    sol_copy = fetch(sol_ref, sol_hbm, sem.at[3])
    basis_copy.wait()
    coef = apply_transposed(basis_ref[0], basis_ref[1], sol)
    first, second = coef[:, :LANES], coef[:, LANES:]
    odd = bit_ref[0] == 1
    own_ref[...] = jnp.where(odd, second, first)
    other_ref[...] = jnp.where(odd, first, second)
    sol_copy.wait()


def node_rhs(upper, own, partner):
    is_upper = upper == 1
    return jnp.concatenate(
        [jnp.where(is_upper, partner, own), jnp.where(is_upper, own, partner)], axis=0
    )


def node_kernel(
    bit_ref, own_ref, partner_ref, inverse_hbm, basis_hbm, sol_hbm, coef_ref,
    inverse_ref, basis_ref, sol_ref, sem, *, level,
):
    inverse_copy = fetch(inverse_hbm.at[0, level], inverse_ref, sem.at[0])
    basis_copy = fetch(basis_hbm.at[0, level], basis_ref, sem.at[1])
    rhs = node_rhs(bit_ref[0], own_ref[...], partner_ref[...])
    inverse_copy.wait()
    sol = apply_complex(inverse_ref[0], inverse_ref[1], rhs)
    sol_ref[...] = sol
    sol_copy = fetch(sol_ref, sol_hbm, sem.at[2])
    basis_copy.wait()
    coef_ref[...] = apply_transposed(basis_ref[0], basis_ref[1], sol)
    sol_copy.wait()


def half_of(bit, x):
    rank = x.shape[0] // 2
    return jnp.where(bit == 1, x[rank:], x[:rank])


def descent_kernel(bits_ref, own_ref, partner_ref, inverse_hbm, lift_hbm, *refs):
    levels = bits_ref.shape[0]
    below = levels - 1
    sols_hbm, coefs = refs[:below], refs[below : 2 * below]
    mine_ref, other_ref, inverse_ref, lift_ref, sols_ref, sem = refs[2 * below :]
    inverse_copy = fetch(inverse_hbm.at[0, below], inverse_ref, sem.at[0])
    copies = {}
    for k in range(below - 1, -1, -1):
        copies[k] = (
            fetch(lift_hbm.at[0, k], lift_ref.at[k], sem.at[1 + 2 * k]),
            fetch(sols_hbm[k], sols_ref.at[k], sem.at[2 + 2 * k]),
        )
    rhs = node_rhs(bits_ref[below], own_ref[...], partner_ref[...])
    inverse_copy.wait()
    down = apply_complex(inverse_ref[0], inverse_ref[1], rhs)
    for k in range(below - 1, -1, -1):
        gap = coefs[k][...] - half_of(bits_ref[k + 1], down)
        for copy in copies[k]:
            copy.wait()
        down = sols_ref[k] - apply_complex(lift_ref[k, 0], lift_ref[k, 1], gap)
    mine_ref[...] = half_of(bits_ref[0], down)
    other_ref[...] = half_of(1 - bits_ref[0], down)


def finish_kernel(
    bit_ref, mine_ref, others_ref, own_ref, other_ref, sol_hbm, lift_hbm, place_ref, send_ref,
    sol_ref, lift_ref, sem, *, devices, capacity,
):
    lift_copy = fetch(lift_hbm, lift_ref, sem.at[0])
    sol_copy = fetch(sol_hbm, sol_ref, sem.at[1])
    leaf_rows = sol_ref.shape[0]
    place = jnp.transpose(place_ref[...])
    where_from = iota((LANES, leaf_rows), 1).astype(F32)
    chosen = jnp.concatenate(
        [
            (where_from == place[:, k : k + 1]).astype(F32).astype(BF16)
            for k in range(place.shape[1])
        ],
        axis=0,
    )
    swap = bit_ref[0] == 1
    mine = own_ref[...] - mine_ref[...]
    other = other_ref[...] - others_ref[...]
    gap = jnp.concatenate([jnp.where(swap, other, mine), jnp.where(swap, mine, other)], axis=1)
    lift_copy.wait()
    change = apply_complex(lift_ref[0], lift_ref[1], gap)
    sol_copy.wait()
    sol = sol_ref[...] - change
    code = scale_code(sol)
    level = jnp.clip(jnp.round(sol * inverse_unit_of(code)), -32767.0, 32767.0)
    high = jnp.round(level * (1.0 / 256.0))
    low = level - high * 256.0
    parts = jnp.concatenate([high.astype(BF16), low.astype(BF16)], axis=1)
    both = matmul(chosen, parts)
    width = sol.shape[1]
    level = (both[:, :width] * 256.0 + both[:, width:]).astype(jnp.int32).astype(jnp.int16)
    send_ref[:, :capacity, :] = level[:, :LANES].reshape(devices, capacity, LANES)
    send_ref[:, capacity : 2 * capacity, :] = level[:, LANES:].reshape(devices, capacity, LANES)
    eight = (EXTRA // 2, LANES)
    extra = jnp.concatenate(
        [jnp.broadcast_to(code[:, :LANES], eight), jnp.broadcast_to(code[:, LANES:], eight)], axis=0
    )
    extra = extra.astype(jnp.int32).astype(jnp.int16)
    send_ref[:, 2 * capacity :, :] = jnp.broadcast_to(
        extra.reshape(1, EXTRA, LANES), (devices, EXTRA, LANES)
    )


def unpack_kernel(got_ref, slot_ref, out_ref, *, devices, capacity):
    leaf_rows = out_ref.shape[0]
    slots = devices * capacity
    extra = got_ref[:, 2 * capacity :, :].astype(jnp.int32).astype(F32)
    halves = []
    for half in range(2):
        level = got_ref[:, half * capacity : (half + 1) * capacity, :]
        level = level.astype(jnp.int32).astype(F32)
        unit = unit_of(extra[:, half * (EXTRA // 2) : half * (EXTRA // 2) + 1, :])
        halves.append((level * unit).reshape(slots, LANES))
    both = two_parts(jnp.concatenate(halves, axis=1))
    slot = jnp.transpose(jnp.broadcast_to(slot_ref[...].astype(F32), (LANES, leaf_rows)))[:, :1]
    chosen = (iota((leaf_rows, slots), 1).astype(F32) == slot).astype(F32).astype(BF16)
    result = folded(matmul(chosen, both))
    first, second = swapped(result[:, :LANES], result[:, LANES:])
    out_ref[:, :LANES] = first
    out_ref[:, LANES:] = second


def call(kernel, outs, operands, scratch=(), vmem=24):
    specs = {
        "smem": pl.BlockSpec(memory_space=pltpu.SMEM),
        "vmem": pl.BlockSpec(memory_space=pltpu.VMEM),
        "hbm": pl.BlockSpec(memory_space=pl.ANY),
    }
    results = pl.pallas_call(
        kernel,
        out_shape=[pltpu.HBM(out.shape, out.dtype) if space == "hbm" else out for out, space in outs],
        in_specs=[specs[space] for _, space in operands],
        out_specs=[specs[space] for _, space in outs],
        scratch_shapes=[
            pltpu.SemaphoreType.DMA((one,)) if isinstance(one, int) else pltpu.VMEM(one.shape, one.dtype)
            for one in scratch
        ],
        compiler_params=pltpu.CompilerParams(vmem_limit_bytes=vmem * 2**20),
    )(
        *[
            pltpu.with_memory_space_constraint(array, pltpu.HBM) if space == "hbm" else array
            for array, space in operands
        ]
    )
    return results


def shape(dims, dtype=F32):
    return jax.ShapeDtypeStruct(dims, dtype)


def from_partner(shard, axis, apart):
    return lax.ppermute(shard, axis, [(i, i ^ 1 << apart) for i in range(lax.axis_size(axis))])


def tree_bit(height, col_levels):
    if height < col_levels:
        return lax.axis_index("col") >> height & 1
    return lax.axis_index("row") >> height - col_levels & 1


def per_device(
    right_sides, tree_order, leaf_inverse, leaf_basis, leaf_lift, node_inverse, node_basis, node_lift
):
    row_count = lax.axis_size("row")
    col_count = lax.axis_size("col")
    devices = row_count * col_count
    col_levels = col_count.bit_length() - 1
    levels = col_levels + row_count.bit_length() - 1
    leaf_rows, width = right_sides.shape
    rank = leaf_basis.shape[3]
    capacity = 2 * leaf_rows // min(devices, leaf_rows // 8)
    block = (devices, 2 * capacity + EXTRA, LANES)
    sizes = dict(devices=devices, capacity=capacity)
    me = (lax.axis_index("row") * col_count + lax.axis_index("col")).astype(jnp.int32)
    bits = [tree_bit(height, col_levels).astype(jnp.int32) for height in range(levels)]

    def exchange(blocks):
        return lax.all_to_all(blocks, ("row", "col"), split_axis=0, concat_axis=0, tiled=True)

    def partner_of(shard, height):
        if height < col_levels:
            return from_partner(shard, "col", height)
        return from_partner(shard, "row", height - col_levels)

    send, slot = call(
        functools.partial(pack_kernel, **sizes),
        [(shape(block, BF16), "vmem"), (shape((1, leaf_rows), jnp.int32), "vmem")],
        [(me.reshape(1), "smem"), (tree_order.reshape(1, leaf_rows), "vmem"), (right_sides, "hbm")],
        [shape(right_sides.shape, BF16), 1],
    )
    got = exchange(send)
    half = shape((rank, LANES))
    leaf_sol, own, other, place = call(
        functools.partial(leaf_kernel, **sizes),
        [
            (shape((leaf_rows, width)), "hbm"),
            (half, "vmem"),
            (half, "vmem"),
            (shape((devices * capacity // LANES, LANES)), "vmem"),
        ],
        [(bits[0].reshape(1), "smem"), (got, "vmem"), (leaf_inverse[0], "hbm"), (leaf_basis[0], "hbm")],
        [
            shape(leaf_inverse.shape[1:], BF16),
            shape(leaf_basis.shape[1:], BF16),
            shape((leaf_rows, width)),
            4,
        ],
    )
    leaf_own, leaf_other = own, other
    whole = shape((2 * rank, LANES))
    inverse_shape = shape(node_inverse.shape[2:], BF16)
    sols, coefs = [], []
    for height in range(1, levels):
        partner = partner_of(other if height == 1 else own, height - 1)
        sol, own = call(
            functools.partial(node_kernel, level=height - 1),
            [(whole, "hbm"), (half, "vmem")],
            [
                (bits[height - 1].reshape(1), "smem"),
                (own, "vmem"),
                (partner, "vmem"),
                (node_inverse, "hbm"),
                (node_basis, "hbm"),
            ],
            [inverse_shape, shape(node_basis.shape[2:], BF16), whole, 3],
            vmem=12,
        )
        sols.append(sol)
        coefs.append(own)
    partner = partner_of(own, levels - 1)
    mine, other = call(
        descent_kernel,
        [(half, "vmem"), (half, "vmem")],
        [(jnp.stack(bits), "smem"), (own, "vmem"), (partner, "vmem"), (node_inverse, "hbm"), (node_lift, "hbm")]
        + [(sol, "hbm") for sol in sols]
        + [(coef, "vmem") for coef in coefs],
        [
            inverse_shape,
            shape(node_lift.shape[1:], BF16),
            shape((levels - 1,) + whole.shape),
            2 * levels - 1,
        ],
        vmem=16,
    )
    other = partner_of(other, 0)
    (back,) = call(
        functools.partial(finish_kernel, **sizes),
        [(shape(block, jnp.int16), "vmem")],
        [
            (bits[0].reshape(1), "smem"),
            (mine, "vmem"),
            (other, "vmem"),
            (leaf_own, "vmem"),
            (leaf_other, "vmem"),
            (leaf_sol, "hbm"),
            (leaf_lift[0], "hbm"),
            (place, "vmem"),
        ],
        [shape((leaf_rows, width)), shape(leaf_lift.shape[1:], BF16), 2],
    )
    returned = exchange(back)
    (result,) = call(
        functools.partial(unpack_kernel, **sizes),
        [(shape((leaf_rows, width)), "vmem")],
        [(returned, "vmem"), (slot, "vmem")],
    )
    return result


def solution(mesh):
    in_specs = (
        P(("row", "col"), None),
        P(("row", "col")),
        P(("row", "col"), None, None, None),
        P(("row", "col"), None, None, None),
        P(("row", "col"), None, None, None),
        P(("row", "col"), None, None, None, None),
        P(("row", "col"), None, None, None, None),
        P(("row", "col"), None, None, None, None),
    )
    out_specs = P(("row", "col"), None)
    return jax.shard_map(
        per_device, mesh=mesh, in_specs=in_specs, out_specs=out_specs, check_vma=False
    )
```

```python
import functools

import jax
import jax.numpy as jnp
from jax import lax
from jax.experimental import pallas as pl
from jax.experimental.pallas import tpu as pltpu
from jax.sharding import PartitionSpec as P

LANES = 128
EXTRA = 8
CODE_BASE = 32
SCALE_STEPS = 64
BF16 = jnp.bfloat16
F32 = jnp.float32


def matmul(a, b):
    return lax.dot_general(a, b, (((1,), (0,)), ((), ())), preferred_element_type=F32)


def matmul_t(a, b):
    return lax.dot_general(a, b, (((0,), (0,)), ((), ())), preferred_element_type=F32)


def matmul_nt(a, b):
    return lax.dot_general(a, b, (((1,), (1,)), ((), ())), preferred_element_type=F32)


def iota(shape, dim):
    return lax.broadcasted_iota(jnp.int32, shape, dim)


def rotated(half):
    low = iota(half.shape, 1) < LANES // 2
    turned = pltpu.roll(half, LANES // 2, 1)
    return jnp.where(low, -turned, turned)


def rotated_all(x):
    return jnp.concatenate(
        [rotated(x[:, at : at + LANES]) for at in range(0, x.shape[1], LANES)], axis=1
    )


def swapped(first, second):
    low = iota(first.shape, 1) < LANES // 2
    return (
        jnp.where(low, first, pltpu.roll(second, LANES // 2, 1)),
        jnp.where(low, pltpu.roll(first, LANES // 2, 1), second),
    )


def two_parts(x):
    high = x.astype(BF16)
    low = (x - high.astype(F32)).astype(BF16)
    return jnp.concatenate([high, low], axis=1)


def folded(both):
    width = both.shape[1] // 2
    return both[:, :width] + both[:, width:]


def apply_complex(real, imag, x):
    turned = rotated_all(x)
    return folded(matmul(real, two_parts(x)) + matmul(imag, two_parts(turned)))


def apply_transposed(real, imag, x):
    turned = rotated_all(x)
    return folded(matmul_t(real, two_parts(x)) + matmul_t(imag, two_parts(turned)))


def unit_of(code):
    return jnp.exp2(code * (1.0 / SCALE_STEPS) - 15.0)


def inverse_unit_of(code):
    return jnp.exp2(15.0 - code * (1.0 / SCALE_STEPS))


def scale_code(x):
    largest = jnp.max(jnp.abs(x), axis=0, keepdims=True)
    return jnp.ceil(jnp.log2(jnp.maximum(largest, 2.0**-110)) * SCALE_STEPS)


def fetch(source, target, sem):
    copy = pltpu.make_async_copy(source, target, sem)
    copy.start()
    return copy


def pack_kernel(me_ref, order_ref, rows_hbm, send_ref, slot_ref, rows_ref, sem, *, devices, capacity):
    rows_copy = fetch(rows_hbm, rows_ref, sem.at[0])
    leaf_rows = rows_ref.shape[0]
    order = order_ref[...]
    target = order // leaf_rows
    position = order - target * leaf_rows
    hits = (iota((devices, leaf_rows), 0) == target).astype(F32)
    upper = (iota((leaf_rows, leaf_rows), 0) < iota((leaf_rows, leaf_rows), 1)).astype(F32)
    before = matmul(hits.astype(BF16), upper.astype(BF16))
    rank = jnp.sum(hits * before, axis=0, keepdims=True).astype(jnp.int32)
    slot = target * capacity + rank
    slot_ref[...] = slot
    group = LANES // capacity
    lane = rank + lax.rem(me_ref[0], group) * capacity
    code = position + 1
    high = code // CODE_BASE
    low = code - high * CODE_BASE
    codes = jnp.concatenate([hits * high.astype(F32), hits * low.astype(F32)], axis=0)
    places = (iota((LANES, leaf_rows), 0) == lane).astype(F32).astype(BF16)
    spread = matmul_nt(codes.astype(BF16), places)
    extra = (devices, EXTRA, LANES)
    send_ref[:, 2 * capacity :, :] = jnp.where(
        iota(extra, 1) < EXTRA // 2,
        jnp.broadcast_to(spread[:devices].reshape(devices, 1, LANES), extra),
        jnp.broadcast_to(spread[devices:].reshape(devices, 1, LANES), extra),
    ).astype(BF16)
    chosen = (iota((devices * capacity, leaf_rows), 0) == slot).astype(F32).astype(BF16)
    rows_copy.wait()
    rows = rows_ref[...].astype(F32)
    first, second = swapped(rows[:, :LANES], rows[:, LANES:])
    rows = jnp.concatenate([first, second], axis=1).astype(BF16)
    sent = matmul(chosen, rows).astype(BF16)
    send_ref[:, :capacity, :] = sent[:, :LANES].reshape(devices, capacity, LANES)
    send_ref[:, capacity : 2 * capacity, :] = sent[:, LANES:].reshape(devices, capacity, LANES)


def positions(got_ref, devices, capacity):
    group = LANES // capacity
    extra = got_ref[:, 2 * capacity :, :].astype(F32)
    code = extra[:, 0, :] * CODE_BASE + extra[:, EXTRA // 2, :]
    return jnp.sum(code.reshape(devices // group, group, LANES), axis=1) - 1.0


def load_kernel(after_ref, *refs, picks):
    count = len(picks)
    sources, targets, sem = refs[:count], refs[count : 2 * count], refs[2 * count]
    copies = [
        fetch(source.at[pick], target, sem.at[k])
        for k, (source, target, pick) in enumerate(zip(sources, targets, picks))
    ]
    for copy in copies:
        copy.wait()


def leaf_kernel(
    bit_ref, got_ref, inverse_hbm, basis_ref, sol_hbm, own_ref, other_ref, place_ref,
    inverse_ref, sol_ref, sem, *, devices, capacity,
):
    copies = [fetch(inverse_hbm.at[0, k], inverse_ref.at[k], sem.at[1 + k]) for k in range(2)]
    leaf_rows = sol_ref.shape[0]
    place = positions(got_ref, devices, capacity)
    place_ref[...] = place
    where_to = iota((leaf_rows, LANES), 0).astype(F32)
    chosen = jnp.concatenate(
        [
            (where_to == place[k : k + 1, :]).astype(F32).astype(BF16)
            for k in range(place.shape[0])
        ],
        axis=1,
    )
    slots = devices * capacity
    got = jnp.concatenate(
        [
            got_ref[:, :capacity, :].reshape(slots, LANES),
            got_ref[:, capacity : 2 * capacity, :].reshape(slots, LANES),
        ],
        axis=1,
    )
    placed = matmul(chosen, got)
    turned = rotated_all(placed)
    copies[0].wait()
    sol = matmul(inverse_ref[0], placed.astype(BF16))
    copies[1].wait()
    sol = sol + matmul(inverse_ref[1], turned.astype(BF16))
    sol_ref[...] = sol
    sol_copy = fetch(sol_ref, sol_hbm, sem.at[0])
    coef = apply_transposed(basis_ref[0], basis_ref[1], sol)
    first, second = coef[:, :LANES], coef[:, LANES:]
    odd = bit_ref[0] == 1
    own_ref[...] = jnp.where(odd, second, first)
    other_ref[...] = jnp.where(odd, first, second)
    sol_copy.wait()


def node_rhs(upper, own, partner):
    is_upper = upper == 1
    return jnp.concatenate(
        [jnp.where(is_upper, partner, own), jnp.where(is_upper, own, partner)], axis=0
    )


def node_kernel(
    bit_ref, own_ref, partner_ref, inverse_ref, basis_ref, sol_hbm, coef_ref, sol_ref, sem
):
    rhs = node_rhs(bit_ref[0], own_ref[...], partner_ref[...])
    sol = apply_complex(inverse_ref[0], inverse_ref[1], rhs)
    sol_ref[...] = sol
    sol_copy = fetch(sol_ref, sol_hbm, sem.at[0])
    coef_ref[...] = apply_transposed(basis_ref[0], basis_ref[1], sol)
    sol_copy.wait()


def half_of(bit, x):
    rank = x.shape[0] // 2
    return jnp.where(bit == 1, x[rank:], x[:rank])


def descent_kernel(bits_ref, own_ref, partner_ref, inverse_ref, lift_ref, *refs):
    levels = bits_ref.shape[0]
    below = levels - 1
    sols, coefs = refs[:below], refs[below : 2 * below]
    mine_ref, other_ref = refs[2 * below :]
    rhs = node_rhs(bits_ref[below], own_ref[...], partner_ref[...])
    down = apply_complex(inverse_ref[0], inverse_ref[1], rhs)
    for k in range(below - 1, -1, -1):
        gap = coefs[k][...] - half_of(bits_ref[k + 1], down)
        down = sols[k][...] - apply_complex(lift_ref[k, 0], lift_ref[k, 1], gap)
    mine_ref[...] = half_of(bits_ref[0], down)
    other_ref[...] = half_of(1 - bits_ref[0], down)


def finish_kernel(
    bit_ref, mine_ref, others_ref, own_ref, other_ref, sol_hbm, lift_hbm, place_ref, send_ref,
    sol_ref, lift_ref, sem, *, devices, capacity,
):
    lift_copy = fetch(lift_hbm, lift_ref, sem.at[0])
    sol_copy = fetch(sol_hbm, sol_ref, sem.at[1])
    leaf_rows = sol_ref.shape[0]
    place = jnp.transpose(place_ref[...])
    where_from = iota((LANES, leaf_rows), 1).astype(F32)
    chosen = jnp.concatenate(
        [
            (where_from == place[:, k : k + 1]).astype(F32).astype(BF16)
            for k in range(place.shape[1])
        ],
        axis=0,
    )
    swap = bit_ref[0] == 1
    mine = own_ref[...] - mine_ref[...]
    other = other_ref[...] - others_ref[...]
    gap = jnp.concatenate([jnp.where(swap, other, mine), jnp.where(swap, mine, other)], axis=1)
    lift_copy.wait()
    change = apply_complex(lift_ref[0], lift_ref[1], gap)
    sol_copy.wait()
    sol = sol_ref[...] - change
    code = scale_code(sol)
    level = jnp.clip(jnp.round(sol * inverse_unit_of(code)), -32767.0, 32767.0)
    high = jnp.round(level * (1.0 / 256.0))
    low = level - high * 256.0
    parts = jnp.concatenate([high.astype(BF16), low.astype(BF16)], axis=1)
    both = matmul(chosen, parts)
    width = sol.shape[1]
    level = (both[:, :width] * 256.0 + both[:, width:]).astype(jnp.int32).astype(jnp.int16)
    send_ref[:, :capacity, :] = level[:, :LANES].reshape(devices, capacity, LANES)
    send_ref[:, capacity : 2 * capacity, :] = level[:, LANES:].reshape(devices, capacity, LANES)
    extra = (EXTRA, LANES)
    extra = jnp.where(
        iota(extra, 0) < EXTRA // 2,
        jnp.broadcast_to(code[:, :LANES], extra),
        jnp.broadcast_to(code[:, LANES:], extra),
    )
    extra = extra.astype(jnp.int32).astype(jnp.int16)
    send_ref[:, 2 * capacity :, :] = jnp.broadcast_to(
        extra.reshape(1, EXTRA, LANES), (devices, EXTRA, LANES)
    )


def unpack_kernel(got_ref, slot_ref, out_ref, *, devices, capacity):
    leaf_rows = out_ref.shape[0]
    slots = devices * capacity
    extra = got_ref[:, 2 * capacity :, :].astype(jnp.int32).astype(F32)
    halves = []
    for half in range(2):
        level = got_ref[:, half * capacity : (half + 1) * capacity, :]
        level = level.astype(jnp.int32).astype(F32)
        unit = unit_of(extra[:, half * (EXTRA // 2) : half * (EXTRA // 2) + 1, :])
        halves.append((level * unit).reshape(slots, LANES))
    both = two_parts(jnp.concatenate(halves, axis=1))
    slot = jnp.transpose(jnp.broadcast_to(slot_ref[...].astype(F32), (LANES, leaf_rows)))[:, :1]
    chosen = (iota((leaf_rows, slots), 1).astype(F32) == slot).astype(F32).astype(BF16)
    result = folded(matmul(chosen, both))
    first, second = swapped(result[:, :LANES], result[:, LANES:])
    out_ref[:, :LANES] = first
    out_ref[:, LANES:] = second


def call(kernel, outs, operands, scratch=(), vmem=24):
    specs = {
        "smem": pl.BlockSpec(memory_space=pltpu.SMEM),
        "vmem": pl.BlockSpec(memory_space=pltpu.VMEM),
        "hbm": pl.BlockSpec(memory_space=pl.ANY),
        "any": pl.BlockSpec(memory_space=pl.ANY),
    }
    results = pl.pallas_call(
        kernel,
        out_shape=[pltpu.HBM(out.shape, out.dtype) if space == "hbm" else out for out, space in outs],
        in_specs=[specs[space] for _, space in operands],
        out_specs=[specs[space] for _, space in outs],
        scratch_shapes=[
            pltpu.SemaphoreType.DMA((one,)) if isinstance(one, int) else pltpu.VMEM(one.shape, one.dtype)
            for one in scratch
        ],
        compiler_params=pltpu.CompilerParams(vmem_limit_bytes=vmem * 2**20),
    )(
        *[
            pltpu.with_memory_space_constraint(array, pltpu.HBM) if space == "hbm" else array
            for array, space in operands
        ]
    )
    return results


def shape(dims, dtype=F32):
    return jax.ShapeDtypeStruct(dims, dtype)


def from_partner(shard, axis, apart):
    return lax.ppermute(shard, axis, [(i, i ^ 1 << apart) for i in range(lax.axis_size(axis))])


def tree_bit(height, col_levels):
    if height < col_levels:
        return lax.axis_index("col") >> height & 1
    return lax.axis_index("row") >> height - col_levels & 1


def per_device(
    right_sides, tree_order, leaf_inverse, leaf_basis, leaf_lift, node_inverse, node_basis, node_lift
):
    row_count = lax.axis_size("row")
    col_count = lax.axis_size("col")
    devices = row_count * col_count
    col_levels = col_count.bit_length() - 1
    levels = col_levels + row_count.bit_length() - 1
    leaf_rows, width = right_sides.shape
    rank = leaf_basis.shape[3]
    capacity = 2 * leaf_rows // min(devices, leaf_rows // 8)
    block = (devices, 2 * capacity + EXTRA, LANES)
    sizes = dict(devices=devices, capacity=capacity)
    me = (lax.axis_index("row") * col_count + lax.axis_index("col")).astype(jnp.int32)
    bits = [tree_bit(height, col_levels).astype(jnp.int32) for height in range(levels)]

    def exchange(blocks):
        return lax.all_to_all(blocks, ("row", "col"), split_axis=0, concat_axis=0, tiled=True)

    def partner_of(shard, height):
        if height < col_levels:
            return from_partner(shard, "col", height)
        return from_partner(shard, "row", height - col_levels)

    send, slot = call(
        functools.partial(pack_kernel, **sizes),
        [(shape(block, BF16), "vmem"), (shape((1, leaf_rows), jnp.int32), "vmem")],
        [(me.reshape(1), "smem"), (tree_order.reshape(1, leaf_rows), "vmem"), (right_sides, "hbm")],
        [shape(right_sides.shape, BF16), 1],
    )
    def load(after, weights, picks):
        shapes = [jax.eval_shape(lambda w, pick=pick: w[pick], w) for w, pick in zip(weights, picks)]
        return call(
            functools.partial(load_kernel, picks=picks),
            [(shape(one.shape, one.dtype), "vmem") for one in shapes],
            [(after, "any")] + [(weight, "hbm") for weight in weights],
            [len(weights)],
            vmem=4,
        )

    got = exchange(send)
    (leaf_basis,) = load(slot, (leaf_basis,), (0,))
    half = shape((rank, LANES))
    leaf_sol, own, other, place = call(
        functools.partial(leaf_kernel, **sizes),
        [
            (shape((leaf_rows, width)), "hbm"),
            (half, "vmem"),
            (half, "vmem"),
            (shape((devices * capacity // LANES, LANES)), "vmem"),
        ],
        [(bits[0].reshape(1), "smem"), (got, "vmem"), (leaf_inverse, "hbm"), (leaf_basis, "vmem")],
        [shape(leaf_inverse.shape[1:], BF16), shape((leaf_rows, width)), 3],
    )
    leaf_own, leaf_other = own, other
    whole = shape((2 * rank, LANES))
    sols, coefs = [], []
    for height in range(1, levels):
        partner = partner_of(other if height == 1 else own, height - 1)
        pick = (0, height - 1)
        inverse, basis = load(own, (node_inverse, node_basis), (pick, pick))
        sol, own = call(
            node_kernel,
            [(whole, "hbm"), (half, "vmem")],
            [
                (bits[height - 1].reshape(1), "smem"),
                (own, "vmem"),
                (partner, "vmem"),
                (inverse, "vmem"),
                (basis, "vmem"),
            ],
            [whole, 1],
            vmem=12,
        )
        sols.append(sol)
        coefs.append(own)
    partner = partner_of(own, levels - 1)
    inverse, lift, *sols = load(
        own, (node_inverse, node_lift, *sols), ((0, levels - 1), 0) + (slice(None),) * (levels - 1)
    )
    mine, other = call(
        descent_kernel,
        [(half, "vmem"), (half, "vmem")],
        [(jnp.stack(bits), "smem"), (own, "vmem"), (partner, "vmem"), (inverse, "vmem"), (lift, "vmem")]
        + [(sol, "vmem") for sol in sols]
        + [(coef, "vmem") for coef in coefs],
        vmem=16,
    )
    other = partner_of(other, 0)
    (back,) = call(
        functools.partial(finish_kernel, **sizes),
        [(shape(block, jnp.int16), "vmem")],
        [
            (bits[0].reshape(1), "smem"),
            (mine, "vmem"),
            (other, "vmem"),
            (leaf_own, "vmem"),
            (leaf_other, "vmem"),
            (leaf_sol, "hbm"),
            (leaf_lift[0], "hbm"),
            (place, "vmem"),
        ],
        [shape((leaf_rows, width)), shape(leaf_lift.shape[1:], BF16), 2],
    )
    returned = exchange(back)
    (result,) = call(
        functools.partial(unpack_kernel, **sizes),
        [(shape((leaf_rows, width)), "vmem")],
        [(returned, "vmem"), (slot, "vmem")],
    )
    return result


def solution(mesh):
    in_specs = (
        P(("row", "col"), None),
        P(("row", "col")),
        P(("row", "col"), None, None, None),
        P(("row", "col"), None, None, None),
        P(("row", "col"), None, None, None),
        P(("row", "col"), None, None, None, None),
        P(("row", "col"), None, None, None, None),
        P(("row", "col"), None, None, None, None),
    )
    out_specs = P(("row", "col"), None)
    return jax.shard_map(
        per_device, mesh=mesh, in_specs=in_specs, out_specs=out_specs, check_vma=False
    )
```

```python
import functools

import jax
import jax.numpy as jnp
from jax import lax
from jax.experimental import pallas as pl
from jax.experimental.pallas import tpu as pltpu
from jax.sharding import PartitionSpec as P

LANES = 128
EXTRA = 8
CODE_BASE = 32
SCALE_STEPS = 64
BF16 = jnp.bfloat16
F32 = jnp.float32


def matmul(a, b):
    return lax.dot_general(a, b, (((1,), (0,)), ((), ())), preferred_element_type=F32)


def matmul_t(a, b):
    return lax.dot_general(a, b, (((0,), (0,)), ((), ())), preferred_element_type=F32)


def matmul_nt(a, b):
    return lax.dot_general(a, b, (((1,), (1,)), ((), ())), preferred_element_type=F32)


def iota(shape, dim):
    return lax.broadcasted_iota(jnp.int32, shape, dim)


def rotated(half):
    low = iota(half.shape, 1) < LANES // 2
    turned = pltpu.roll(half, LANES // 2, 1)
    return jnp.where(low, -turned, turned)


def rotated_all(x):
    return jnp.concatenate(
        [rotated(x[:, at : at + LANES]) for at in range(0, x.shape[1], LANES)], axis=1
    )


def swapped(first, second):
    low = iota(first.shape, 1) < LANES // 2
    return (
        jnp.where(low, first, pltpu.roll(second, LANES // 2, 1)),
        jnp.where(low, pltpu.roll(first, LANES // 2, 1), second),
    )


def two_parts(x):
    high = x.astype(BF16)
    low = (x - high.astype(F32)).astype(BF16)
    return jnp.concatenate([high, low], axis=1)


def folded(both):
    width = both.shape[1] // 2
    return both[:, :width] + both[:, width:]


def apply_complex(real, imag, x):
    turned = rotated_all(x)
    return folded(matmul(real, two_parts(x)) + matmul(imag, two_parts(turned)))


def apply_transposed(real, imag, x):
    turned = rotated_all(x)
    return folded(matmul_t(real, two_parts(x)) + matmul_t(imag, two_parts(turned)))


def unit_of(code):
    return jnp.exp2(code * (1.0 / SCALE_STEPS) - 15.0)


def inverse_unit_of(code):
    return jnp.exp2(15.0 - code * (1.0 / SCALE_STEPS))


def scale_code(x):
    largest = jnp.max(jnp.abs(x), axis=0, keepdims=True)
    return jnp.ceil(jnp.log2(jnp.maximum(largest, 2.0**-110)) * SCALE_STEPS)


def fetch(source, target, sem):
    copy = pltpu.make_async_copy(source, target, sem)
    copy.start()
    return copy


def wide_one_hot(index, blocks):
    turned = jnp.transpose(index)
    lane = iota((LANES, LANES), 1).astype(F32)
    parts = []
    for k in range(index.shape[0]):
        entry = turned[:, k : k + 1]
        block = jnp.floor(entry * (1.0 / LANES))
        parts.append(jnp.where(lane == entry - block * LANES, block, -1.0))
    chosen = jnp.concatenate(parts, axis=0).astype(BF16)
    one, zero = jnp.ones((), BF16), jnp.zeros((), BF16)
    return jnp.concatenate(
        [jnp.where(chosen == jnp.array(g, BF16), one, zero) for g in range(blocks)], axis=1
    )


def row_blocks(x):
    return jnp.concatenate([x[:, at : at + LANES] for at in range(0, x.shape[1], LANES)], axis=0)


def ranks(hits):
    rows, width = hits.shape
    upper = (iota((LANES, LANES), 0) < iota((LANES, LANES), 1)).astype(F32).astype(BF16)
    pieces = jnp.concatenate(
        [hits[:, at : at + LANES] for at in range(0, width, LANES)], axis=0
    ).astype(BF16)
    inside = matmul(pieces, upper)
    totals = matmul(pieces, jnp.ones((LANES, LANES), BF16))
    ahead = jnp.zeros((rows, LANES), F32)
    parts = []
    for k in range(width // LANES):
        parts.append(inside[k * rows : (k + 1) * rows] + ahead)
        ahead = ahead + totals[k * rows : (k + 1) * rows]
    return jnp.concatenate(parts, axis=1)


def pack_kernel(
    me_ref, order_hbm, rows_hbm, send_ref, slot_ref, order_ref, rows_ref, sem, *, devices, capacity
):
    order_copy = fetch(order_hbm, order_ref, sem.at[0])
    rows_copy = fetch(rows_hbm, rows_ref, sem.at[1])
    leaf_rows = rows_ref.shape[0]
    order_copy.wait()
    order = order_ref[...]
    target = order // leaf_rows
    position = order - target * leaf_rows
    hits = (iota((devices, leaf_rows), 0) == target).astype(F32)
    rank = jnp.sum(hits * ranks(hits), axis=0, keepdims=True).astype(jnp.int32)
    slot_ref[...] = row_blocks((target * capacity + rank).astype(F32))
    group = LANES // capacity
    lane = rank + lax.rem(me_ref[0], group) * capacity
    high = position // CODE_BASE
    low = position - high * CODE_BASE
    codes = jnp.concatenate([hits * (high + 1).astype(F32), hits * low.astype(F32)], axis=0)
    places = (iota((LANES, leaf_rows), 0) == lane).astype(F32).astype(BF16)
    spread = matmul_nt(codes.astype(BF16), places)
    extra = (devices, EXTRA, LANES)
    send_ref[:, 2 * capacity :, :] = jnp.where(
        iota(extra, 1) < EXTRA // 2,
        jnp.broadcast_to(spread[:devices].reshape(devices, 1, LANES), extra),
        jnp.broadcast_to(spread[devices:].reshape(devices, 1, LANES), extra),
    ).astype(BF16)
    in_slot = (iota((capacity, leaf_rows), 0) == rank).astype(F32).astype(BF16)
    hits = hits.astype(BF16)
    chosen = jnp.concatenate([in_slot * hits[t : t + 1, :] for t in range(devices)], axis=0)
    rows_copy.wait()
    rows = rows_ref[...].astype(F32)
    first, second = swapped(rows[:, :LANES], rows[:, LANES:])
    rows = jnp.concatenate([first, second], axis=1).astype(BF16)
    sent = matmul(chosen, rows).astype(BF16)
    send_ref[:, :capacity, :] = sent[:, :LANES].reshape(devices, capacity, LANES)
    send_ref[:, capacity : 2 * capacity, :] = sent[:, LANES:].reshape(devices, capacity, LANES)


def codes_of(got_ref, devices, capacity):
    group = LANES // capacity
    extra = got_ref[:, 2 * capacity :, :].astype(F32)
    grouped = (devices // group, group, LANES)
    high = jnp.sum(extra[:, 0, :].reshape(grouped), axis=1)
    low = jnp.sum(extra[:, EXTRA // 2, :].reshape(grouped), axis=1)
    return high, low


def load_kernel(after_ref, *refs, picks, turned, stores):
    count = len(picks)
    sources, stored = refs[:count], refs[count : count + stores]
    targets = refs[count + stores : 2 * count + stores]
    kept = refs[2 * count + stores : 2 * count + 2 * stores]
    scratch, sem = refs[2 * count + 2 * stores : -1], refs[-1]
    plain = count - turned
    landing = targets[:plain] + scratch
    copies = [
        fetch(source.at[pick], target, sem.at[k])
        for k, (source, target, pick) in enumerate(zip(sources, landing, picks))
    ]
    copies += [fetch(stored[k], kept[k], sem.at[count + k]) for k in range(stores)]
    for k in range(turned):
        copies[plain + k].wait()
        for part in range(2):
            targets[plain + k][part] = jnp.transpose(scratch[k][part])
    for k, copy in enumerate(copies):
        if not plain <= k < count:
            copy.wait()


def leaf_kernel(
    bit_ref, got_ref, inverse_hbm, basis_ref, sol_hbm, own_ref, other_ref, place_ref,
    inverse_ref, sol_ref, sem, *, devices, capacity,
):
    copies = [fetch(inverse_hbm.at[0, k], inverse_ref.at[k], sem.at[1 + k]) for k in range(2)]
    leaf_rows = sol_ref.shape[0]
    high, low = codes_of(got_ref, devices, capacity)
    place_ref[...] = (high - 1.0) * CODE_BASE + low
    code = iota((CODE_BASE, LANES), 0).astype(F32)
    groups = high.shape[0]
    is_low = jnp.concatenate(
        [(code == low[k : k + 1]).astype(F32) for k in range(groups)], axis=1
    ).astype(BF16)
    is_high = jnp.concatenate(
        [(code == high[k : k + 1] - 1.0).astype(F32) for k in range(groups)], axis=1
    ).astype(BF16)
    chosen = jnp.concatenate(
        [is_low * is_high[h : h + 1, :] for h in range(leaf_rows // CODE_BASE)], axis=0
    )
    slots = devices * capacity
    got = jnp.concatenate(
        [
            got_ref[:, :capacity, :].reshape(slots, LANES),
            got_ref[:, capacity : 2 * capacity, :].reshape(slots, LANES),
        ],
        axis=1,
    )
    placed = matmul(chosen, got)
    turned = rotated_all(placed)
    copies[0].wait()
    sol = matmul(inverse_ref[0], placed.astype(BF16))
    copies[1].wait()
    sol = sol + matmul(inverse_ref[1], turned.astype(BF16))
    sol_ref[...] = sol
    sol_copy = fetch(sol_ref, sol_hbm, sem.at[0])
    coef = apply_complex(basis_ref[0], basis_ref[1], sol)
    first, second = coef[:, :LANES], coef[:, LANES:]
    odd = bit_ref[0] == 1
    own_ref[...] = jnp.where(odd, second, first)
    other_ref[...] = jnp.where(odd, first, second)
    sol_copy.wait()


def node_rhs(upper, own, partner):
    is_upper = upper == 1
    return jnp.concatenate(
        [jnp.where(is_upper, partner, own), jnp.where(is_upper, own, partner)], axis=0
    )


def node_kernel(bit_ref, own_ref, partner_ref, inverse_ref, basis_ref, sol_ref, coef_ref):
    rhs = node_rhs(bit_ref[0], own_ref[...], partner_ref[...])
    sol = apply_complex(inverse_ref[0], inverse_ref[1], rhs)
    sol_ref[...] = sol
    coef_ref[...] = apply_complex(basis_ref[0], basis_ref[1], sol)


def descent_kernel(bits_ref, own_ref, partner_ref, inverse_ref, lift_ref, *refs):
    levels = bits_ref.shape[0]
    below = levels - 1
    sols, coefs = refs[:below], refs[below : 2 * below]
    mine_ref, other_ref = refs[2 * below :]
    rank = own_ref.shape[0]

    def half(bit):
        return pl.ds(pl.multiple_of(bit * rank, rank), rank)

    rhs = node_rhs(bits_ref[below], own_ref[...], partner_ref[...])
    rows = half(bits_ref[below])
    down = apply_complex(inverse_ref[0, rows, :], inverse_ref[1, rows, :], rhs)
    for k in range(below - 1, 0, -1):
        gap = coefs[k][...] - down
        rows = half(bits_ref[k])
        down = sols[k][rows, :] - apply_complex(lift_ref[k, 0, rows, :], lift_ref[k, 1, rows, :], gap)
    gap = coefs[0][...] - down
    down = sols[0][...] - apply_complex(lift_ref[0, 0], lift_ref[0, 1], gap)
    swap = bits_ref[0] == 1
    mine_ref[...] = jnp.where(swap, down[rank:], down[:rank])
    other_ref[...] = jnp.where(swap, down[:rank], down[rank:])


def finish_kernel(
    bit_ref, mine_ref, others_ref, own_ref, other_ref, sol_hbm, lift_hbm, place_ref, send_ref,
    sol_ref, lift_ref, sem, *, devices, capacity,
):
    lift_copy = fetch(lift_hbm, lift_ref, sem.at[0])
    sol_copy = fetch(sol_hbm, sol_ref, sem.at[1])
    leaf_rows = sol_ref.shape[0]
    chosen = wide_one_hot(place_ref[...], leaf_rows // LANES)
    swap = bit_ref[0] == 1
    mine = own_ref[...] - mine_ref[...]
    other = other_ref[...] - others_ref[...]
    gap = jnp.concatenate([jnp.where(swap, other, mine), jnp.where(swap, mine, other)], axis=1)
    lift_copy.wait()
    change = apply_complex(lift_ref[0], lift_ref[1], gap)
    sol_copy.wait()
    sol = sol_ref[...] - change
    code = scale_code(sol)
    level = jnp.clip(jnp.round(sol * inverse_unit_of(code)), -32767.0, 32767.0)
    high = jnp.round(level * (1.0 / 256.0))
    low = level - high * 256.0
    parts = jnp.concatenate([high.astype(BF16), low.astype(BF16)], axis=1)
    both = matmul(chosen, parts)
    width = sol.shape[1]
    level = (both[:, :width] * 256.0 + both[:, width:]).astype(jnp.int32).astype(jnp.int16)
    send_ref[:, :capacity, :] = level[:, :LANES].reshape(devices, capacity, LANES)
    send_ref[:, capacity : 2 * capacity, :] = level[:, LANES:].reshape(devices, capacity, LANES)
    extra = (EXTRA, LANES)
    extra = jnp.where(
        iota(extra, 0) < EXTRA // 2,
        jnp.broadcast_to(code[:, :LANES], extra),
        jnp.broadcast_to(code[:, LANES:], extra),
    )
    extra = extra.astype(jnp.int32).astype(jnp.int16)
    send_ref[:, 2 * capacity :, :] = jnp.broadcast_to(
        extra.reshape(1, EXTRA, LANES), (devices, EXTRA, LANES)
    )


def unpack_kernel(got_ref, slot_ref, out_ref, *, devices, capacity):
    leaf_rows = out_ref.shape[0]
    slots = devices * capacity
    extra = got_ref[:, 2 * capacity :, :].astype(jnp.int32).astype(F32)
    halves = []
    for half in range(2):
        level = got_ref[:, half * capacity : (half + 1) * capacity, :]
        level = level.astype(jnp.int32).astype(F32)
        unit = unit_of(extra[:, half * (EXTRA // 2) : half * (EXTRA // 2) + 1, :])
        halves.append((level * unit).reshape(slots, LANES))
    both = two_parts(jnp.concatenate(halves, axis=1))
    chosen = wide_one_hot(slot_ref[...], slots // LANES)
    result = folded(matmul(chosen, both))
    first, second = swapped(result[:, :LANES], result[:, LANES:])
    out_ref[:, :LANES] = first
    out_ref[:, LANES:] = second


def call(kernel, outs, operands, scratch=(), vmem=24):
    specs = {
        "smem": pl.BlockSpec(memory_space=pltpu.SMEM),
        "vmem": pl.BlockSpec(memory_space=pltpu.VMEM),
        "hbm": pl.BlockSpec(memory_space=pl.ANY),
        "any": pl.BlockSpec(memory_space=pl.ANY),
    }
    results = pl.pallas_call(
        kernel,
        out_shape=[pltpu.HBM(out.shape, out.dtype) if space == "hbm" else out for out, space in outs],
        in_specs=[specs[space] for _, space in operands],
        out_specs=[specs[space] for _, space in outs],
        scratch_shapes=[
            pltpu.SemaphoreType.DMA((one,)) if isinstance(one, int) else pltpu.VMEM(one.shape, one.dtype)
            for one in scratch
        ],
        compiler_params=pltpu.CompilerParams(vmem_limit_bytes=vmem * 2**20),
    )(
        *[
            pltpu.with_memory_space_constraint(array, pltpu.HBM) if space == "hbm" else array
            for array, space in operands
        ]
    )
    return results


def shape(dims, dtype=F32):
    return jax.ShapeDtypeStruct(dims, dtype)


def from_partner(shard, axis, apart):
    return lax.ppermute(shard, axis, [(i, i ^ 1 << apart) for i in range(lax.axis_size(axis))])


def tree_bit(height, col_levels):
    if height < col_levels:
        return lax.axis_index("col") >> height & 1
    return lax.axis_index("row") >> height - col_levels & 1


def per_device(
    right_sides, tree_order, leaf_inverse, leaf_basis, leaf_lift, node_inverse, node_basis, node_lift
):
    row_count = lax.axis_size("row")
    col_count = lax.axis_size("col")
    devices = row_count * col_count
    col_levels = col_count.bit_length() - 1
    levels = col_levels + row_count.bit_length() - 1
    leaf_rows, width = right_sides.shape
    rank = leaf_basis.shape[3]
    capacity = 2 * leaf_rows // min(devices, leaf_rows // 8)
    block = (devices, 2 * capacity + EXTRA, LANES)
    sizes = dict(devices=devices, capacity=capacity)
    me = (lax.axis_index("row") * col_count + lax.axis_index("col")).astype(jnp.int32)
    bits = [tree_bit(height, col_levels).astype(jnp.int32) for height in range(levels)]

    def exchange(blocks):
        return lax.all_to_all(blocks, ("row", "col"), split_axis=0, concat_axis=0, tiled=True)

    def partner_of(shard, height):
        if height < col_levels:
            return from_partner(shard, "col", height)
        return from_partner(shard, "row", height - col_levels)

    send, slot = call(
        functools.partial(pack_kernel, **sizes),
        [(shape(block, BF16), "vmem"), (shape((leaf_rows // LANES, LANES)), "vmem")],
        [(me.reshape(1), "smem"), (tree_order.reshape(1, leaf_rows), "hbm"), (right_sides, "hbm")],
        [shape((1, leaf_rows), jnp.int32), shape(right_sides.shape, BF16), 2],
    )
    def load(after, weights, picks, turned=0, stores=()):
        shapes = [jax.eval_shape(lambda w, pick=pick: w[pick], w) for w, pick in zip(weights, picks)]
        plain = len(weights) - turned
        outs = [shape(one.shape, one.dtype) for one in shapes[:plain]]
        outs += [shape((2, one.shape[2], one.shape[1]), one.dtype) for one in shapes[plain:]]
        return call(
            functools.partial(load_kernel, picks=picks, turned=turned, stores=len(stores)),
            [(out, "vmem") for out in outs] + [(shape(one.shape), "hbm") for one in stores],
            [(after, "any")] + [(weight, "hbm") for weight in weights] + [(one, "any") for one in stores],
            [shape(one.shape, one.dtype) for one in shapes[plain:]] + [len(weights) + len(stores)],
            vmem=6,
        )

    got = exchange(send)
    (leaf_basis,) = load(slot, (leaf_basis,), (0,), turned=1)
    half = shape((rank, LANES))
    leaf_sol, own, other, place = call(
        functools.partial(leaf_kernel, **sizes),
        [
            (shape((leaf_rows, width)), "hbm"),
            (half, "vmem"),
            (half, "vmem"),
            (shape((devices * capacity // LANES, LANES)), "vmem"),
        ],
        [(bits[0].reshape(1), "smem"), (got, "vmem"), (leaf_inverse, "hbm"), (leaf_basis, "vmem")],
        [shape(leaf_inverse.shape[1:], BF16), shape((leaf_rows, width)), 3],
    )
    leaf_own, leaf_other = own, other
    whole = shape((2 * rank, LANES))
    sols, stored, coefs = [], [], []
    for height in range(1, levels):
        partner = partner_of(other if height == 1 else own, height - 1)
        pick = (0, height - 1)
        inverse, basis, *kept = load(own, (node_inverse, node_basis), (pick, pick), 1, sols[-1:])
        stored += kept
        sol, own = call(
            node_kernel,
            [(whole, "vmem"), (half, "vmem")],
            [
                (bits[height - 1].reshape(1), "smem"),
                (own, "vmem"),
                (partner, "vmem"),
                (inverse, "vmem"),
                (basis, "vmem"),
            ],
            vmem=8,
        )
        sols.append(sol)
        coefs.append(own)
    partner = partner_of(own, levels - 1)
    inverse, lift, *stored = load(
        own, (node_inverse, node_lift, *stored), ((0, levels - 1), 0) + (slice(None),) * len(stored)
    )
    sols = stored + sols[-1:]
    mine, other = call(
        descent_kernel,
        [(half, "vmem"), (half, "vmem")],
        [(jnp.stack(bits), "smem"), (own, "vmem"), (partner, "vmem"), (inverse, "vmem"), (lift, "vmem")]
        + [(sol, "vmem") for sol in sols]
        + [(coef, "vmem") for coef in coefs],
        vmem=8,
    )
    other = partner_of(other, 0)
    (back,) = call(
        functools.partial(finish_kernel, **sizes),
        [(shape(block, jnp.int16), "vmem")],
        [
            (bits[0].reshape(1), "smem"),
            (mine, "vmem"),
            (other, "vmem"),
            (leaf_own, "vmem"),
            (leaf_other, "vmem"),
            (leaf_sol, "hbm"),
            (leaf_lift[0], "hbm"),
            (place, "vmem"),
        ],
        [shape((leaf_rows, width)), shape(leaf_lift.shape[1:], BF16), 2],
    )
    returned = exchange(back)
    (result,) = call(
        functools.partial(unpack_kernel, **sizes),
        [(shape((leaf_rows, width)), "vmem")],
        [(returned, "vmem"), (slot, "vmem")],
    )
    return result


def solution(mesh):
    in_specs = (
        P(("row", "col"), None),
        P(("row", "col")),
        P(("row", "col"), None, None, None),
        P(("row", "col"), None, None, None),
        P(("row", "col"), None, None, None),
        P(("row", "col"), None, None, None, None),
        P(("row", "col"), None, None, None, None),
        P(("row", "col"), None, None, None, None),
    )
    out_specs = P(("row", "col"), None)
    return jax.shard_map(
        per_device, mesh=mesh, in_specs=in_specs, out_specs=out_specs, check_vma=False
    )
```

```python
import functools

import jax
import jax.numpy as jnp
from jax import lax
from jax.experimental import pallas as pl
from jax.experimental.pallas import tpu as pltpu
from jax.sharding import PartitionSpec as P

LANES = 128
EXTRA = 8
CODE_BASE = 32
SCALE_STEPS = 64
HEADROOM = 1.002
ROUNDER = 1.5 * 2.0**23
TAIL = 16
STEP = 256
PIECES = 4
BF16 = jnp.bfloat16
F32 = jnp.float32


def whole_matmul(a, b):
    return lax.dot_general(a, b, (((1,), (0,)), ((), ())), preferred_element_type=F32)


def matmul(a, b):
    pieces = [whole_matmul(a[at : at + STEP], b) for at in range(0, a.shape[0], STEP)]
    return pieces[0] if len(pieces) == 1 else jnp.concatenate(pieces, axis=0)


def matmul_nt(a, b):
    return lax.dot_general(a, b, (((1,), (1,)), ((), ())), preferred_element_type=F32)


def iota(shape, dim):
    return lax.broadcasted_iota(jnp.int32, shape, dim)


def rotated(x):
    if x.shape[1] == LANES:
        turned = pltpu.roll(x, LANES // 2, 1)
        return jnp.where(iota(x.shape, 1) < LANES // 2, -turned, turned)
    return jnp.concatenate([-x[:, LANES:], x[:, :LANES]], axis=1)


def swapped(first, second):
    low = iota(first.shape, 1) < LANES // 2
    return (
        jnp.where(low, first, pltpu.roll(second, LANES // 2, 1)),
        jnp.where(low, pltpu.roll(first, LANES // 2, 1), second),
    )


def two_parts(x):
    high = x.astype(BF16)
    low = (x - high.astype(F32)).astype(BF16)
    return jnp.concatenate([high, low], axis=1)


def folded(both):
    width = both.shape[1] // 2
    return both[:, :width] + both[:, width:]


def apply_complex(real, imag, x):
    return folded(matmul(real, two_parts(x)) + matmul(imag, two_parts(rotated(x))))


def unit_of(code):
    return jnp.exp2(code * (1.0 / SCALE_STEPS) - 15.0) * HEADROOM


def inverse_unit_of(code):
    return jnp.exp2(15.0 - code * (1.0 / SCALE_STEPS)) * (1.0 / HEADROOM)


def rounded(x):
    return (x + ROUNDER) - ROUNDER


def to_int16(x):
    return x.astype(jnp.int32).astype(jnp.int16)


def from_int16(x):
    return x.astype(jnp.int32).astype(F32)


def encoded(x):
    code = scale_code(x)
    level = rounded(x * inverse_unit_of(code))
    return to_int16(jnp.concatenate([level, jnp.broadcast_to(code, (TAIL, LANES))], axis=0))


def decoded(levels):
    values = from_int16(levels)
    return values[:-TAIL] * unit_of(values[-TAIL : 1 - TAIL])


def scale_code(x):
    largest = jnp.max(jnp.abs(x), axis=0, keepdims=True)
    return jnp.ceil(jnp.log2(jnp.maximum(largest, 2.0**-110)) * SCALE_STEPS)


def fetch(source, target, sem):
    copy = pltpu.make_async_copy(source, target, sem)
    copy.start()
    return copy


def wide_one_hot(columns, blocks):
    lane = iota((LANES, LANES), 1).astype(F32)
    one, zero = jnp.ones((), BF16), jnp.zeros((), BF16)
    names = []
    for entry in columns:
        block = jnp.floor(entry * (1.0 / LANES))
        names.append(jnp.where(lane == entry - block * LANES, block, -1.0))
    names = jnp.concatenate(names, axis=0).astype(BF16)
    return jnp.concatenate([jnp.where(names == jnp.array(g, BF16), one, zero) for g in range(blocks)], axis=1)


def row_blocks(x):
    return jnp.concatenate([x[:, at : at + LANES] for at in range(0, x.shape[1], LANES)], axis=0)


def ranks(hits):
    rows, width = hits.shape
    upper = (iota((LANES, LANES), 0) < iota((LANES, LANES), 1)).astype(F32).astype(BF16)
    pieces = jnp.concatenate(
        [hits[:, at : at + LANES] for at in range(0, width, LANES)], axis=0
    ).astype(BF16)
    inside = matmul(pieces, upper)
    totals = matmul(pieces, jnp.ones((LANES, LANES), BF16))
    ahead = jnp.zeros((rows, LANES), F32)
    parts = []
    for k in range(width // LANES):
        parts.append(inside[k * rows : (k + 1) * rows] + ahead)
        ahead = ahead + totals[k * rows : (k + 1) * rows]
    return jnp.concatenate(parts, axis=1)


def pack_kernel(
    me_ref, order_hbm, rows_hbm, send_hbm, slot_ref, order_ref, rows_ref, chosen_ref, send_ref, sem, *,
    devices, capacity,
):
    order_copy = fetch(order_hbm, order_ref, sem.at[0])
    rows_copy = fetch(rows_hbm, rows_ref, sem.at[1])
    leaf_rows = rows_ref.shape[0]
    order_copy.wait()
    order = order_ref[...]
    target = order // leaf_rows
    position = order - target * leaf_rows
    hits = (iota((devices, leaf_rows), 0) == target).astype(F32)
    rank = jnp.sum(hits * ranks(hits), axis=0, keepdims=True).astype(jnp.int32)
    slot_ref[...] = row_blocks((target * capacity + rank).astype(F32))
    group = LANES // capacity
    lane = rank + lax.rem(me_ref[0], group) * capacity
    high = position // CODE_BASE
    low = position - high * CODE_BASE
    codes = jnp.concatenate([hits * (high + 1).astype(F32), hits * low.astype(F32)], axis=0)
    places = (iota((LANES, leaf_rows), 0) == lane).astype(F32).astype(BF16)
    spread = matmul_nt(codes.astype(BF16), places)
    extra = (devices, EXTRA, LANES)
    send_ref[:, 2 * capacity :, :] = jnp.where(
        iota(extra, 1) < EXTRA // 2,
        jnp.broadcast_to(spread[:devices].reshape(devices, 1, LANES), extra),
        jnp.broadcast_to(spread[devices:].reshape(devices, 1, LANES), extra),
    ).astype(BF16)
    in_slot = (iota((capacity, leaf_rows), 0) == rank).astype(F32).astype(BF16)
    hits = hits.astype(BF16)
    for t in range(devices):
        chosen_ref[t * capacity : (t + 1) * capacity, :] = in_slot * hits[t : t + 1, :]
    rows_copy.wait()
    count = devices // PIECES
    copies = []
    for piece in range(PIECES):
        blocks = pl.ds(piece * count, count)
        sent = matmul(chosen_ref[pl.ds(piece * count * capacity, count * capacity), :], rows_ref[...])
        sent = sent.astype(BF16)
        send_ref[blocks, :capacity, :] = sent[:, :LANES].reshape(count, capacity, LANES)
        send_ref[blocks, capacity : 2 * capacity, :] = sent[:, LANES:].reshape(count, capacity, LANES)
        copies.append(fetch(send_ref.at[blocks], send_hbm.at[blocks], sem.at[2 + piece]))
    for copy in copies:
        copy.wait()


def codes_of(got_ref, devices, capacity):
    group = LANES // capacity
    extra = got_ref[:, 2 * capacity :, :].astype(F32)
    return [sum(extra[k + g] for g in range(group)) for k in range(0, devices, group)]


def load_kernel(after_ref, *refs, picks, turned, stores, rows_of, groups, kept):
    refs = list(refs)

    def take(count):
        taken = refs[:count]
        del refs[:count]
        return taken

    count = len(picks)
    plain = count - turned
    gathers = 1 if rows_of else 0
    sources, stored, given = take(count), take(stores), take(2 * gathers)
    targets, held, gathered = take(count), take(stores), take(gathers)
    scratch, chosen, landed = take(turned), take(gathers), take(rows_of == "lift")
    work, (sem,) = take(gathers and not kept), refs
    landing = targets[:plain] + scratch
    if landed:
        lift_copy = fetch(given[1].at[0], landed[0], sem.at[count + stores])
    copies = [
        fetch(source.at[pick], target, sem.at[k])
        for k, (source, target, pick) in enumerate(zip(sources, landing, picks))
    ]
    copies += [fetch(stored[k], held[k], sem.at[count + k]) for k in range(stores)]
    if rows_of:
        out_ref = gathered[0] if kept else work[0]
        (chosen_ref,) = chosen
        chosen_ref[...] = wide_one_hot(place_columns(given[0], groups), chosen_ref.shape[1] // LANES)
        if landed:
            lift_copy.wait()
            width = landed[0].shape[2]
            for part in range(2):
                columns = slice(part * width, (part + 1) * width)
                out_ref[:, columns] = matmul(chosen_ref[...], landed[0][part]).astype(BF16)
        else:
            out_ref[...] = folded(matmul(chosen_ref[...], given[1][...]))
        if not kept:
            copies.append(fetch(out_ref, gathered[0], sem.at[count + stores + 1]))
    for k in range(turned):
        copies[plain + k].wait()
        for part in range(2):
            targets[plain + k][part] = jnp.transpose(scratch[k][part])
    for k, copy in enumerate(copies):
        if not plain <= k < count:
            copy.wait()


def place_columns(place_ref, groups):
    turned = jnp.transpose(place_ref[...])
    return [
        (turned[:, k * EXTRA : k * EXTRA + 1] - 1.0) * CODE_BASE
        + turned[:, k * EXTRA + EXTRA // 2 : k * EXTRA + EXTRA // 2 + 1]
        for k in range(*groups)
    ]


def place_kernel(
    got_ref, inverse_hbm, placed_ref, place_ref, inverse_ref, chosen_ref, rows_ref, sem, *, devices, capacity
):
    inverse_copy = fetch(inverse_hbm.at[0], inverse_ref, sem.at[0])
    leaf_rows = placed_ref.shape[0]
    codes = codes_of(got_ref, devices, capacity)
    place_ref[...] = jnp.concatenate(codes, axis=0)
    code = iota((CODE_BASE, LANES), 0).astype(F32)
    is_low = jnp.concatenate(
        [(code == one[EXTRA // 2 : EXTRA // 2 + 1]).astype(F32) for one in codes], axis=1
    ).astype(BF16)
    is_high = jnp.concatenate([(code == one[:1] - 1.0).astype(F32) for one in codes], axis=1).astype(BF16)
    for h in range(leaf_rows // CODE_BASE):
        chosen_ref[h * CODE_BASE : (h + 1) * CODE_BASE, :] = is_low * is_high[h : h + 1, :]
    slots = devices * capacity
    rows_ref[:, :LANES] = got_ref[:, :capacity, :].reshape(slots, LANES)
    rows_ref[:, LANES:] = got_ref[:, capacity : 2 * capacity, :].reshape(slots, LANES)
    placed_ref[...] = matmul(chosen_ref[...], rows_ref[...]).astype(BF16)
    inverse_copy.wait()


def leaf_kernel(placed_ref, inverse_ref, parts_ref):
    placed = placed_ref[...]
    parts_ref[...] = two_parts(matmul(inverse_ref[0], placed) + matmul(inverse_ref[1], rotated(placed)))


def coef_kernel(bit_ref, parts_ref, basis_ref, own_ref, other_ref):
    width = parts_ref.shape[1] // 2
    parts = parts_ref[...]
    turned = jnp.concatenate([rotated(parts[:, :width]), rotated(parts[:, width:])], axis=1)
    coef = folded(matmul(basis_ref[0], parts) + matmul(basis_ref[1], turned))
    first, second = swapped(coef[:, :LANES], coef[:, LANES:])
    odd = bit_ref[0] == 1
    own_ref[...] = jnp.where(odd, second, first)
    other_ref[...] = jnp.where(odd, first, second)


def node_rhs(upper, own, partner):
    is_upper = upper == 1
    return jnp.concatenate(
        [jnp.where(is_upper, partner, own), jnp.where(is_upper, own, partner)], axis=0
    )


def node_kernel(bit_ref, own_ref, partner_ref, inverse_ref, basis_ref, sol_ref, coef_ref, code_ref):
    partner = partner_ref[...]
    rhs = node_rhs(bit_ref[0], own_ref[...], partner if partner.dtype == F32 else decoded(partner))
    sol = apply_complex(inverse_ref[0], inverse_ref[1], rhs)
    sol_ref[...] = sol
    coef = apply_complex(basis_ref[0], basis_ref[1], sol)
    coef_ref[...] = coef
    code_ref[...] = encoded(coef)


def fetch_pieces(pieces, target, sem):
    copies, at = [], 0
    for k, piece in enumerate(pieces):
        copies.append(fetch(piece, target.at[pl.ds(at, piece.shape[0])], sem.at[k]))
        at += piece.shape[0]
    return copies


def descent_kernel(bits_ref, own_ref, partner_ref, inverse_ref, lift_hbm, *refs):
    levels = bits_ref.shape[0]
    below = levels - 1
    sols, coefs = refs[:below], refs[below : 2 * below]
    gathered = refs[2 * below : -5]
    mine_ref, other_ref, moved_ref, lift_ref, sem = refs[-5:]
    lift_copies = [
        fetch(lift_hbm.at[0, k], lift_ref.at[k], sem.at[len(gathered) + k]) for k in range(below - 1, -1, -1)
    ]
    rank = own_ref.shape[0]
    copies = fetch_pieces(gathered, moved_ref, sem)

    def half(bit):
        return pl.ds(pl.multiple_of(bit * rank, rank), rank)

    rhs = node_rhs(bits_ref[below], own_ref[...], decoded(partner_ref[...]))
    rows = half(bits_ref[below])
    down = apply_complex(inverse_ref[0, rows, :], inverse_ref[1, rows, :], rhs)
    for k in range(below - 1, 0, -1):
        gap = coefs[k][...] - down
        rows = half(bits_ref[k])
        lift_copies[below - 1 - k].wait()
        down = sols[k][rows, :] - apply_complex(lift_ref[k, 0, rows, :], lift_ref[k, 1, rows, :], gap)
    gap = coefs[0][...] - down
    lift_copies[-1].wait()
    down = sols[0][...] - apply_complex(lift_ref[0, 0], lift_ref[0, 1], gap)
    swap = bits_ref[0] == 1
    mine_ref[...] = jnp.where(swap, down[rank:], down[:rank])
    other_ref[...] = jnp.where(swap, down[:rank], down[rank:])
    for copy in copies:
        copy.wait()


def finish_kernel(
    bit_ref, mine_ref, others_ref, own_ref, other_ref, *refs, devices, capacity
):
    *pieces, send_ref = refs
    moved, pieces = pieces[:2], pieces[2:]
    swap = bit_ref[0] == 1
    mine = own_ref[...] - mine_ref[...]
    other = other_ref[...] - others_ref[...]
    first, second = swapped(jnp.where(swap, other, mine), jnp.where(swap, mine, other))
    gap = jnp.concatenate([first, second], axis=1)
    rank, width = gap.shape
    moved = jnp.concatenate([piece[...] for piece in moved], axis=0)
    change = matmul(moved[:, :rank], two_parts(gap)) + matmul(moved[:, rank:], two_parts(rotated(gap)))
    sol = jnp.concatenate([piece[...] for piece in pieces], axis=0) - folded(change)
    code = scale_code(sol)
    level = to_int16(rounded(sol * inverse_unit_of(code)))
    send_ref[:, :capacity, :] = level[:, :LANES].reshape(devices, capacity, LANES)
    send_ref[:, capacity : 2 * capacity, :] = level[:, LANES:].reshape(devices, capacity, LANES)
    extra = (EXTRA, LANES)
    extra = jnp.where(
        iota(extra, 0) < EXTRA // 2,
        jnp.broadcast_to(code[:, :LANES], extra),
        jnp.broadcast_to(code[:, LANES:], extra),
    )
    extra = to_int16(extra)
    send_ref[:, 2 * capacity :, :] = jnp.broadcast_to(
        extra.reshape(1, EXTRA, LANES), (devices, EXTRA, LANES)
    )


def unpack_kernel(got_ref, slot_ref, out_ref, *, devices, capacity):
    slots = devices * capacity
    turned = jnp.transpose(slot_ref[...])
    chosen = wide_one_hot([turned[:, k : k + 1] for k in range(turned.shape[1])], slots // LANES)
    extra = from_int16(got_ref[:, 2 * capacity :, :])
    halves = []
    for half in range(2):
        level = from_int16(got_ref[:, half * capacity : (half + 1) * capacity, :])
        unit = unit_of(extra[:, half * (EXTRA // 2) : half * (EXTRA // 2) + 1, :])
        halves.append((level * unit).reshape(slots, LANES))
    parts = two_parts(jnp.concatenate(halves, axis=1))
    out_ref[...] = folded(whole_matmul(chosen, parts))


def call(kernel, outs, operands, scratch=(), vmem=24):
    specs = {
        "smem": pl.BlockSpec(memory_space=pltpu.SMEM),
        "vmem": pl.BlockSpec(memory_space=pltpu.VMEM),
        "hbm": pl.BlockSpec(memory_space=pl.ANY),
        "any": pl.BlockSpec(memory_space=pl.ANY),
    }
    results = pl.pallas_call(
        kernel,
        out_shape=[pltpu.HBM(out.shape, out.dtype) if space == "hbm" else out for out, space in outs],
        in_specs=[specs[space] for _, space in operands],
        out_specs=[specs[space] for _, space in outs],
        scratch_shapes=[
            pltpu.SemaphoreType.DMA((one,)) if isinstance(one, int) else pltpu.VMEM(one.shape, one.dtype)
            for one in scratch
        ],
        compiler_params=pltpu.CompilerParams(vmem_limit_bytes=vmem * 2**20),
    )(
        *[
            pltpu.with_memory_space_constraint(array, pltpu.HBM) if space == "hbm" else array
            for array, space in operands
        ]
    )
    return results


def shape(dims, dtype=F32):
    return jax.ShapeDtypeStruct(dims, dtype)


def from_partner(shard, axis, apart):
    return lax.ppermute(shard, axis, [(i, i ^ 1 << apart) for i in range(lax.axis_size(axis))])


def tree_bit(height, col_levels):
    if height < col_levels:
        return lax.axis_index("col") >> height & 1
    return lax.axis_index("row") >> height - col_levels & 1


def per_device(
    right_sides, tree_order, leaf_inverse, leaf_basis, leaf_lift, node_inverse, node_basis, node_lift
):
    row_count = lax.axis_size("row")
    col_count = lax.axis_size("col")
    devices = row_count * col_count
    col_levels = col_count.bit_length() - 1
    levels = col_levels + row_count.bit_length() - 1
    leaf_rows, width = right_sides.shape
    rank = leaf_basis.shape[3]
    capacity = 2 * leaf_rows // min(devices, leaf_rows // 8)
    block = (devices, 2 * capacity + EXTRA, LANES)
    sizes = dict(devices=devices, capacity=capacity)
    me = (lax.axis_index("row") * col_count + lax.axis_index("col")).astype(jnp.int32)
    bits = [tree_bit(height, col_levels).astype(jnp.int32) for height in range(levels)]

    def exchange(blocks):
        return lax.all_to_all(blocks, ("row", "col"), split_axis=0, concat_axis=0, tiled=True)

    def partner_of(shard, height):
        if height < col_levels:
            return from_partner(shard, "col", height)
        return from_partner(shard, "row", height - col_levels)

    send, slot = call(
        functools.partial(pack_kernel, **sizes),
        [(shape(block, BF16), "hbm"), (shape((leaf_rows // LANES, LANES)), "vmem")],
        [(me.reshape(1), "smem"), (tree_order.reshape(1, leaf_rows), "hbm"), (right_sides, "hbm")],
        [
            shape((1, leaf_rows), jnp.int32),
            shape(right_sides.shape, BF16),
            shape((devices * capacity, leaf_rows), BF16),
            shape(block, BF16),
            2 + PIECES,
        ],
    )
    slots = devices * capacity
    total = slots // LANES
    gathers = {
        levels - 3: ("sol", (0, total // 2), False),
        levels - 2: ("sol", (total // 2, total), False),
        levels - 1: ("lift", (0, 3 * total // 8), False),
        levels: ("lift", (3 * total // 8, total), True),
    }

    def load(after, weights, picks, turned=0, stores=(), gather=("", (0, 0), False)):
        shapes = [jax.eval_shape(lambda w, pick=pick: w[pick], w) for w, pick in zip(weights, picks)]
        plain = len(weights) - turned
        outs = [shape(one.shape, one.dtype) for one in shapes[:plain]]
        outs += [shape((2, one.shape[2], one.shape[1]), one.dtype) for one in shapes[plain:]]
        rows_of, groups, kept = gather
        rows = (groups[1] - groups[0]) * LANES
        taken = {
            "": [],
            "sol": [shape((rows, width))],
            "lift": [shape((rows, 2 * rank), BF16)],
        }[rows_of]
        given = {"": [], "sol": [(place, "vmem"), (parts, "vmem")], "lift": [(place, "vmem"), (leaf_lift, "hbm")]}
        work = [shape((rows, leaf_rows), BF16)] if rows_of else []
        work += [shape(leaf_lift.shape[1:], BF16)] if rows_of == "lift" else []
        work += [] if kept else taken
        return call(
            functools.partial(
                load_kernel,
                picks=picks,
                turned=turned,
                stores=len(stores),
                rows_of=rows_of,
                groups=groups,
                kept=kept,
            ),
            [(out, "vmem") for out in outs]
            + [(shape(one.shape), "hbm") for one in stores]
            + [(one, "vmem" if kept else "hbm") for one in taken],
            [(after, "any")]
            + [(weight, "hbm") for weight in weights]
            + [(one, "any") for one in stores]
            + given[rows_of],
            [shape(one.shape, one.dtype) for one in shapes[plain:]]
            + work
            + [len(weights) + len(stores) + 2 * bool(rows_of)],
            vmem=14 if rows_of else 6,
        )

    place = parts = None
    got = exchange(send)
    (leaf_basis,) = load(slot, (leaf_basis,), (0,), turned=1)
    half = shape((rank, LANES))
    placed, place, inverse = call(
        functools.partial(place_kernel, **sizes),
        [
            (shape((leaf_rows, width), BF16), "vmem"),
            (shape((slots // LANES * EXTRA, LANES)), "vmem"),
            (shape(leaf_inverse.shape[1:], BF16), "vmem"),
        ],
        [(got, "vmem"), (leaf_inverse, "hbm")],
        [shape((leaf_rows, slots), BF16), shape((slots, width), BF16), 1],
    )
    (parts,) = call(
        leaf_kernel,
        [(shape((leaf_rows, 2 * width), BF16), "vmem")],
        [(placed, "vmem"), (inverse, "vmem")],
    )
    own, other = call(
        coef_kernel,
        [(half, "vmem"), (half, "vmem")],
        [(bits[0].reshape(1), "smem"), (parts, "vmem"), (leaf_basis, "vmem")],
    )
    leaf_own, leaf_other = own, other
    whole = shape((2 * rank, LANES))
    sols, stored, coefs, gathered = [], [], [], []
    no_gather = ("", (0, 0), False)
    for height in range(1, levels):
        partner = partner_of(other if height == 1 else code, height - 1)
        pick = (0, height - 1)
        inverse, basis, *kept = load(
            own, (node_inverse, node_basis), (pick, pick), 1, sols[-1:], gathers.get(height, no_gather)
        )
        stored += kept[: len(sols[-1:])]
        gathered += kept[len(sols[-1:]) :]
        sol, own, code = call(
            node_kernel,
            [(whole, "vmem"), (half, "vmem"), (shape((rank + TAIL, LANES), jnp.int16), "vmem")],
            [
                (bits[height - 1].reshape(1), "smem"),
                (own, "vmem"),
                (partner, "vmem"),
                (inverse, "vmem"),
                (basis, "vmem"),
            ],
            vmem=8,
        )
        sols.append(sol)
        coefs.append(own)
    partner = partner_of(code, levels - 1)
    inverse, *kept = load(
        own,
        (node_inverse, *stored),
        ((0, levels - 1),) + (slice(None),) * len(stored),
        gather=gathers[levels],
    )
    sols = kept[: len(stored)] + sols[-1:]
    gathered += kept[len(stored) :]
    mine, other, moved = call(
        descent_kernel,
        [
            (half, "vmem"),
            (half, "vmem"),
            (shape(gathered[2].shape, BF16), "vmem"),
        ],
        [(jnp.stack(bits), "smem"), (own, "vmem"), (partner, "vmem"), (inverse, "vmem"), (node_lift, "hbm")]
        + [(sol, "vmem") for sol in sols]
        + [(coef, "vmem") for coef in coefs]
        + [(one, "hbm") for one in gathered[2:-1]],
        [shape(node_lift.shape[1:], BF16), len(gathered) - 3 + levels - 1],
        vmem=12,
    )
    other_sent = other
    other = partner_of(other_sent, 0)
    bases = load(other_sent, gathered[:2], (slice(None),) * 2)
    (back,) = call(
        functools.partial(finish_kernel, **sizes),
        [(shape(block, jnp.int16), "vmem")],
        [
            (bits[0].reshape(1), "smem"),
            (mine, "vmem"),
            (other, "vmem"),
            (leaf_own, "vmem"),
            (leaf_other, "vmem"),
            (moved, "vmem"),
            (gathered[-1], "vmem"),
        ]
        + [(one, "vmem") for one in bases],
    )
    returned = exchange(back)
    (result,) = call(
        functools.partial(unpack_kernel, **sizes),
        [(shape((leaf_rows, width)), "vmem")],
        [(returned, "vmem"), (slot, "vmem")],
    )
    return result


def solution(mesh):
    in_specs = (
        P(("row", "col"), None),
        P(("row", "col")),
        P(("row", "col"), None, None, None),
        P(("row", "col"), None, None, None),
        P(("row", "col"), None, None, None),
        P(("row", "col"), None, None, None, None),
        P(("row", "col"), None, None, None, None),
        P(("row", "col"), None, None, None, None),
    )
    out_specs = P(("row", "col"), None)
    return jax.shard_map(
        per_device, mesh=mesh, in_specs=in_specs, out_specs=out_specs, check_vma=False
    )
```

```python
import functools

import jax
import jax.numpy as jnp
from jax import lax
from jax.experimental import pallas as pl
from jax.experimental.pallas import tpu as pltpu
from jax.sharding import PartitionSpec as P

LANES = 128
EXTRA = 8
CODE_BASE = 32
SCALE_STEPS = 64
HEADROOM = 1.002
ROUNDER = 1.5 * 2.0**23
TAIL = 16
STEP = 256
PIECES = 4
BF16 = jnp.bfloat16
F32 = jnp.float32


def whole_matmul(a, b):
    return lax.dot_general(a, b, (((1,), (0,)), ((), ())), preferred_element_type=F32)


def matmul(a, b):
    pieces = [whole_matmul(a[at : at + STEP], b) for at in range(0, a.shape[0], STEP)]
    return pieces[0] if len(pieces) == 1 else jnp.concatenate(pieces, axis=0)


def matmul_nt(a, b):
    return lax.dot_general(a, b, (((1,), (1,)), ((), ())), preferred_element_type=F32)


def tree_bits(levels):
    index = lax.axis_index("row") * lax.axis_size("col") + lax.axis_index("col")
    return [index >> height & 1 for height in range(levels)]


def iota(shape, dim):
    return lax.broadcasted_iota(jnp.int32, shape, dim)


def rotated(x):
    if x.shape[1] == LANES:
        turned = pltpu.roll(x, LANES // 2, 1)
        return jnp.where(iota(x.shape, 1) < LANES // 2, -turned, turned)
    return jnp.concatenate([-x[:, LANES:], x[:, :LANES]], axis=1)


def swapped(first, second):
    low = iota(first.shape, 1) < LANES // 2
    return (
        jnp.where(low, first, pltpu.roll(second, LANES // 2, 1)),
        jnp.where(low, pltpu.roll(first, LANES // 2, 1), second),
    )


def two_parts(x):
    high = x.astype(BF16)
    low = (x - high.astype(F32)).astype(BF16)
    return jnp.concatenate([high, low], axis=1)


def folded(both):
    width = both.shape[1] // 2
    return both[:, :width] + both[:, width:]


def apply_complex(real, imag, x):
    return folded(matmul(real, two_parts(x)) + matmul(imag, two_parts(rotated(x))))


def unit_of(code):
    return jnp.exp2(code * (1.0 / SCALE_STEPS) - 15.0) * HEADROOM


def inverse_unit_of(code):
    return jnp.exp2(15.0 - code * (1.0 / SCALE_STEPS)) * (1.0 / HEADROOM)


def rounded(x):
    return (x + ROUNDER) - ROUNDER


def to_int16(x):
    return x.astype(jnp.int32).astype(jnp.int16)


def from_int16(x):
    return x.astype(jnp.int32).astype(F32)


def encoded(x):
    code = scale_code(x)
    level = rounded(x * inverse_unit_of(code))
    return to_int16(jnp.concatenate([level, jnp.broadcast_to(code, (TAIL, LANES))], axis=0))


def decoded(levels):
    values = from_int16(levels)
    return values[:-TAIL] * unit_of(values[-TAIL : 1 - TAIL])


def scale_code(x):
    largest = jnp.max(jnp.abs(x), axis=0, keepdims=True)
    return jnp.ceil(jnp.log2(jnp.maximum(largest, 2.0**-110)) * SCALE_STEPS)


def fetch(source, target, sem):
    copy = pltpu.make_async_copy(source, target, sem)
    copy.start()
    return copy


def wide_one_hot(columns, blocks):
    lane = iota((LANES, LANES), 1).astype(F32)
    one, zero = jnp.ones((), BF16), jnp.zeros((), BF16)
    names = []
    for entry in columns:
        block = jnp.floor(entry * (1.0 / LANES))
        names.append(jnp.where(lane == entry - block * LANES, block, -1.0))
    names = jnp.concatenate(names, axis=0).astype(BF16)
    return jnp.concatenate([jnp.where(names == jnp.array(g, BF16), one, zero) for g in range(blocks)], axis=1)


def row_blocks(x):
    return jnp.concatenate([x[:, at : at + LANES] for at in range(0, x.shape[1], LANES)], axis=0)


def ranks(hits):
    rows, width = hits.shape
    upper = (iota((LANES, LANES), 0) < iota((LANES, LANES), 1)).astype(F32).astype(BF16)
    pieces = jnp.concatenate(
        [hits[:, at : at + LANES] for at in range(0, width, LANES)], axis=0
    ).astype(BF16)
    inside = matmul(pieces, upper)
    totals = matmul(pieces, jnp.ones((LANES, LANES), BF16))
    ahead = jnp.zeros((rows, LANES), F32)
    parts = []
    for k in range(width // LANES):
        parts.append(inside[k * rows : (k + 1) * rows] + ahead)
        ahead = ahead + totals[k * rows : (k + 1) * rows]
    return jnp.concatenate(parts, axis=1)


def pack_kernel(
    order_hbm, rows_hbm, send_ref, slot_ref, order_ref, rows_ref, chosen_ref, sem, *,
    devices, capacity,
):
    order_copy = fetch(order_hbm, order_ref, sem.at[0])
    rows_copy = fetch(rows_hbm, rows_ref, sem.at[1])
    leaf_rows = rows_ref.shape[0]
    order_copy.wait()
    order = order_ref[...]
    target = order // leaf_rows
    position = order - target * leaf_rows
    hits = (iota((devices, leaf_rows), 0) == target).astype(F32)
    rank = jnp.sum(hits * ranks(hits), axis=0, keepdims=True).astype(jnp.int32)
    slot_ref[...] = row_blocks((target * capacity + rank).astype(F32))
    group = LANES // capacity
    lane = rank + lax.rem(lax.axis_index("row") * lax.axis_size("col") + lax.axis_index("col"), group) * capacity
    high = position // CODE_BASE
    low = position - high * CODE_BASE
    codes = jnp.concatenate([hits * (high + 1).astype(F32), hits * low.astype(F32)], axis=0)
    places = (iota((LANES, leaf_rows), 0) == lane).astype(F32).astype(BF16)
    spread = matmul_nt(codes.astype(BF16), places)
    extra = (devices, EXTRA, LANES)
    send_ref[:, 2 * capacity :, :] = jnp.where(
        iota(extra, 1) < EXTRA // 2,
        jnp.broadcast_to(spread[:devices].reshape(devices, 1, LANES), extra),
        jnp.broadcast_to(spread[devices:].reshape(devices, 1, LANES), extra),
    ).astype(BF16)
    in_slot = (iota((capacity, leaf_rows), 0) == rank).astype(F32).astype(BF16)
    hits = hits.astype(BF16)
    for t in range(devices):
        chosen_ref[t * capacity : (t + 1) * capacity, :] = in_slot * hits[t : t + 1, :]
    rows_copy.wait()
    count = devices // PIECES
    for piece in range(PIECES):
        blocks = pl.ds(piece * count, count)
        sent = matmul(chosen_ref[pl.ds(piece * count * capacity, count * capacity), :], rows_ref[...])
        sent = sent.astype(BF16)
        send_ref[blocks, :capacity, :] = sent[:, :LANES].reshape(count, capacity, LANES)
        send_ref[blocks, capacity : 2 * capacity, :] = sent[:, LANES:].reshape(count, capacity, LANES)


def codes_of(got_ref, devices, capacity):
    group = LANES // capacity
    extra = got_ref[:, 2 * capacity :, :].astype(F32)
    return [sum(extra[k + g] for g in range(group)) for k in range(0, devices, group)]


def load_kernel(after_ref, *refs, picks, turned, stores, rows_of, groups, kept, levels):
    refs = list(refs)

    def take(count):
        taken = refs[:count]
        del refs[:count]
        return taken

    count = len(picks)
    plain = count - turned
    gathers = 1 if rows_of else 0
    sources, stored, given = take(count), take(stores), take(2 * gathers)
    targets, held, gathered = take(count), take(stores), take(gathers)
    scratch, chosen, landed = take(turned), take(gathers), take(rows_of == "lift")
    work, (sem,) = take(gathers and not kept), refs
    landing = targets[:plain] + scratch
    if landed:
        lift_copy = fetch(given[1].at[0], landed[0], sem.at[count + stores])

    bits = tree_bits(levels) if any(isinstance(one, tuple) for pick in picks for one in pick) else []

    def part(pick, rows):
        return tuple(
            pl.ds(pl.multiple_of(bits[one[1]] * rows, rows), rows) if isinstance(one, tuple) else one
            for one in pick
        )

    copies = [
        fetch(source.at[part(pick, target.shape[-2])], target, sem.at[k])
        for k, (source, target, pick) in enumerate(zip(sources, landing, picks))
    ]
    copies += [fetch(stored[k], held[k], sem.at[count + k]) for k in range(stores)]
    if rows_of:
        out_ref = gathered[0] if kept else work[0]
        (chosen_ref,) = chosen
        chosen_ref[...] = wide_one_hot(place_columns(given[0], groups), chosen_ref.shape[1] // LANES)
        if landed:
            lift_copy.wait()
            width = landed[0].shape[2]
            for part in range(2):
                columns = slice(part * width, (part + 1) * width)
                out_ref[:, columns] = matmul(chosen_ref[...], landed[0][part]).astype(BF16)
        else:
            out_ref[...] = folded(matmul(chosen_ref[...], given[1][...]))
        if not kept:
            copies.append(fetch(out_ref, gathered[0], sem.at[count + stores + 1]))
    for k in range(turned):
        copies[plain + k].wait()
        for part in range(2):
            targets[plain + k][part] = jnp.transpose(scratch[k][part])
    for k, copy in enumerate(copies):
        if not plain <= k < count:
            copy.wait()


def place_columns(place_ref, groups):
    turned = jnp.transpose(place_ref[...])
    return [
        (turned[:, k * EXTRA : k * EXTRA + 1] - 1.0) * CODE_BASE
        + turned[:, k * EXTRA + EXTRA // 2 : k * EXTRA + EXTRA // 2 + 1]
        for k in range(*groups)
    ]


def place_kernel(
    got_ref, inverse_hbm, basis_hbm, placed_ref, place_ref, inverse_ref, turned_ref,
    chosen_ref, rows_ref, basis_ref, sem, *, devices, capacity,
):
    basis_copy = fetch(basis_hbm.at[0], basis_ref, sem.at[1])
    inverse_copy = fetch(inverse_hbm.at[0], inverse_ref, sem.at[0])
    leaf_rows = placed_ref.shape[0]
    codes = codes_of(got_ref, devices, capacity)
    place_ref[...] = jnp.concatenate(codes, axis=0)
    code = iota((CODE_BASE, LANES), 0).astype(F32)
    is_low = jnp.concatenate(
        [(code == one[EXTRA // 2 : EXTRA // 2 + 1]).astype(F32) for one in codes], axis=1
    ).astype(BF16)
    is_high = jnp.concatenate([(code == one[:1] - 1.0).astype(F32) for one in codes], axis=1).astype(BF16)
    for h in range(leaf_rows // CODE_BASE):
        chosen_ref[h * CODE_BASE : (h + 1) * CODE_BASE, :] = is_low * is_high[h : h + 1, :]
    slots = devices * capacity
    rows_ref[:, :LANES] = got_ref[:, :capacity, :].reshape(slots, LANES)
    rows_ref[:, LANES:] = got_ref[:, capacity : 2 * capacity, :].reshape(slots, LANES)
    placed_ref[...] = matmul(chosen_ref[...], rows_ref[...]).astype(BF16)
    basis_copy.wait()
    for part in range(2):
        turned_ref[part] = jnp.transpose(basis_ref[part])
    inverse_copy.wait()


def leaf_kernel(placed_ref, inverse_ref, parts_ref):
    placed = placed_ref[...]
    parts_ref[...] = two_parts(matmul(inverse_ref[0], placed) + matmul(inverse_ref[1], rotated(placed)))


def coef_kernel(parts_ref, basis_ref, own_ref, other_ref):
    width = parts_ref.shape[1] // 2
    parts = parts_ref[...]
    turned = jnp.concatenate([rotated(parts[:, :width]), rotated(parts[:, width:])], axis=1)
    coef = folded(matmul(basis_ref[0], parts) + matmul(basis_ref[1], turned))
    first, second = swapped(coef[:, :LANES], coef[:, LANES:])
    odd = tree_bits(1)[0] == 1
    own_ref[...] = jnp.where(odd, second, first)
    other_ref[...] = jnp.where(odd, first, second)


def node_rhs(upper, own, partner):
    is_upper = upper == 1
    return jnp.concatenate(
        [jnp.where(is_upper, partner, own), jnp.where(is_upper, own, partner)], axis=0
    )


def node_kernel(own_ref, partner_ref, inverse_ref, basis_ref, sol_ref, coef_ref, code_ref, *, height):
    partner = partner_ref[...]
    rhs = node_rhs(tree_bits(height)[-1], own_ref[...], partner if partner.dtype == F32 else decoded(partner))
    sol = apply_complex(inverse_ref[0], inverse_ref[1], rhs)
    sol_ref[...] = sol
    coef = apply_complex(basis_ref[0], basis_ref[1], sol)
    coef_ref[...] = coef
    code_ref[...] = encoded(coef)


def descent_kernel(own_ref, partner_ref, inverse_ref, *refs, levels):
    below = levels - 1
    bits = tree_bits(levels)
    lifts, sols, coefs = refs[:below], refs[below : 2 * below], refs[2 * below : 3 * below]
    moved_hbm, mine_ref, other_ref, moved_ref, sem = refs[3 * below :]
    moved_copy = fetch(moved_hbm, moved_ref, sem.at[0])
    rank = own_ref.shape[0]
    rhs = node_rhs(bits[below], own_ref[...], decoded(partner_ref[...]))
    down = apply_complex(inverse_ref[0], inverse_ref[1], rhs)
    for k in range(below - 1, -1, -1):
        gap = coefs[k][...] - down
        if k == below - 1:
            sol = sols[k][pl.ds(pl.multiple_of(bits[k] * rank, rank), rank), :]
        else:
            sol = sols[k][...]
        down = sol - apply_complex(lifts[k][0], lifts[k][1], gap)
    swap = bits[0] == 1
    mine_ref[...] = jnp.where(swap, down[rank:], down[:rank])
    other_ref[...] = jnp.where(swap, down[:rank], down[rank:])
    moved_copy.wait()


def finish_kernel(
    mine_ref, others_ref, own_ref, other_ref, *refs, devices, capacity
):
    *pieces, send_ref = refs
    moved, pieces = pieces[:2], pieces[2:]
    swap = tree_bits(1)[0] == 1
    mine = own_ref[...] - mine_ref[...]
    other = other_ref[...] - others_ref[...]
    first, second = swapped(jnp.where(swap, other, mine), jnp.where(swap, mine, other))
    gap = jnp.concatenate([first, second], axis=1)
    rank, width = gap.shape
    moved = jnp.concatenate([piece[...] for piece in moved], axis=0)
    change = matmul(moved[:, :rank], two_parts(gap)) + matmul(moved[:, rank:], two_parts(rotated(gap)))
    sol = jnp.concatenate([piece[...] for piece in pieces], axis=0) - folded(change)
    code = scale_code(sol)
    level = to_int16(rounded(sol * inverse_unit_of(code)))
    send_ref[:, :capacity, :] = level[:, :LANES].reshape(devices, capacity, LANES)
    send_ref[:, capacity : 2 * capacity, :] = level[:, LANES:].reshape(devices, capacity, LANES)
    extra = (EXTRA, LANES)
    extra = jnp.where(
        iota(extra, 0) < EXTRA // 2,
        jnp.broadcast_to(code[:, :LANES], extra),
        jnp.broadcast_to(code[:, LANES:], extra),
    )
    extra = to_int16(extra)
    send_ref[:, 2 * capacity :, :] = jnp.broadcast_to(
        extra.reshape(1, EXTRA, LANES), (devices, EXTRA, LANES)
    )


def unpack_kernel(got_ref, slot_ref, out_ref, *, devices, capacity):
    slots = devices * capacity
    turned = jnp.transpose(slot_ref[...])
    chosen = wide_one_hot([turned[:, k : k + 1] for k in range(turned.shape[1])], slots // LANES)
    extra = from_int16(got_ref[:, 2 * capacity :, :])
    halves = []
    for half in range(2):
        level = from_int16(got_ref[:, half * capacity : (half + 1) * capacity, :])
        unit = unit_of(extra[:, half * (EXTRA // 2) : half * (EXTRA // 2) + 1, :])
        halves.append((level * unit).reshape(slots, LANES))
    parts = two_parts(jnp.concatenate(halves, axis=1))
    out_ref[...] = folded(whole_matmul(chosen, parts))


def call(kernel, outs, operands, scratch=(), vmem=24):
    specs = {
        "vmem": pl.BlockSpec(memory_space=pltpu.VMEM),
        "hbm": pl.BlockSpec(memory_space=pl.ANY),
        "any": pl.BlockSpec(memory_space=pl.ANY),
    }
    results = pl.pallas_call(
        kernel,
        out_shape=[pltpu.HBM(out.shape, out.dtype) if space == "hbm" else out for out, space in outs],
        in_specs=[specs[space] for _, space in operands],
        out_specs=[specs[space] for _, space in outs],
        scratch_shapes=[
            pltpu.SemaphoreType.DMA((one,)) if isinstance(one, int) else pltpu.VMEM(one.shape, one.dtype)
            for one in scratch
        ],
        compiler_params=pltpu.CompilerParams(vmem_limit_bytes=vmem * 2**20),
    )(
        *[
            pltpu.with_memory_space_constraint(array, pltpu.HBM) if space == "hbm" else array
            for array, space in operands
        ]
    )
    return results


def shape(dims, dtype=F32):
    return jax.ShapeDtypeStruct(dims, dtype)


def from_partner(shard, axis, apart):
    return lax.ppermute(shard, axis, [(i, i ^ 1 << apart) for i in range(lax.axis_size(axis))])


def per_device(
    right_sides, tree_order, leaf_inverse, leaf_basis, leaf_lift, node_inverse, node_basis, node_lift
):
    row_count = lax.axis_size("row")
    col_count = lax.axis_size("col")
    devices = row_count * col_count
    col_levels = col_count.bit_length() - 1
    levels = col_levels + row_count.bit_length() - 1
    leaf_rows, width = right_sides.shape
    rank = leaf_basis.shape[3]
    capacity = 2 * leaf_rows // min(devices, leaf_rows // 8)
    block = (devices, 2 * capacity + EXTRA, LANES)
    sizes = dict(devices=devices, capacity=capacity)
    def exchange(blocks):
        return lax.all_to_all(blocks, ("row", "col"), split_axis=0, concat_axis=0, tiled=True)

    def partner_of(shard, height):
        if height < col_levels:
            return from_partner(shard, "col", height)
        return from_partner(shard, "row", height - col_levels)

    send, slot = call(
        functools.partial(pack_kernel, **sizes),
        [(shape(block, BF16), "vmem"), (shape((leaf_rows // LANES, LANES)), "vmem")],
        [(tree_order.reshape(1, leaf_rows), "hbm"), (right_sides, "hbm")],
        [
            shape((1, leaf_rows), jnp.int32),
            shape(right_sides.shape, BF16),
            shape((devices * capacity, leaf_rows), BF16),
            2,
        ],
    )
    slots = devices * capacity
    total = slots // LANES
    gathers = {
        levels - 3: ("sol", (0, total // 2), False),
        levels - 2: ("sol", (total // 2, total), False),
        levels - 1: ("lift", (0, 3 * total // 8), False),
        levels: ("lift", (3 * total // 8, total), True),
    }

    def load(after, weights, picks, turned=0, stores=(), gather=("", (0, 0), False)):
        shapes = [
            jax.eval_shape(
                lambda w, pick=pick: w[tuple(slice(0, rank) if isinstance(p, tuple) else p for p in pick)], w
            )
            for w, pick in zip(weights, picks)
        ]
        plain = len(weights) - turned
        outs = [shape(one.shape, one.dtype) for one in shapes[:plain]]
        outs += [shape((2, one.shape[2], one.shape[1]), one.dtype) for one in shapes[plain:]]
        rows_of, groups, kept = gather
        rows = (groups[1] - groups[0]) * LANES
        taken = {
            "": [],
            "sol": [shape((rows, width))],
            "lift": [shape((rows, 2 * rank), BF16)],
        }[rows_of]
        given = {"": [], "sol": [(place, "vmem"), (parts, "vmem")], "lift": [(place, "vmem"), (leaf_lift, "hbm")]}
        work = [shape((rows, leaf_rows), BF16)] if rows_of else []
        work += [shape(leaf_lift.shape[1:], BF16)] if rows_of == "lift" else []
        work += [] if kept else taken
        return call(
            functools.partial(
                load_kernel,
                picks=picks,
                turned=turned,
                stores=len(stores),
                rows_of=rows_of,
                groups=groups,
                kept=kept,
                levels=levels,
            ),
            [(out, "vmem") for out in outs]
            + [(shape(one.shape), "hbm") for one in stores]
            + [(one, "vmem" if kept else "hbm") for one in taken],
            [(after, "any")]
            + [(weight, "hbm") for weight in weights]
            + [(one, "any") for one in stores]
            + given[rows_of],
            [shape(one.shape, one.dtype) for one in shapes[plain:]]
            + work
            + [len(weights) + len(stores) + 2 * bool(rows_of)],
            vmem=14 if rows_of else 6,
        )

    place = parts = None
    got = exchange(send)
    half = shape((rank, LANES))
    placed, place, inverse, basis = call(
        functools.partial(place_kernel, **sizes),
        [
            (shape((leaf_rows, width), BF16), "vmem"),
            (shape((slots // LANES * EXTRA, LANES)), "vmem"),
            (shape(leaf_inverse.shape[1:], BF16), "vmem"),
            (shape((2, rank, leaf_rows), BF16), "vmem"),
        ],
        [(got, "vmem"), (leaf_inverse, "hbm"), (leaf_basis, "hbm")],
        [
            shape((leaf_rows, slots), BF16),
            shape((slots, width), BF16),
            shape(leaf_basis.shape[1:], BF16),
            2,
        ],
    )
    (parts,) = call(
        leaf_kernel,
        [(shape((leaf_rows, 2 * width), BF16), "vmem")],
        [(placed, "vmem"), (inverse, "vmem")],
    )
    own, other = call(
        coef_kernel,
        [(half, "vmem"), (half, "vmem")],
        [(parts, "vmem"), (basis, "vmem")],
    )
    leaf_own, leaf_other = own, other
    whole = shape((2 * rank, LANES))
    sols, stored, coefs, gathered = [], [], [], []
    no_gather = ("", (0, 0), False)
    for height in range(1, levels):
        partner = partner_of(other if height == 1 else code, height - 1)
        pick = (0, height - 1)
        inverse, basis, *kept = load(
            own, (node_inverse, node_basis), (pick, pick), 1, sols[-1:], gathers.get(height, no_gather)
        )
        stored += kept[: len(sols[-1:])]
        gathered += kept[len(sols[-1:]) :]
        sol, own, code = call(
            functools.partial(node_kernel, height=height),
            [(whole, "vmem"), (half, "vmem"), (shape((rank + TAIL, LANES), jnp.int16), "vmem")],
            [
                (own, "vmem"),
                (partner, "vmem"),
                (inverse, "vmem"),
                (basis, "vmem"),
            ],
            vmem=8,
        )
        sols.append(sol)
        coefs.append(own)
    partner = partner_of(code, levels - 1)
    loaded = load(
        own,
        (node_inverse, *(node_lift for _ in coefs), *stored),
        (
            (0, levels - 1, slice(None), ("half", levels - 1)),
            (0, 0),
            *((0, k, slice(None), ("half", k)) for k in range(1, levels - 1)),
            (),
            *((("half", k),) for k in range(1, levels - 2)),
        ),
        gather=gathers[levels],
    )
    inverse, lifts, sols = loaded[0], loaded[1:levels], [*loaded[levels:-1], sols[-1]]
    gathered.append(loaded[-1])
    mine, other, moved = call(
        functools.partial(descent_kernel, levels=levels),
        [
            (half, "vmem"),
            (half, "vmem"),
            (shape(gathered[2].shape, BF16), "vmem"),
        ],
        [(own, "vmem"), (partner, "vmem"), (inverse, "vmem")]
        + [(lift, "vmem") for lift in lifts]
        + [(sol, "vmem") for sol in sols]
        + [(coef, "vmem") for coef in coefs]
        + [(one, "hbm") for one in gathered[2:-1]],
        [1],
        vmem=8,
    )
    other_sent = other
    other = partner_of(other_sent, 0)
    bases = load(other_sent, gathered[:2], ((),) * 2)
    (back,) = call(
        functools.partial(finish_kernel, **sizes),
        [(shape(block, jnp.int16), "vmem")],
        [
            (mine, "vmem"),
            (other, "vmem"),
            (leaf_own, "vmem"),
            (leaf_other, "vmem"),
            (moved, "vmem"),
            (gathered[-1], "vmem"),
        ]
        + [(one, "vmem") for one in bases],
    )
    returned = exchange(back)
    (result,) = call(
        functools.partial(unpack_kernel, **sizes),
        [(shape((leaf_rows, width)), "vmem")],
        [(returned, "vmem"), (slot, "vmem")],
    )
    return result


def solution(mesh):
    in_specs = (
        P(("row", "col"), None),
        P(("row", "col")),
        P(("row", "col"), None, None, None),
        P(("row", "col"), None, None, None),
        P(("row", "col"), None, None, None),
        P(("row", "col"), None, None, None, None),
        P(("row", "col"), None, None, None, None),
        P(("row", "col"), None, None, None, None),
    )
    out_specs = P(("row", "col"), None)
    return jax.shard_map(
        per_device, mesh=mesh, in_specs=in_specs, out_specs=out_specs, check_vma=False
    )
```

```python
import functools

import jax
import jax.numpy as jnp
from jax import lax
from jax.experimental import pallas as pl
from jax.experimental.pallas import tpu as pltpu
from jax.sharding import PartitionSpec as P

LANES = 128
EXTRA = 8
CODE_BASE = 32
SCALE_STEPS = 64
HEADROOM = 1.002
ROUNDER = 1.5 * 2.0**23
TAIL = 16
STEP = 256
PIECES = 4
NODE_STEP = 128
FINISH_PIECES = 8
BF16 = jnp.bfloat16
F32 = jnp.float32


def whole_matmul(a, b):
    return lax.dot_general(a, b, (((1,), (0,)), ((), ())), preferred_element_type=F32)


def matmul(a, b, step=STEP):
    pieces = [whole_matmul(a[at : at + step], b) for at in range(0, a.shape[0], step)]
    return pieces[0] if len(pieces) == 1 else jnp.concatenate(pieces, axis=0)


def matmul_nt(a, b):
    return lax.dot_general(a, b, (((1,), (1,)), ((), ())), preferred_element_type=F32)


def tree_bits(levels):
    index = lax.axis_index("row") * lax.axis_size("col") + lax.axis_index("col")
    return [index >> height & 1 for height in range(levels)]


def iota(shape, dim):
    return lax.broadcasted_iota(jnp.int32, shape, dim)


def rotated(x):
    if x.shape[1] == LANES:
        turned = pltpu.roll(x, LANES // 2, 1)
        return jnp.where(iota(x.shape, 1) < LANES // 2, -turned, turned)
    return jnp.concatenate([-x[:, LANES:], x[:, :LANES]], axis=1)


def swapped(first, second):
    low = iota(first.shape, 1) < LANES // 2
    return (
        jnp.where(low, first, pltpu.roll(second, LANES // 2, 1)),
        jnp.where(low, pltpu.roll(first, LANES // 2, 1), second),
    )


def two_parts(x):
    high = x.astype(BF16)
    low = (x - high.astype(F32)).astype(BF16)
    return jnp.concatenate([high, low], axis=1)


def folded(both):
    width = both.shape[1] // 2
    return both[:, :width] + both[:, width:]


def apply_complex(real, imag, x, step=STEP):
    both = jnp.concatenate([two_parts(x), two_parts(rotated(x))], axis=0)
    return folded(matmul(jnp.concatenate([real, imag], axis=1), both, step))


def unit_of(code):
    return jnp.exp2(code * (1.0 / SCALE_STEPS) - 15.0) * HEADROOM


def inverse_unit_of(code):
    return jnp.exp2(15.0 - code * (1.0 / SCALE_STEPS)) * (1.0 / HEADROOM)


def rounded(x):
    return (x + ROUNDER) - ROUNDER


def to_int16(x):
    return x.astype(jnp.int32).astype(jnp.int16)


def from_int16(x):
    return x.astype(jnp.int32).astype(F32)


def encoded(x):
    code = scale_code(x)
    level = rounded(x * inverse_unit_of(code))
    return to_int16(jnp.concatenate([level, jnp.broadcast_to(code, (TAIL, LANES))], axis=0))


def decoded(levels):
    values = from_int16(levels)
    return values[:-TAIL] * unit_of(values[-TAIL : 1 - TAIL])


def scale_code(x):
    largest = jnp.max(jnp.abs(x), axis=0, keepdims=True)
    return jnp.ceil(jnp.log2(jnp.maximum(largest, 2.0**-110)) * SCALE_STEPS)


def fetch(source, target, sem):
    copy = pltpu.make_async_copy(source, target, sem)
    copy.start()
    return copy


def wide_one_hot(columns, blocks):
    lane = iota((LANES, LANES), 1).astype(F32)
    one, zero = jnp.ones((), BF16), jnp.zeros((), BF16)
    names = []
    for entry in columns:
        block = jnp.floor(entry * (1.0 / LANES))
        names.append(jnp.where(lane == entry - block * LANES, block, -1.0))
    names = jnp.concatenate(names, axis=0).astype(BF16)
    return jnp.concatenate([jnp.where(names == jnp.array(g, BF16), one, zero) for g in range(blocks)], axis=1)


def row_blocks(x):
    return jnp.concatenate([x[:, at : at + LANES] for at in range(0, x.shape[1], LANES)], axis=0)


def ranks(hits):
    rows, width = hits.shape
    upper = (iota((LANES, LANES), 0) < iota((LANES, LANES), 1)).astype(F32).astype(BF16)
    pieces = jnp.concatenate(
        [hits[:, at : at + LANES] for at in range(0, width, LANES)], axis=0
    ).astype(BF16)
    inside = matmul(pieces, upper)
    totals = matmul(pieces, jnp.ones((LANES, LANES), BF16))
    ahead = jnp.zeros((rows, LANES), F32)
    parts = []
    for k in range(width // LANES):
        parts.append(inside[k * rows : (k + 1) * rows] + ahead)
        ahead = ahead + totals[k * rows : (k + 1) * rows]
    return jnp.concatenate(parts, axis=1)


def pack_kernel(
    order_hbm, rows_hbm, inverse_hbm, basis_hbm, send_ref, slot_ref, real_ref, basis_ref,
    order_ref, rows_ref, chosen_ref, sem, *,
    devices, capacity,
):
    order_copy = fetch(order_hbm, order_ref, sem.at[0])
    rows_copy = fetch(rows_hbm, rows_ref, sem.at[1])
    basis_copy = fetch(basis_hbm.at[0], basis_ref, sem.at[2])
    real_copy = fetch(inverse_hbm.at[0, 0], real_ref, sem.at[3])
    leaf_rows = rows_ref.shape[0]
    order_copy.wait()
    order = order_ref[...]
    target = order // leaf_rows
    position = order - target * leaf_rows
    hits = (iota((devices, leaf_rows), 0) == target).astype(F32)
    rank = jnp.sum(hits * ranks(hits), axis=0, keepdims=True).astype(jnp.int32)
    slot_ref[...] = row_blocks((target * capacity + rank).astype(F32))
    group = LANES // capacity
    lane = rank + lax.rem(lax.axis_index("row") * lax.axis_size("col") + lax.axis_index("col"), group) * capacity
    high = position // CODE_BASE
    low = position - high * CODE_BASE
    codes = jnp.concatenate([hits * (high + 1).astype(F32), hits * low.astype(F32)], axis=0)
    places = (iota((LANES, leaf_rows), 0) == lane).astype(F32).astype(BF16)
    spread = matmul_nt(codes.astype(BF16), places)
    extra = (devices, EXTRA, LANES)
    send_ref[:, 2 * capacity :, :] = jnp.where(
        iota(extra, 1) < EXTRA // 2,
        jnp.broadcast_to(spread[:devices].reshape(devices, 1, LANES), extra),
        jnp.broadcast_to(spread[devices:].reshape(devices, 1, LANES), extra),
    ).astype(BF16)
    in_slot = (iota((capacity, leaf_rows), 0) == rank).astype(F32).astype(BF16)
    hits = hits.astype(BF16)
    for t in range(devices):
        chosen_ref[t * capacity : (t + 1) * capacity, :] = in_slot * hits[t : t + 1, :]
    rows_copy.wait()
    count = devices // PIECES
    for piece in range(PIECES):
        blocks = pl.ds(piece * count, count)
        sent = matmul(chosen_ref[pl.ds(piece * count * capacity, count * capacity), :], rows_ref[...])
        sent = sent.astype(BF16)
        send_ref[blocks, :capacity, :] = sent[:, :LANES].reshape(count, capacity, LANES)
        send_ref[blocks, capacity : 2 * capacity, :] = sent[:, LANES:].reshape(count, capacity, LANES)
    basis_copy.wait()
    real_copy.wait()


def codes_of(got_ref, devices, capacity):
    group = LANES // capacity
    extra = got_ref[:, 2 * capacity :, :].astype(F32)
    return [sum(extra[k + g] for g in range(group)) for k in range(0, devices, group)]


def load_kernel(after_ref, *refs, picks, turned, stores, rows_of, groups, kept, levels):
    refs = list(refs)

    def take(count):
        taken = refs[:count]
        del refs[:count]
        return taken

    count = len(picks)
    plain = count - turned
    gathers = 1 if rows_of else 0
    sources, stored, given = take(count), take(stores), take(2 * gathers)
    targets, held, gathered = take(count), take(stores), take(gathers)
    scratch, chosen, landed = take(turned), take(gathers), take(rows_of == "lift")
    work, (sem,) = take(gathers and not kept), refs
    landing = targets[:plain] + scratch
    if landed:
        lift_copy = fetch(given[1].at[0], landed[0], sem.at[count + stores])

    bits = tree_bits(levels) if any(isinstance(one, tuple) for pick in picks for one in pick) else []

    def part(pick, rows):
        return tuple(
            pl.ds(pl.multiple_of(bits[one[1]] * rows, rows), rows) if isinstance(one, tuple) else one
            for one in pick
        )

    copies = [
        fetch(source.at[part(pick, target.shape[-2])], target, sem.at[k])
        for k, (source, target, pick) in enumerate(zip(sources, landing, picks))
    ]
    copies += [fetch(stored[k], held[k], sem.at[count + k]) for k in range(stores)]
    if rows_of:
        out_ref = gathered[0] if kept else work[0]
        (chosen_ref,) = chosen
        chosen_ref[...] = wide_one_hot(place_columns(given[0], groups), chosen_ref.shape[1] // LANES)
        if landed:
            lift_copy.wait()
            width = landed[0].shape[2]
            for part in range(2):
                columns = slice(part * width, (part + 1) * width)
                out_ref[:, columns] = matmul(chosen_ref[...], landed[0][part]).astype(BF16)
        else:
            out_ref[...] = folded(matmul(chosen_ref[...], given[1][...]))
        if not kept:
            copies.append(fetch(out_ref, gathered[0], sem.at[count + stores + 1]))
    for k in range(turned):
        copies[plain + k].wait()
        for part in range(2):
            targets[plain + k][part] = jnp.transpose(scratch[k][part])
    for k, copy in enumerate(copies):
        if not plain <= k < count:
            copy.wait()


def place_columns(place_ref, groups):
    turned = jnp.transpose(place_ref[...])
    return [
        (turned[:, k * EXTRA : k * EXTRA + 1] - 1.0) * CODE_BASE
        + turned[:, k * EXTRA + EXTRA // 2 : k * EXTRA + EXTRA // 2 + 1]
        for k in range(*groups)
    ]


def place_kernel(
    got_ref, inverse_hbm, basis_ref, placed_ref, place_ref, imag_ref, turned_ref, chosen_ref, rows_ref, sem, *,
    devices, capacity,
):
    imag_copy = fetch(inverse_hbm.at[0, 1], imag_ref, sem.at[0])
    leaf_rows = placed_ref.shape[0]
    codes = codes_of(got_ref, devices, capacity)
    place_ref[...] = jnp.concatenate(codes, axis=0)
    code = iota((CODE_BASE, LANES), 0).astype(F32)
    is_low = jnp.concatenate(
        [(code == one[EXTRA // 2 : EXTRA // 2 + 1]).astype(F32) for one in codes], axis=1
    ).astype(BF16)
    is_high = jnp.concatenate([(code == one[:1] - 1.0).astype(F32) for one in codes], axis=1).astype(BF16)
    for h in range(leaf_rows // CODE_BASE):
        chosen_ref[h * CODE_BASE : (h + 1) * CODE_BASE, :] = is_low * is_high[h : h + 1, :]
    slots = devices * capacity
    rows_ref[:, :LANES] = got_ref[:, :capacity, :].reshape(slots, LANES)
    rows_ref[:, LANES:] = got_ref[:, capacity : 2 * capacity, :].reshape(slots, LANES)
    placed_ref[...] = matmul(chosen_ref[...], rows_ref[...]).astype(BF16)
    for part in range(2):
        turned_ref[part] = jnp.transpose(basis_ref[part])
    imag_copy.wait()


def leaf_kernel(placed_ref, real_ref, imag_ref, parts_ref):
    placed = placed_ref[...]
    parts_ref[...] = two_parts(matmul(real_ref[...], placed) + matmul(imag_ref[...], rotated(placed)))


def coef_kernel(parts_ref, basis_ref, own_ref, other_ref):
    width = parts_ref.shape[1] // 2
    parts = parts_ref[...]
    turned = jnp.concatenate([rotated(parts[:, :width]), rotated(parts[:, width:])], axis=1)
    coef = folded(matmul(basis_ref[0], parts) + matmul(basis_ref[1], turned))
    first, second = swapped(coef[:, :LANES], coef[:, LANES:])
    odd = tree_bits(1)[0] == 1
    own_ref[...] = jnp.where(odd, second, first)
    other_ref[...] = jnp.where(odd, first, second)


def node_rhs(upper, own, partner):
    is_upper = upper == 1
    return jnp.concatenate(
        [jnp.where(is_upper, partner, own), jnp.where(is_upper, own, partner)], axis=0
    )


def node_kernel(own_ref, partner_ref, inverse_ref, basis_ref, sol_ref, coef_ref, code_ref, *, height):
    partner = partner_ref[...]
    rhs = node_rhs(tree_bits(height)[-1], own_ref[...], partner if partner.dtype == F32 else decoded(partner))
    sol = apply_complex(inverse_ref[0], inverse_ref[1], rhs, NODE_STEP)
    sol_ref[...] = sol
    coef = apply_complex(basis_ref[0], basis_ref[1], sol, NODE_STEP)
    coef_ref[...] = coef
    code_ref[...] = encoded(coef)


def descent_kernel(own_ref, partner_ref, inverse_ref, *refs, levels):
    below = levels - 1
    bits = tree_bits(levels)
    lifts, sols, coefs = refs[:below], refs[below : 2 * below], refs[2 * below : 3 * below]
    moved_hbm, mine_ref, other_ref, moved_ref, sem = refs[3 * below :]
    moved_copy = fetch(moved_hbm, moved_ref, sem.at[0])
    rank = own_ref.shape[0]
    rhs = node_rhs(bits[below], own_ref[...], decoded(partner_ref[...]))
    down = apply_complex(inverse_ref[0], inverse_ref[1], rhs)
    for k in range(below - 1, -1, -1):
        gap = coefs[k][...] - down
        if k == below - 1:
            sol = sols[k][pl.ds(pl.multiple_of(bits[k] * rank, rank), rank), :]
        else:
            sol = sols[k][...]
        down = sol - apply_complex(lifts[k][0], lifts[k][1], gap)
    swap = bits[0] == 1
    mine_ref[...] = jnp.where(swap, down[rank:], down[:rank])
    other_ref[...] = jnp.where(swap, down[:rank], down[rank:])
    moved_copy.wait()


def rows_of(refs, rows):
    parts, at = [], 0
    for ref in refs:
        first, last = max(rows.start - at, 0), min(rows.stop - at, ref.shape[0])
        if first < last:
            parts.append(ref[first:last, :])
        at += ref.shape[0]
    return parts[0] if len(parts) == 1 else jnp.concatenate(parts, axis=0)


def finish_kernel(
    mine_ref, others_ref, own_ref, other_ref, *refs, devices, capacity
):
    *pieces, send_ref = refs
    moved, pieces = pieces[:2], pieces[2:]
    swap = tree_bits(1)[0] == 1
    mine = own_ref[...] - mine_ref[...]
    other = other_ref[...] - others_ref[...]
    first, second = swapped(jnp.where(swap, other, mine), jnp.where(swap, mine, other))
    gap = jnp.concatenate([first, second], axis=1)
    rank, width = gap.shape
    parts = jnp.concatenate([two_parts(gap), two_parts(rotated(gap))], axis=0)
    count = devices // FINISH_PIECES
    for at in range(0, devices, count):
        rows = slice(at * capacity, (at + count) * capacity)
        sol = rows_of(pieces, rows) - folded(matmul(rows_of(moved, rows), parts))
        code = scale_code(sol)
        level = to_int16(rounded(sol * inverse_unit_of(code)))
        blocks = slice(at, at + count)
        send_ref[blocks, :capacity, :] = level[:, :LANES].reshape(count, capacity, LANES)
        send_ref[blocks, capacity : 2 * capacity, :] = level[:, LANES:].reshape(count, capacity, LANES)
        extra = (EXTRA, LANES)
        extra = jnp.where(
            iota(extra, 0) < EXTRA // 2,
            jnp.broadcast_to(code[:, :LANES], extra),
            jnp.broadcast_to(code[:, LANES:], extra),
        )
        send_ref[blocks, 2 * capacity :, :] = jnp.broadcast_to(
            to_int16(extra).reshape(1, EXTRA, LANES), (count, EXTRA, LANES)
        )


def unpack_kernel(got_ref, slot_ref, out_hbm, out_ref, sem, *, devices, capacity):
    slots = devices * capacity
    turned = jnp.transpose(slot_ref[...])
    chosen = wide_one_hot([turned[:, k : k + 1] for k in range(turned.shape[1])], slots // LANES)
    extra = from_int16(got_ref[:, 2 * capacity :, :])
    halves = []
    for half in range(2):
        level = from_int16(got_ref[:, half * capacity : (half + 1) * capacity, :])
        unit = unit_of(extra[:, half * (EXTRA // 2) : half * (EXTRA // 2) + 1, :])
        halves.append((level * unit).reshape(slots, LANES))
    parts = two_parts(jnp.concatenate(halves, axis=1))
    count = out_ref.shape[0] // PIECES
    copies = []
    for piece in range(PIECES):
        rows = pl.ds(piece * count, count)
        out_ref[rows, :] = folded(whole_matmul(chosen[piece * count : (piece + 1) * count], parts))
        copies.append(fetch(out_ref.at[rows], out_hbm.at[rows], sem.at[piece]))
    for copy in copies:
        copy.wait()


def call(kernel, outs, operands, scratch=(), vmem=24):
    specs = {
        "vmem": pl.BlockSpec(memory_space=pltpu.VMEM),
        "hbm": pl.BlockSpec(memory_space=pl.ANY),
        "any": pl.BlockSpec(memory_space=pl.ANY),
    }
    results = pl.pallas_call(
        kernel,
        out_shape=[pltpu.HBM(out.shape, out.dtype) if space == "hbm" else out for out, space in outs],
        in_specs=[specs[space] for _, space in operands],
        out_specs=[specs[space] for _, space in outs],
        scratch_shapes=[
            pltpu.SemaphoreType.DMA((one,)) if isinstance(one, int) else pltpu.VMEM(one.shape, one.dtype)
            for one in scratch
        ],
        compiler_params=pltpu.CompilerParams(vmem_limit_bytes=vmem * 2**20),
    )(
        *[
            pltpu.with_memory_space_constraint(array, pltpu.HBM) if space == "hbm" else array
            for array, space in operands
        ]
    )
    return results


def shape(dims, dtype=F32):
    return jax.ShapeDtypeStruct(dims, dtype)


def from_partner(shard, axis, apart):
    return lax.ppermute(shard, axis, [(i, i ^ 1 << apart) for i in range(lax.axis_size(axis))])


def per_device(
    right_sides, tree_order, leaf_inverse, leaf_basis, leaf_lift, node_inverse, node_basis, node_lift
):
    row_count = lax.axis_size("row")
    col_count = lax.axis_size("col")
    devices = row_count * col_count
    col_levels = col_count.bit_length() - 1
    levels = col_levels + row_count.bit_length() - 1
    leaf_rows, width = right_sides.shape
    rank = leaf_basis.shape[3]
    capacity = 2 * leaf_rows // min(devices, leaf_rows // 8)
    block = (devices, 2 * capacity + EXTRA, LANES)
    sizes = dict(devices=devices, capacity=capacity)
    def exchange(blocks):
        return lax.all_to_all(blocks, ("row", "col"), split_axis=0, concat_axis=0, tiled=True)

    def partner_of(shard, height):
        if height < col_levels:
            return from_partner(shard, "col", height)
        return from_partner(shard, "row", height - col_levels)

    send, slot, real, basis = call(
        functools.partial(pack_kernel, **sizes),
        [
            (shape(block, BF16), "vmem"),
            (shape((leaf_rows // LANES, LANES)), "vmem"),
            (shape(leaf_inverse.shape[2:], BF16), "vmem"),
            (shape(leaf_basis.shape[1:], BF16), "vmem"),
        ],
        [(tree_order.reshape(1, leaf_rows), "hbm"), (right_sides, "hbm")]
        + [(leaf_inverse, "hbm"), (leaf_basis, "hbm")],
        [
            shape((1, leaf_rows), jnp.int32),
            shape(right_sides.shape, BF16),
            shape((devices * capacity, leaf_rows), BF16),
            4,
        ],
    )
    slots = devices * capacity
    total = slots // LANES
    gathers = {
        levels - 3: ("sol", (0, total // 2), False),
        levels - 2: ("sol", (total // 2, total), False),
        levels - 1: ("lift", (0, 3 * total // 8), False),
        levels: ("lift", (3 * total // 8, total), True),
    }

    def load(after, weights, picks, turned=0, stores=(), gather=("", (0, 0), False)):
        shapes = [
            jax.eval_shape(
                lambda w, pick=pick: w[tuple(slice(0, rank) if isinstance(p, tuple) else p for p in pick)], w
            )
            for w, pick in zip(weights, picks)
        ]
        plain = len(weights) - turned
        outs = [shape(one.shape, one.dtype) for one in shapes[:plain]]
        outs += [shape((2, one.shape[2], one.shape[1]), one.dtype) for one in shapes[plain:]]
        rows_of, groups, kept = gather
        rows = (groups[1] - groups[0]) * LANES
        taken = {
            "": [],
            "sol": [shape((rows, width))],
            "lift": [shape((rows, 2 * rank), BF16)],
        }[rows_of]
        given = {"": [], "sol": [(place, "vmem"), (parts, "vmem")], "lift": [(place, "vmem"), (leaf_lift, "hbm")]}
        work = [shape((rows, leaf_rows), BF16)] if rows_of else []
        work += [shape(leaf_lift.shape[1:], BF16)] if rows_of == "lift" else []
        work += [] if kept else taken
        return call(
            functools.partial(
                load_kernel,
                picks=picks,
                turned=turned,
                stores=len(stores),
                rows_of=rows_of,
                groups=groups,
                kept=kept,
                levels=levels,
            ),
            [(out, "vmem") for out in outs]
            + [(shape(one.shape), "hbm") for one in stores]
            + [(one, "vmem" if kept else "hbm") for one in taken],
            [(after, "any")]
            + [(weight, "hbm") for weight in weights]
            + [(one, "any") for one in stores]
            + given[rows_of],
            [shape(one.shape, one.dtype) for one in shapes[plain:]]
            + work
            + [len(weights) + len(stores) + 2 * bool(rows_of)],
            vmem=14 if rows_of else 6,
        )

    place = parts = None
    got = exchange(send)
    half = shape((rank, LANES))
    placed, place, imag, basis = call(
        functools.partial(place_kernel, **sizes),
        [
            (shape((leaf_rows, width), BF16), "vmem"),
            (shape((slots // LANES * EXTRA, LANES)), "vmem"),
            (shape(leaf_inverse.shape[2:], BF16), "vmem"),
            (shape((2, rank, leaf_rows), BF16), "vmem"),
        ],
        [(got, "vmem"), (leaf_inverse, "hbm"), (basis, "vmem")],
        [shape((leaf_rows, slots), BF16), shape((slots, width), BF16), 1],
    )
    (parts,) = call(
        leaf_kernel,
        [(shape((leaf_rows, 2 * width), BF16), "vmem")],
        [(placed, "vmem"), (real, "vmem"), (imag, "vmem")],
    )
    own, other = call(
        coef_kernel,
        [(half, "vmem"), (half, "vmem")],
        [(parts, "vmem"), (basis, "vmem")],
    )
    leaf_own, leaf_other = own, other
    whole = shape((2 * rank, LANES))
    sols, stored, coefs, gathered = [], [], [], []
    no_gather = ("", (0, 0), False)
    for height in range(1, levels):
        partner = partner_of(other if height == 1 else code, height - 1)
        pick = (0, height - 1)
        inverse, basis, *kept = load(
            own, (node_inverse, node_basis), (pick, pick), 1, sols[-1:], gathers.get(height, no_gather)
        )
        stored += kept[: len(sols[-1:])]
        gathered += kept[len(sols[-1:]) :]
        sol, own, code = call(
            functools.partial(node_kernel, height=height),
            [(whole, "vmem"), (half, "vmem"), (shape((rank + TAIL, LANES), jnp.int16), "vmem")],
            [
                (own, "vmem"),
                (partner, "vmem"),
                (inverse, "vmem"),
                (basis, "vmem"),
            ],
            vmem=8,
        )
        sols.append(sol)
        coefs.append(own)
    partner = partner_of(code, levels - 1)
    loaded = load(
        own,
        (node_inverse, *(node_lift for _ in coefs), *stored),
        (
            (0, levels - 1, slice(None), ("half", levels - 1)),
            (0, 0),
            *((0, k, slice(None), ("half", k)) for k in range(1, levels - 1)),
            (),
            *((("half", k),) for k in range(1, levels - 2)),
        ),
        gather=gathers[levels],
    )
    inverse, lifts, sols = loaded[0], loaded[1:levels], [*loaded[levels:-1], sols[-1]]
    gathered.append(loaded[-1])
    mine, other, moved = call(
        functools.partial(descent_kernel, levels=levels),
        [
            (half, "vmem"),
            (half, "vmem"),
            (shape(gathered[2].shape, BF16), "vmem"),
        ],
        [(own, "vmem"), (partner, "vmem"), (inverse, "vmem")]
        + [(lift, "vmem") for lift in lifts]
        + [(sol, "vmem") for sol in sols]
        + [(coef, "vmem") for coef in coefs]
        + [(one, "hbm") for one in gathered[2:-1]],
        [1],
        vmem=8,
    )
    other_sent = other
    other = partner_of(other_sent, 0)
    bases = load(other_sent, gathered[:2], ((),) * 2)
    (back,) = call(
        functools.partial(finish_kernel, **sizes),
        [(shape(block, jnp.int16), "vmem")],
        [
            (mine, "vmem"),
            (other, "vmem"),
            (leaf_own, "vmem"),
            (leaf_other, "vmem"),
            (moved, "vmem"),
            (gathered[-1], "vmem"),
        ]
        + [(one, "vmem") for one in bases],
    )
    returned = exchange(back)
    (result,) = call(
        functools.partial(unpack_kernel, **sizes),
        [(shape((leaf_rows, width)), "hbm")],
        [(returned, "vmem"), (slot, "vmem")],
        [shape((leaf_rows, width)), PIECES],
    )
    return result


def solution(mesh):
    in_specs = (
        P(("row", "col"), None),
        P(("row", "col")),
        P(("row", "col"), None, None, None),
        P(("row", "col"), None, None, None),
        P(("row", "col"), None, None, None),
        P(("row", "col"), None, None, None, None),
        P(("row", "col"), None, None, None, None),
        P(("row", "col"), None, None, None, None),
    )
    out_specs = P(("row", "col"), None)
    return jax.shard_map(
        per_device, mesh=mesh, in_specs=in_specs, out_specs=out_specs, check_vma=False
    )
```

```python
import functools

import jax
import jax.numpy as jnp
from jax import lax
from jax.experimental import pallas as pl
from jax.experimental.pallas import tpu as pltpu
from jax.sharding import PartitionSpec as P

LANES = 128
EXTRA = 8
CODE_BASE = 32
SCALE_STEPS = 64
HEADROOM = 1.002
ROUNDER = 1.5 * 2.0**23
TAIL = 16
STEP = 256
PIECES = 4
NODE_STEP = 128
FINISH_PIECES = 8
BF16 = jnp.bfloat16
F32 = jnp.float32
F8 = jnp.float8_e4m3fn


def whole_matmul(a, b):
    return lax.dot_general(a, b, (((1,), (0,)), ((), ())), preferred_element_type=F32)


def matmul(a, b, step=STEP):
    pieces = [whole_matmul(a[at : at + step], b) for at in range(0, a.shape[0], step)]
    return pieces[0] if len(pieces) == 1 else jnp.concatenate(pieces, axis=0)


def matmul_nt(a, b):
    return lax.dot_general(a, b, (((1,), (1,)), ((), ())), preferred_element_type=F32)


def tree_bits(levels):
    index = lax.axis_index("row") * lax.axis_size("col") + lax.axis_index("col")
    return [index >> height & 1 for height in range(levels)]


def iota(shape, dim):
    return lax.broadcasted_iota(jnp.int32, shape, dim)


def rotated(x):
    if x.shape[1] == LANES:
        turned = pltpu.roll(x, LANES // 2, 1)
        return jnp.where(iota(x.shape, 1) < LANES // 2, -turned, turned)
    return jnp.concatenate([-x[:, LANES:], x[:, :LANES]], axis=1)


def swapped(first, second):
    low = iota(first.shape, 1) < LANES // 2
    return (
        jnp.where(low, first, pltpu.roll(second, LANES // 2, 1)),
        jnp.where(low, pltpu.roll(first, LANES // 2, 1), second),
    )


def two_parts(x):
    high = x.astype(BF16)
    low = (x - high.astype(F32)).astype(BF16)
    return jnp.concatenate([high, low], axis=1)


def folded(both):
    width = both.shape[1] // 2
    return both[:, :width] + both[:, width:]


def apply_complex(real, imag, x, step=STEP):
    both = jnp.concatenate([two_parts(x), two_parts(rotated(x))], axis=0)
    return folded(matmul(jnp.concatenate([real, imag], axis=1), both, step))


def unit_of(code):
    return jnp.exp2(code * (1.0 / SCALE_STEPS) - 15.0) * HEADROOM


def inverse_unit_of(code):
    return jnp.exp2(15.0 - code * (1.0 / SCALE_STEPS)) * (1.0 / HEADROOM)


def rounded(x):
    return (x + ROUNDER) - ROUNDER


def to_int16(x):
    return x.astype(jnp.int32).astype(jnp.int16)


def from_int16(x):
    return x.astype(jnp.int32).astype(F32)


def encoded(x):
    code = scale_code(x)
    level = rounded(x * inverse_unit_of(code))
    return to_int16(jnp.concatenate([level, jnp.broadcast_to(code, (TAIL, LANES))], axis=0))


def decoded(levels):
    values = from_int16(levels)
    return values[:-TAIL] * unit_of(values[-TAIL : 1 - TAIL])


def scale_code(x):
    largest = jnp.max(jnp.abs(x), axis=0, keepdims=True)
    return jnp.ceil(jnp.log2(jnp.maximum(largest, 2.0**-110)) * SCALE_STEPS)


def fetch(source, target, sem):
    copy = pltpu.make_async_copy(source, target, sem)
    copy.start()
    return copy


def wide_one_hot(columns, blocks):
    lane = iota((LANES, LANES), 1).astype(F32)
    one, zero = jnp.ones((), BF16), jnp.zeros((), BF16)
    names = []
    for entry in columns:
        block = jnp.floor(entry * (1.0 / LANES))
        names.append(jnp.where(lane == entry - block * LANES, block, -1.0))
    names = jnp.concatenate(names, axis=0).astype(BF16)
    return jnp.concatenate([jnp.where(names == jnp.array(g, BF16), one, zero) for g in range(blocks)], axis=1)


def row_blocks(x):
    return jnp.concatenate([x[:, at : at + LANES] for at in range(0, x.shape[1], LANES)], axis=0)


def ranks(hits):
    rows, width = hits.shape
    upper = (iota((LANES, LANES), 0) < iota((LANES, LANES), 1)).astype(F32).astype(BF16)
    pieces = jnp.concatenate(
        [hits[:, at : at + LANES] for at in range(0, width, LANES)], axis=0
    ).astype(BF16)
    inside = matmul(pieces, upper)
    totals = matmul(pieces, jnp.ones((LANES, LANES), BF16))
    ahead = jnp.zeros((rows, LANES), F32)
    parts = []
    for k in range(width // LANES):
        parts.append(inside[k * rows : (k + 1) * rows] + ahead)
        ahead = ahead + totals[k * rows : (k + 1) * rows]
    return jnp.concatenate(parts, axis=1)


def pack_kernel(
    order_hbm, rows_hbm, inverse_hbm, basis_hbm, send_ref, slot_ref, real_ref, basis_ref,
    order_ref, rows_ref, chosen_ref, sem, *,
    devices, capacity,
):
    order_copy = fetch(order_hbm, order_ref, sem.at[0])
    rows_copy = fetch(rows_hbm, rows_ref, sem.at[1])
    basis_copy = fetch(basis_hbm.at[0], basis_ref, sem.at[2])
    real_copy = fetch(inverse_hbm.at[0, 0], real_ref, sem.at[3])
    leaf_rows = rows_ref.shape[0]
    order_copy.wait()
    order = order_ref[...]
    target = order // leaf_rows
    position = order - target * leaf_rows
    hits = (iota((devices, leaf_rows), 0) == target).astype(F32)
    rank = jnp.sum(hits * ranks(hits), axis=0, keepdims=True).astype(jnp.int32)
    slot_ref[...] = row_blocks((target * capacity + rank).astype(F32))
    group = LANES // capacity
    lane = rank + lax.rem(lax.axis_index("row") * lax.axis_size("col") + lax.axis_index("col"), group) * capacity
    high = position // CODE_BASE
    low = position - high * CODE_BASE
    codes = jnp.concatenate([hits * (high + 1).astype(F32), hits * low.astype(F32)], axis=0)
    places = (iota((LANES, leaf_rows), 0) == lane).astype(F32).astype(BF16)
    spread = matmul_nt(codes.astype(BF16), places)
    extra = (devices, EXTRA, LANES)
    send_ref[:, 2 * capacity :, :] = jnp.where(
        iota(extra, 1) < EXTRA // 2,
        jnp.broadcast_to(spread[:devices].reshape(devices, 1, LANES), extra),
        jnp.broadcast_to(spread[devices:].reshape(devices, 1, LANES), extra),
    ).astype(BF16)
    in_slot = (iota((capacity, leaf_rows), 0) == rank).astype(F32).astype(BF16)
    hits = hits.astype(BF16)
    for t in range(devices):
        chosen_ref[t * capacity : (t + 1) * capacity, :] = in_slot * hits[t : t + 1, :]
    rows_copy.wait()
    count = devices // PIECES
    for piece in range(PIECES):
        blocks = pl.ds(piece * count, count)
        sent = matmul(chosen_ref[pl.ds(piece * count * capacity, count * capacity), :], rows_ref[...])
        sent = sent.astype(BF16)
        send_ref[blocks, :capacity, :] = sent[:, :LANES].reshape(count, capacity, LANES)
        send_ref[blocks, capacity : 2 * capacity, :] = sent[:, LANES:].reshape(count, capacity, LANES)
    basis_copy.wait()
    real_copy.wait()


def codes_of(got_ref, devices, capacity):
    group = LANES // capacity
    extra = got_ref[:, 2 * capacity :, :].astype(F32)
    return [sum(extra[k + g] for g in range(group)) for k in range(0, devices, group)]


def load_kernel(after_ref, *refs, picks, turned, stores, rows_of, groups, kept, levels, height):
    refs = list(refs)

    def take(count):
        taken = refs[:count]
        del refs[:count]
        return taken

    count = len(picks)
    plain = count - turned
    gathers = 1 if rows_of else 0
    sources, stored, given = take(count), take(stores), take(2 * gathers)
    targets, held, gathered, early = take(count), take(stores), take(gathers), take(height > 0)
    scratch, chosen, landed = take(turned), take(gathers), take(rows_of == "lift")
    work, (sem,) = take(gathers and not kept), refs
    landing = targets[:plain] + scratch
    if landed:
        lift_copy = fetch(given[1].at[0], landed[0], sem.at[count + stores])

    bits = tree_bits(levels) if any(isinstance(one, tuple) for pick in picks for one in pick) else []

    def part(pick, rows):
        return tuple(
            pl.ds(pl.multiple_of(bits[one[1]] * rows, rows), rows) if isinstance(one, tuple) else one
            for one in pick
        )

    copies = [
        fetch(source.at[part(pick, target.shape[-2])], target, sem.at[k])
        for k, (source, target, pick) in enumerate(zip(sources, landing, picks))
    ]
    copies += [fetch(stored[k], held[k], sem.at[count + k]) for k in range(stores)]
    if rows_of:
        out_ref = gathered[0] if kept else work[0]
        (chosen_ref,) = chosen
        chosen_ref[...] = wide_one_hot(place_columns(given[0], groups), chosen_ref.shape[1] // LANES)
        if landed:
            lift_copy.wait()
            width = landed[0].shape[2]
            for part in range(2):
                columns = slice(part * width, (part + 1) * width)
                out_ref[:, columns] = matmul(chosen_ref[...], landed[0][part]).astype(BF16)
        else:
            out_ref[...] = folded(matmul(chosen_ref[...], given[1][...]))
        if not kept:
            copies.append(fetch(out_ref, gathered[0], sem.at[count + stores + 1]))
    if early:
        copies[0].wait()
        early[0][...] = half_product(targets[0], tree_bits(height)[-1], after_ref[...])
    for k in range(turned):
        copies[plain + k].wait()
        for part in range(2):
            targets[plain + k][part] = jnp.transpose(scratch[k][part])
    for k, copy in enumerate(copies):
        if not plain <= k < count and not (early and k == 0):
            copy.wait()


def half_product(inverse_ref, upper, half):
    rank = half.shape[0]
    columns = pl.ds(pl.multiple_of(upper * rank, rank), rank)
    return apply_complex(inverse_ref[0, :, columns], inverse_ref[1, :, columns], half, NODE_STEP)


def place_columns(place_ref, groups):
    turned = jnp.transpose(place_ref[...])
    return [
        (turned[:, k * EXTRA : k * EXTRA + 1] - 1.0) * CODE_BASE
        + turned[:, k * EXTRA + EXTRA // 2 : k * EXTRA + EXTRA // 2 + 1]
        for k in range(*groups)
    ]


def place_kernel(
    got_ref, inverse_hbm, basis_ref, placed_ref, place_ref, imag_ref, turned_ref, chosen_ref, rows_ref, sem, *,
    devices, capacity,
):
    imag_copy = fetch(inverse_hbm.at[0, 1], imag_ref, sem.at[0])
    leaf_rows = placed_ref.shape[0]
    codes = codes_of(got_ref, devices, capacity)
    place_ref[...] = jnp.concatenate(codes, axis=0)
    code = iota((CODE_BASE, LANES), 0).astype(F32)
    is_low = jnp.concatenate(
        [(code == one[EXTRA // 2 : EXTRA // 2 + 1]).astype(F32) for one in codes], axis=1
    ).astype(BF16)
    is_high = jnp.concatenate([(code == one[:1] - 1.0).astype(F32) for one in codes], axis=1).astype(BF16)
    for h in range(leaf_rows // CODE_BASE):
        chosen_ref[h * CODE_BASE : (h + 1) * CODE_BASE, :] = is_low * is_high[h : h + 1, :]
    slots = devices * capacity
    rows_ref[:, :LANES] = got_ref[:, :capacity, :].reshape(slots, LANES)
    rows_ref[:, LANES:] = got_ref[:, capacity : 2 * capacity, :].reshape(slots, LANES)
    placed_ref[...] = matmul(chosen_ref[...], rows_ref[...]).astype(BF16)
    for part in range(2):
        turned_ref[part] = jnp.transpose(basis_ref[part])
    imag_copy.wait()


def leaf_kernel(placed_ref, real_ref, imag_ref, inverse_hbm, parts_ref, inverse_ref, sem):
    copy = fetch(inverse_hbm.at[0, 0], inverse_ref, sem.at[0])
    placed = placed_ref[...]
    parts_ref[...] = two_parts(matmul(real_ref[...], placed) + matmul(imag_ref[...], rotated(placed)))
    copy.wait()


def coef_kernel(parts_ref, basis_ref, own_ref, other_ref):
    width = parts_ref.shape[1] // 2
    parts = parts_ref[...]
    turned = jnp.concatenate([rotated(parts[:, :width]), rotated(parts[:, width:])], axis=1)
    coef = folded(matmul(basis_ref[0], parts) + matmul(basis_ref[1], turned))
    first, second = swapped(coef[:, :LANES], coef[:, LANES:])
    odd = tree_bits(1)[0] == 1
    own_ref[...] = jnp.where(odd, second, first)
    other_ref[...] = jnp.where(odd, first, second)


def node_rhs(upper, own, partner):
    is_upper = upper == 1
    return jnp.concatenate(
        [jnp.where(is_upper, partner, own), jnp.where(is_upper, own, partner)], axis=0
    )


def node_kernel(own_ref, partner_ref, inverse_ref, basis_ref, sol_ref, coef_ref, code_ref, *, height):
    bit = tree_bits(height)[-1]
    if height == 1:
        rhs = node_rhs(bit, own_ref[...], partner_ref[...])
        sol = apply_complex(inverse_ref[0], inverse_ref[1], rhs, NODE_STEP)
    else:
        sol = own_ref[...] + half_product(inverse_ref, 1 - bit, decoded(partner_ref[...]))
    sol_ref[...] = sol
    coef = apply_complex(basis_ref[0], basis_ref[1], sol, NODE_STEP)
    coef_ref[...] = coef
    code_ref[...] = encoded(coef)


def descent_kernel(own_ref, partner_ref, inverse_ref, *refs, levels):
    below = levels - 1
    bits = tree_bits(levels)
    lifts, sols, coefs = refs[:below], refs[below : 2 * below], refs[2 * below : 3 * below]
    moved_hbm, mine_ref, other_ref, moved_ref, sem = refs[3 * below :]
    moved_copy = fetch(moved_hbm, moved_ref, sem.at[0])
    rank = own_ref.shape[0]
    down = own_ref[...] + half_product(inverse_ref, 1 - bits[below], decoded(partner_ref[...]))
    for k in range(below - 1, -1, -1):
        gap = coefs[k][...] - down
        if k == below - 1:
            sol = sols[k][pl.ds(pl.multiple_of(bits[k] * rank, rank), rank), :]
        else:
            sol = sols[k][...]
        down = sol - apply_complex(lifts[k][0], lifts[k][1], gap)
    swap = bits[0] == 1
    mine_ref[...] = jnp.where(swap, down[rank:], down[:rank])
    other_ref[...] = jnp.where(swap, down[:rank], down[rank:])
    moved_copy.wait()


def rows_of(refs, rows):
    parts, at = [], 0
    for ref in refs:
        first, last = max(rows.start - at, 0), min(rows.stop - at, ref.shape[0])
        if first < last:
            parts.append(ref[first:last, :])
        at += ref.shape[0]
    return parts[0] if len(parts) == 1 else jnp.concatenate(parts, axis=0)


def finish_kernel(
    mine_ref, others_ref, own_ref, other_ref, *refs, devices, capacity
):
    *pieces, send_ref = refs
    moved, pieces = pieces[:2], pieces[2:]
    swap = tree_bits(1)[0] == 1
    mine = own_ref[...] - mine_ref[...]
    other = other_ref[...] - others_ref[...]
    first, second = swapped(jnp.where(swap, other, mine), jnp.where(swap, mine, other))
    gap = jnp.concatenate([first, second], axis=1)
    rank, width = gap.shape
    parts = jnp.concatenate([two_parts(gap), two_parts(rotated(gap))], axis=0)
    count = devices // FINISH_PIECES
    for at in range(0, devices, count):
        rows = slice(at * capacity, (at + count) * capacity)
        sol = rows_of(pieces, rows) - folded(matmul(rows_of(moved, rows), parts))
        code = scale_code(sol)
        level = to_int16(rounded(sol * inverse_unit_of(code)))
        blocks = slice(at, at + count)
        send_ref[blocks, :capacity, :] = level[:, :LANES].reshape(count, capacity, LANES)
        send_ref[blocks, capacity : 2 * capacity, :] = level[:, LANES:].reshape(count, capacity, LANES)
        extra = (EXTRA, LANES)
        extra = jnp.where(
            iota(extra, 0) < EXTRA // 2,
            jnp.broadcast_to(code[:, :LANES], extra),
            jnp.broadcast_to(code[:, LANES:], extra),
        )
        send_ref[blocks, 2 * capacity :, :] = jnp.broadcast_to(
            to_int16(extra).reshape(1, EXTRA, LANES), (count, EXTRA, LANES)
        )


def unpack_kernel(got_ref, slot_ref, out_hbm, out_ref, sem, *, devices, capacity):
    slots = devices * capacity
    turned = jnp.transpose(slot_ref[...])
    chosen = wide_one_hot([turned[:, k : k + 1] for k in range(turned.shape[1])], slots // LANES)
    extra = from_int16(got_ref[:, 2 * capacity :, :])
    unit = unit_of(extra)
    unit = jnp.concatenate([unit[:, :1, :], unit[:, EXTRA // 2 : EXTRA // 2 + 1, :]], axis=2)
    largest = jnp.max(unit, axis=0)
    inverse = 1.0 / largest
    highs, lows = [], []
    for half in range(2):
        lanes = slice(half * LANES, (half + 1) * LANES)
        level = from_int16(got_ref[:, half * capacity : (half + 1) * capacity, :])
        value = (level * unit[:, :, lanes]).reshape(slots, LANES)
        high = value.astype(BF16)
        highs.append(high)
        lows.append(((value - high.astype(F32)) * inverse[:, lanes]).astype(F8))
    high, low = jnp.concatenate(highs, axis=1), jnp.concatenate(lows, axis=1)
    count = out_ref.shape[0] // PIECES
    copies = []
    for piece in range(PIECES):
        rows = pl.ds(piece * count, count)
        some = chosen[piece * count : (piece + 1) * count]
        out_ref[rows, :] = whole_matmul(some, high) + whole_matmul(some.astype(F8), low) * largest
        copies.append(fetch(out_ref.at[rows], out_hbm.at[rows], sem.at[piece]))
    for copy in copies:
        copy.wait()


def call(kernel, outs, operands, scratch=(), vmem=24):
    specs = {
        "vmem": pl.BlockSpec(memory_space=pltpu.VMEM),
        "hbm": pl.BlockSpec(memory_space=pl.ANY),
        "any": pl.BlockSpec(memory_space=pl.ANY),
    }
    results = pl.pallas_call(
        kernel,
        out_shape=[pltpu.HBM(out.shape, out.dtype) if space == "hbm" else out for out, space in outs],
        in_specs=[specs[space] for _, space in operands],
        out_specs=[specs[space] for _, space in outs],
        scratch_shapes=[
            pltpu.SemaphoreType.DMA((one,)) if isinstance(one, int) else pltpu.VMEM(one.shape, one.dtype)
            for one in scratch
        ],
        compiler_params=pltpu.CompilerParams(vmem_limit_bytes=vmem * 2**20),
    )(
        *[
            pltpu.with_memory_space_constraint(array, pltpu.HBM) if space == "hbm" else array
            for array, space in operands
        ]
    )
    return results


def shape(dims, dtype=F32):
    return jax.ShapeDtypeStruct(dims, dtype)


def from_partner(shard, axis, apart):
    return lax.ppermute(shard, axis, [(i, i ^ 1 << apart) for i in range(lax.axis_size(axis))])


def per_device(
    right_sides, tree_order, leaf_inverse, leaf_basis, leaf_lift, node_inverse, node_basis, node_lift
):
    row_count = lax.axis_size("row")
    col_count = lax.axis_size("col")
    devices = row_count * col_count
    col_levels = col_count.bit_length() - 1
    levels = col_levels + row_count.bit_length() - 1
    leaf_rows, width = right_sides.shape
    rank = leaf_basis.shape[3]
    capacity = 2 * leaf_rows // min(devices, leaf_rows // 8)
    block = (devices, 2 * capacity + EXTRA, LANES)
    sizes = dict(devices=devices, capacity=capacity)
    def exchange(blocks):
        return lax.all_to_all(blocks, ("row", "col"), split_axis=0, concat_axis=0, tiled=True)

    def partner_of(shard, height):
        if height < col_levels:
            return from_partner(shard, "col", height)
        return from_partner(shard, "row", height - col_levels)

    send, slot, real, basis = call(
        functools.partial(pack_kernel, **sizes),
        [
            (shape(block, BF16), "vmem"),
            (shape((leaf_rows // LANES, LANES)), "vmem"),
            (shape(leaf_inverse.shape[2:], BF16), "vmem"),
            (shape(leaf_basis.shape[1:], BF16), "vmem"),
        ],
        [(tree_order.reshape(1, leaf_rows), "hbm"), (right_sides, "hbm")]
        + [(leaf_inverse, "hbm"), (leaf_basis, "hbm")],
        [
            shape((1, leaf_rows), jnp.int32),
            shape(right_sides.shape, BF16),
            shape((devices * capacity, leaf_rows), BF16),
            4,
        ],
    )
    slots = devices * capacity
    total = slots // LANES
    gathers = {
        levels - 3: ("sol", (0, total // 2), False),
        levels - 2: ("sol", (total // 2, total), False),
        levels - 1: ("lift", (0, 3 * total // 8), False),
        levels: ("lift", (3 * total // 8, total), True),
    }

    def load(after, weights, picks, turned=0, stores=(), gather=("", (0, 0), False), height=0):
        shapes = [
            jax.eval_shape(
                lambda w, pick=pick: w[tuple(slice(0, rank) if isinstance(p, tuple) else p for p in pick)], w
            )
            for w, pick in zip(weights, picks)
        ]
        plain = len(weights) - turned
        outs = [shape(one.shape, one.dtype) for one in shapes[:plain]]
        outs += [shape((2, one.shape[2], one.shape[1]), one.dtype) for one in shapes[plain:]]
        rows_of, groups, kept = gather
        rows = (groups[1] - groups[0]) * LANES
        taken = {
            "": [],
            "sol": [shape((rows, width))],
            "lift": [shape((rows, 2 * rank), BF16)],
        }[rows_of]
        given = {"": [], "sol": [(place, "vmem"), (parts, "vmem")], "lift": [(place, "vmem"), (leaf_lift, "hbm")]}
        work = [shape((rows, leaf_rows), BF16)] if rows_of else []
        work += [shape(leaf_lift.shape[1:], BF16)] if rows_of == "lift" else []
        work += [] if kept else taken
        return call(
            functools.partial(
                load_kernel,
                picks=picks,
                turned=turned,
                stores=len(stores),
                rows_of=rows_of,
                groups=groups,
                kept=kept,
                levels=levels,
                height=height,
            ),
            [(out, "vmem") for out in outs]
            + [(shape(one.shape), "hbm") for one in stores]
            + [(one, "vmem" if kept else "hbm") for one in taken]
            + ([(shape((shapes[0].shape[1], LANES)), "vmem")] if height else []),
            [(after, "vmem" if height else "any")]
            + [(weight, "hbm") for weight in weights]
            + [(one, "any") for one in stores]
            + given[rows_of],
            [shape(one.shape, one.dtype) for one in shapes[plain:]]
            + work
            + [len(weights) + len(stores) + 2 * bool(rows_of)],
            vmem=14 if rows_of else 6,
        )

    place = parts = None
    got = exchange(send)
    half = shape((rank, LANES))
    placed, place, imag, basis = call(
        functools.partial(place_kernel, **sizes),
        [
            (shape((leaf_rows, width), BF16), "vmem"),
            (shape((slots // LANES * EXTRA, LANES)), "vmem"),
            (shape(leaf_inverse.shape[2:], BF16), "vmem"),
            (shape((2, rank, leaf_rows), BF16), "vmem"),
        ],
        [(got, "vmem"), (leaf_inverse, "hbm"), (basis, "vmem")],
        [shape((leaf_rows, slots), BF16), shape((slots, width), BF16), 1],
    )
    parts, lowest = call(
        leaf_kernel,
        [(shape((leaf_rows, 2 * width), BF16), "vmem"), (shape(node_inverse.shape[2:], BF16), "vmem")],
        [(placed, "vmem"), (real, "vmem"), (imag, "vmem"), (node_inverse, "hbm")],
        [1],
    )
    own, other = call(
        coef_kernel,
        [(half, "vmem"), (half, "vmem")],
        [(parts, "vmem"), (basis, "vmem")],
    )
    leaf_own, leaf_other = own, other
    whole = shape((2 * rank, LANES))
    sols, stored, coefs, gathered = [], [], [], []
    no_gather = ("", (0, 0), False)
    for height in range(1, levels):
        partner = partner_of(other if height == 1 else code, height - 1)
        pick = (0, height - 1)
        first = height == 1
        loaded = load(
            own,
            (node_basis,) if first else (node_inverse, node_basis),
            (pick,) if first else (pick, pick),
            1,
            sols[-1:],
            gathers.get(height, no_gather),
            0 if first else height,
        )
        (inverse, basis, *kept) = (lowest, *loaded) if first else loaded
        early = own if first else kept.pop()
        stored += kept[: len(sols[-1:])]
        gathered += kept[len(sols[-1:]) :]
        sol, own, code = call(
            functools.partial(node_kernel, height=height),
            [(whole, "vmem"), (half, "vmem"), (shape((rank + TAIL, LANES), jnp.int16), "vmem")],
            [
                (early, "vmem"),
                (partner, "vmem"),
                (inverse, "vmem"),
                (basis, "vmem"),
            ],
            vmem=8,
        )
        sols.append(sol)
        coefs.append(own)
    partner = partner_of(code, levels - 1)
    loaded = load(
        own,
        (node_inverse, *(node_lift for _ in coefs), *stored),
        (
            (0, levels - 1, slice(None), ("half", levels - 1)),
            (0, 0),
            *((0, k, slice(None), ("half", k)) for k in range(1, levels - 1)),
            (),
            *((("half", k),) for k in range(1, levels - 2)),
        ),
        gather=gathers[levels],
        height=levels,
    )
    *loaded, early = loaded
    inverse, lifts, sols = loaded[0], loaded[1:levels], [*loaded[levels:-1], sols[-1]]
    gathered.append(loaded[-1])
    mine, other, moved = call(
        functools.partial(descent_kernel, levels=levels),
        [
            (half, "vmem"),
            (half, "vmem"),
            (shape(gathered[2].shape, BF16), "vmem"),
        ],
        [(early, "vmem"), (partner, "vmem"), (inverse, "vmem")]
        + [(lift, "vmem") for lift in lifts]
        + [(sol, "vmem") for sol in sols]
        + [(coef, "vmem") for coef in coefs]
        + [(one, "hbm") for one in gathered[2:-1]],
        [1],
        vmem=8,
    )
    other_sent = other
    other = partner_of(other_sent, 0)
    bases = load(other_sent, gathered[:2], ((),) * 2)
    (back,) = call(
        functools.partial(finish_kernel, **sizes),
        [(shape(block, jnp.int16), "vmem")],
        [
            (mine, "vmem"),
            (other, "vmem"),
            (leaf_own, "vmem"),
            (leaf_other, "vmem"),
            (moved, "vmem"),
            (gathered[-1], "vmem"),
        ]
        + [(one, "vmem") for one in bases],
    )
    returned = exchange(back)
    (result,) = call(
        functools.partial(unpack_kernel, **sizes),
        [(shape((leaf_rows, width)), "hbm")],
        [(returned, "vmem"), (slot, "vmem")],
        [shape((leaf_rows, width)), PIECES],
    )
    return result


def solution(mesh):
    in_specs = (
        P(("row", "col"), None),
        P(("row", "col")),
        P(("row", "col"), None, None, None),
        P(("row", "col"), None, None, None),
        P(("row", "col"), None, None, None),
        P(("row", "col"), None, None, None, None),
        P(("row", "col"), None, None, None, None),
        P(("row", "col"), None, None, None, None),
    )
    out_specs = P(("row", "col"), None)
    return jax.shard_map(
        per_device, mesh=mesh, in_specs=in_specs, out_specs=out_specs, check_vma=False
    )
```

```python
import functools

import jax
import jax.numpy as jnp
from jax import lax
from jax.experimental import pallas as pl
from jax.experimental.pallas import tpu as pltpu
from jax.sharding import PartitionSpec as P

LANES = 128
EXTRA = 8
CODE_BASE = 32
SCALE_STEPS = 64
HEADROOM = 1.002
ROUNDER = 1.5 * 2.0**23
TAIL = 16
STEP = 256
PIECES = 4
NODE_STEP = 128
FINISH_PIECES = 8
BF16 = jnp.bfloat16
F32 = jnp.float32
F8 = jnp.float8_e4m3fn


def whole_matmul(a, b):
    return lax.dot_general(a, b, (((1,), (0,)), ((), ())), preferred_element_type=F32)


def matmul(a, b, step=STEP):
    pieces = [whole_matmul(a[at : at + step], b) for at in range(0, a.shape[0], step)]
    return pieces[0] if len(pieces) == 1 else jnp.concatenate(pieces, axis=0)


def matmul_nt(a, b):
    return lax.dot_general(a, b, (((1,), (1,)), ((), ())), preferred_element_type=F32)


def tree_bits(levels):
    index = lax.axis_index("row") * lax.axis_size("col") + lax.axis_index("col")
    return [index >> height & 1 for height in range(levels)]


def iota(shape, dim):
    return lax.broadcasted_iota(jnp.int32, shape, dim)


def rotated(x):
    if x.shape[1] == LANES:
        turned = pltpu.roll(x, LANES // 2, 1)
        return jnp.where(iota(x.shape, 1) < LANES // 2, -turned, turned)
    return jnp.concatenate([-x[:, LANES:], x[:, :LANES]], axis=1)


def swapped(first, second):
    low = iota(first.shape, 1) < LANES // 2
    return (
        jnp.where(low, first, pltpu.roll(second, LANES // 2, 1)),
        jnp.where(low, pltpu.roll(first, LANES // 2, 1), second),
    )


def two_parts(x):
    high = x.astype(BF16)
    low = (x - high.astype(F32)).astype(BF16)
    return jnp.concatenate([high, low], axis=1)


def folded(both):
    width = both.shape[1] // 2
    return both[:, :width] + both[:, width:]


def apply_complex(real, imag, x, step=STEP):
    both = jnp.concatenate([two_parts(x), two_parts(rotated(x))], axis=0)
    return folded(matmul(jnp.concatenate([real, imag], axis=1), both, step))


def unit_of(code):
    return jnp.exp2(code * (1.0 / SCALE_STEPS) - 15.0) * HEADROOM


def inverse_unit_of(code):
    return jnp.exp2(15.0 - code * (1.0 / SCALE_STEPS)) * (1.0 / HEADROOM)


def rounded(x):
    return (x + ROUNDER) - ROUNDER


def to_int16(x):
    return x.astype(jnp.int32).astype(jnp.int16)


def from_int16(x):
    return x.astype(jnp.int32).astype(F32)


def encoded(x):
    code = scale_code(x)
    level = rounded(x * inverse_unit_of(code))
    return to_int16(jnp.concatenate([level, jnp.broadcast_to(code, (TAIL, LANES))], axis=0))


def decoded(levels):
    values = from_int16(levels)
    return values[:-TAIL] * unit_of(values[-TAIL : 1 - TAIL])


def scale_code(x):
    largest = jnp.max(jnp.abs(x), axis=0, keepdims=True)
    return jnp.ceil(jnp.log2(jnp.maximum(largest, 2.0**-110)) * SCALE_STEPS)


def fetch(source, target, sem):
    copy = pltpu.make_async_copy(source, target, sem)
    copy.start()
    return copy


def wide_one_hot(columns, blocks):
    lane = iota((LANES, LANES), 1).astype(F32)
    one, zero = jnp.ones((), BF16), jnp.zeros((), BF16)
    names = []
    for entry in columns:
        block = jnp.floor(entry * (1.0 / LANES))
        names.append(jnp.where(lane == entry - block * LANES, block, -1.0))
    names = jnp.concatenate(names, axis=0).astype(BF16)
    return jnp.concatenate([jnp.where(names == jnp.array(g, BF16), one, zero) for g in range(blocks)], axis=1)


def row_blocks(x):
    return jnp.concatenate([x[:, at : at + LANES] for at in range(0, x.shape[1], LANES)], axis=0)


def ranks(hits):
    rows, width = hits.shape
    upper = (iota((LANES, LANES), 0) < iota((LANES, LANES), 1)).astype(F32).astype(BF16)
    pieces = jnp.concatenate(
        [hits[:, at : at + LANES] for at in range(0, width, LANES)], axis=0
    ).astype(BF16)
    inside = matmul(pieces, upper)
    totals = matmul(pieces, jnp.ones((LANES, LANES), BF16))
    ahead = jnp.zeros((rows, LANES), F32)
    parts = []
    for k in range(width // LANES):
        parts.append(inside[k * rows : (k + 1) * rows] + ahead)
        ahead = ahead + totals[k * rows : (k + 1) * rows]
    return jnp.concatenate(parts, axis=1)


def pack_kernel(
    order_hbm, rows_hbm, inverse_hbm, basis_hbm, send_ref, slot_ref, real_ref, basis_ref,
    order_ref, rows_ref, chosen_ref, sem, *,
    devices, capacity,
):
    order_copy = fetch(order_hbm, order_ref, sem.at[0])
    rows_copy = fetch(rows_hbm, rows_ref, sem.at[1])
    basis_copy = fetch(basis_hbm.at[0], basis_ref, sem.at[2])
    real_copy = fetch(inverse_hbm.at[0, 0], real_ref, sem.at[3])
    leaf_rows = rows_ref.shape[0]
    order_copy.wait()
    order = order_ref[...]
    target = order // leaf_rows
    position = order - target * leaf_rows
    hits = (iota((devices, leaf_rows), 0) == target).astype(F32)
    rank = jnp.sum(hits * ranks(hits), axis=0, keepdims=True).astype(jnp.int32)
    slot_ref[...] = row_blocks((target * capacity + rank).astype(F32))
    group = LANES // capacity
    lane = rank + lax.rem(lax.axis_index("row") * lax.axis_size("col") + lax.axis_index("col"), group) * capacity
    high = position // CODE_BASE
    low = position - high * CODE_BASE
    codes = jnp.concatenate([hits * (high + 1).astype(F32), hits * low.astype(F32)], axis=0)
    places = (iota((LANES, leaf_rows), 0) == lane).astype(F32).astype(BF16)
    spread = matmul_nt(codes.astype(BF16), places)
    extra = (devices, EXTRA, LANES)
    send_ref[:, 2 * capacity :, :] = jnp.where(
        iota(extra, 1) < EXTRA // 2,
        jnp.broadcast_to(spread[:devices].reshape(devices, 1, LANES), extra),
        jnp.broadcast_to(spread[devices:].reshape(devices, 1, LANES), extra),
    ).astype(BF16)
    in_slot = (iota((capacity, leaf_rows), 0) == rank).astype(F32).astype(BF16)
    hits = hits.astype(BF16)
    for t in range(devices):
        chosen_ref[t * capacity : (t + 1) * capacity, :] = in_slot * hits[t : t + 1, :]
    rows_copy.wait()
    count = devices // PIECES
    for piece in range(PIECES):
        blocks = pl.ds(piece * count, count)
        sent = matmul(chosen_ref[pl.ds(piece * count * capacity, count * capacity), :], rows_ref[...])
        sent = sent.astype(BF16)
        send_ref[blocks, :capacity, :] = sent[:, :LANES].reshape(count, capacity, LANES)
        send_ref[blocks, capacity : 2 * capacity, :] = sent[:, LANES:].reshape(count, capacity, LANES)
    basis_copy.wait()
    real_copy.wait()


def codes_of(got_ref, devices, capacity):
    group = LANES // capacity
    extra = got_ref[:, 2 * capacity :, :].astype(F32)
    return [sum(extra[k + g] for g in range(group)) for k in range(0, devices, group)]


def load_kernel(after_ref, *refs, picks, turned, stores, rows_of, groups, kept, levels, height):
    refs = list(refs)

    def take(count):
        taken = refs[:count]
        del refs[:count]
        return taken

    count = len(picks)
    plain = count - turned
    gathers = 1 if rows_of else 0
    sources, stored, given = take(count), take(stores), take(2 * gathers)
    targets, held, gathered, early = take(count), take(stores), take(gathers), take(height > 0)
    scratch, chosen, landed = take(turned), take(gathers), take(rows_of == "lift")
    work, (sem,) = take(gathers and not kept), refs
    landing = targets[:plain] + scratch
    if landed:
        lift_copy = fetch(given[1].at[0], landed[0], sem.at[count + stores])

    bits = tree_bits(levels) if any(isinstance(one, tuple) for pick in picks for one in pick) else []

    def part(pick, rows):
        return tuple(
            pl.ds(pl.multiple_of(bits[one[1]] * rows, rows), rows) if isinstance(one, tuple) else one
            for one in pick
        )

    copies = [
        fetch(source.at[part(pick, target.shape[-2])], target, sem.at[k])
        for k, (source, target, pick) in enumerate(zip(sources, landing, picks))
    ]
    copies += [fetch(stored[k], held[k], sem.at[count + k]) for k in range(stores)]
    if rows_of:
        out_ref = gathered[0] if kept else work[0]
        (chosen_ref,) = chosen
        chosen_ref[...] = wide_one_hot(place_columns(given[0], groups), chosen_ref.shape[1] // LANES)
        if landed:
            lift_copy.wait()
            width = landed[0].shape[2]
            for part in range(2):
                columns = slice(part * width, (part + 1) * width)
                out_ref[:, columns] = matmul(chosen_ref[...], landed[0][part]).astype(BF16)
        else:
            out_ref[...] = folded(matmul(chosen_ref[...], given[1][...]))
        if not kept:
            copies.append(fetch(out_ref, gathered[0], sem.at[count + stores + 1]))
    if early:
        copies[0].wait()
        early[0][...] = half_product(targets[0], tree_bits(height)[-1], after_ref[...])
    for k in range(turned):
        copies[plain + k].wait()
        for part in range(2):
            targets[plain + k][part] = jnp.transpose(scratch[k][part])
    for k, copy in enumerate(copies):
        if not plain <= k < count and not (early and k == 0):
            copy.wait()


def half_product(inverse_ref, upper, half):
    rank = half.shape[0]
    columns = pl.ds(pl.multiple_of(upper * rank, rank), rank)
    return apply_complex(inverse_ref[0, :, columns], inverse_ref[1, :, columns], half, NODE_STEP)


def place_columns(place_ref, groups):
    turned = jnp.transpose(place_ref[...])
    return [
        (turned[:, k * EXTRA : k * EXTRA + 1] - 1.0) * CODE_BASE
        + turned[:, k * EXTRA + EXTRA // 2 : k * EXTRA + EXTRA // 2 + 1]
        for k in range(*groups)
    ]


def place_kernel(
    got_ref, inverse_hbm, basis_ref, placed_ref, place_ref, imag_ref, turned_ref, chosen_ref, rows_ref, sem, *,
    devices, capacity,
):
    imag_copy = fetch(inverse_hbm.at[0, 1], imag_ref, sem.at[0])
    leaf_rows = placed_ref.shape[0]
    codes = codes_of(got_ref, devices, capacity)
    place_ref[...] = jnp.concatenate(codes, axis=0)
    code = iota((CODE_BASE, LANES), 0).astype(F32)
    is_low = jnp.concatenate(
        [(code == one[EXTRA // 2 : EXTRA // 2 + 1]).astype(F32) for one in codes], axis=1
    ).astype(BF16)
    is_high = jnp.concatenate([(code == one[:1] - 1.0).astype(F32) for one in codes], axis=1).astype(BF16)
    for h in range(leaf_rows // CODE_BASE):
        chosen_ref[h * CODE_BASE : (h + 1) * CODE_BASE, :] = is_low * is_high[h : h + 1, :]
    slots = devices * capacity
    rows_ref[:, :LANES] = got_ref[:, :capacity, :].reshape(slots, LANES)
    rows_ref[:, LANES:] = got_ref[:, capacity : 2 * capacity, :].reshape(slots, LANES)
    placed_ref[...] = matmul(chosen_ref[...], rows_ref[...]).astype(BF16)
    for part in range(2):
        turned_ref[part] = jnp.transpose(basis_ref[part])
    imag_copy.wait()


def leaf_kernel(placed_ref, real_ref, imag_ref, inverse_hbm, parts_ref, inverse_ref, sem):
    copy = fetch(inverse_hbm.at[0, 0], inverse_ref, sem.at[0])
    placed = placed_ref[...]
    parts_ref[...] = two_parts(matmul(real_ref[...], placed) + matmul(imag_ref[...], rotated(placed)))
    copy.wait()


def coef_kernel(parts_ref, basis_ref, own_ref, other_ref):
    width = parts_ref.shape[1] // 2
    parts = parts_ref[...]
    turned = jnp.concatenate([rotated(parts[:, :width]), rotated(parts[:, width:])], axis=1)
    coef = folded(matmul(basis_ref[0], parts) + matmul(basis_ref[1], turned))
    first, second = swapped(coef[:, :LANES], coef[:, LANES:])
    odd = tree_bits(1)[0] == 1
    own_ref[...] = jnp.where(odd, second, first)
    other_ref[...] = jnp.where(odd, first, second)


def node_rhs(upper, own, partner):
    is_upper = upper == 1
    return jnp.concatenate(
        [jnp.where(is_upper, partner, own), jnp.where(is_upper, own, partner)], axis=0
    )


def node_kernel(own_ref, partner_ref, inverse_ref, basis_ref, sol_ref, coef_ref, code_ref, *, height):
    bit = tree_bits(height)[-1]
    if height == 1:
        rhs = node_rhs(bit, own_ref[...], partner_ref[...])
        sol = apply_complex(inverse_ref[0], inverse_ref[1], rhs, NODE_STEP)
    else:
        sol = own_ref[...] + half_product(inverse_ref, 1 - bit, decoded(partner_ref[...]))
    sol_ref[...] = sol
    coef = apply_complex(basis_ref[0], basis_ref[1], sol, NODE_STEP)
    coef_ref[...] = coef
    code_ref[...] = encoded(coef)


def descent_kernel(own_ref, partner_ref, inverse_ref, *refs, levels):
    below = levels - 1
    bits = tree_bits(levels)
    lifts, sols, coefs = refs[:below], refs[below : 2 * below], refs[2 * below : 3 * below]
    mine_ref, other_ref = refs[3 * below :]
    rank = own_ref.shape[0]
    down = own_ref[...] + half_product(inverse_ref, 1 - bits[below], decoded(partner_ref[...]))
    for k in range(below - 1, -1, -1):
        gap = coefs[k][...] - down
        if k == below - 1:
            sol = sols[k][pl.ds(pl.multiple_of(bits[k] * rank, rank), rank), :]
        else:
            sol = sols[k][...]
        down = sol - apply_complex(lifts[k][0], lifts[k][1], gap)
    swap = bits[0] == 1
    mine_ref[...] = jnp.where(swap, down[rank:], down[:rank])
    other_ref[...] = jnp.where(swap, down[:rank], down[rank:])


def rows_of(refs, rows):
    parts, at = [], 0
    for ref in refs:
        first, last = max(rows.start - at, 0), min(rows.stop - at, ref.shape[0])
        if first < last:
            parts.append(ref[first:last, :])
        at += ref.shape[0]
    return parts[0] if len(parts) == 1 else jnp.concatenate(parts, axis=0)


def finish_kernel(
    mine_ref, others_ref, own_ref, other_ref, *refs, devices, capacity
):
    *pieces, send_ref = refs
    moved, pieces = pieces[:2], pieces[2:]
    swap = tree_bits(1)[0] == 1
    mine = own_ref[...] - mine_ref[...]
    other = other_ref[...] - others_ref[...]
    first, second = swapped(jnp.where(swap, other, mine), jnp.where(swap, mine, other))
    gap = jnp.concatenate([first, second], axis=1)
    rank, width = gap.shape
    parts = jnp.concatenate([two_parts(gap), two_parts(rotated(gap))], axis=0)
    count = devices // FINISH_PIECES
    for at in range(0, devices, count):
        rows = slice(at * capacity, (at + count) * capacity)
        sol = rows_of(pieces, rows) - folded(matmul(rows_of(moved, rows), parts, NODE_STEP))
        code = scale_code(sol)
        level = to_int16(rounded(sol * inverse_unit_of(code)))
        blocks = slice(at, at + count)
        send_ref[blocks, :capacity, :] = level[:, :LANES].reshape(count, capacity, LANES)
        send_ref[blocks, capacity : 2 * capacity, :] = level[:, LANES:].reshape(count, capacity, LANES)
        extra = (EXTRA, LANES)
        extra = jnp.where(
            iota(extra, 0) < EXTRA // 2,
            jnp.broadcast_to(code[:, :LANES], extra),
            jnp.broadcast_to(code[:, LANES:], extra),
        )
        send_ref[blocks, 2 * capacity :, :] = jnp.broadcast_to(
            to_int16(extra).reshape(1, EXTRA, LANES), (count, EXTRA, LANES)
        )


def unpack_kernel(got_ref, slot_ref, out_hbm, out_ref, sem, *, devices, capacity):
    slots = devices * capacity
    turned = jnp.transpose(slot_ref[...])
    chosen = wide_one_hot([turned[:, k : k + 1] for k in range(turned.shape[1])], slots // LANES)
    extra = from_int16(got_ref[:, 2 * capacity :, :])
    unit = unit_of(extra)
    unit = jnp.concatenate([unit[:, :1, :], unit[:, EXTRA // 2 : EXTRA // 2 + 1, :]], axis=2)
    largest = jnp.max(unit, axis=0)
    inverse = 1.0 / largest
    highs, lows = [], []
    for half in range(2):
        lanes = slice(half * LANES, (half + 1) * LANES)
        level = from_int16(got_ref[:, half * capacity : (half + 1) * capacity, :])
        value = (level * unit[:, :, lanes]).reshape(slots, LANES)
        high = value.astype(BF16)
        highs.append(high)
        lows.append(((value - high.astype(F32)) * inverse[:, lanes]).astype(F8))
    high, low = jnp.concatenate(highs, axis=1), jnp.concatenate(lows, axis=1)
    count = out_ref.shape[0] // PIECES
    copies = []
    for piece in range(PIECES):
        rows = pl.ds(piece * count, count)
        some = chosen[piece * count : (piece + 1) * count]
        out_ref[rows, :] = whole_matmul(some, high) + whole_matmul(some.astype(F8), low) * largest
        copies.append(fetch(out_ref.at[rows], out_hbm.at[rows], sem.at[piece]))
    for copy in copies:
        copy.wait()


def call(kernel, outs, operands, scratch=(), vmem=24):
    specs = {
        "vmem": pl.BlockSpec(memory_space=pltpu.VMEM),
        "hbm": pl.BlockSpec(memory_space=pl.ANY),
        "any": pl.BlockSpec(memory_space=pl.ANY),
    }
    results = pl.pallas_call(
        kernel,
        out_shape=[pltpu.HBM(out.shape, out.dtype) if space == "hbm" else out for out, space in outs],
        in_specs=[specs[space] for _, space in operands],
        out_specs=[specs[space] for _, space in outs],
        scratch_shapes=[
            pltpu.SemaphoreType.DMA((one,)) if isinstance(one, int) else pltpu.VMEM(one.shape, one.dtype)
            for one in scratch
        ],
        compiler_params=pltpu.CompilerParams(vmem_limit_bytes=vmem * 2**20),
    )(
        *[
            pltpu.with_memory_space_constraint(array, pltpu.HBM) if space == "hbm" else array
            for array, space in operands
        ]
    )
    return results


def shape(dims, dtype=F32):
    return jax.ShapeDtypeStruct(dims, dtype)


def from_partner(shard, axis, apart):
    return lax.ppermute(shard, axis, [(i, i ^ 1 << apart) for i in range(lax.axis_size(axis))])


def per_device(
    right_sides, tree_order, leaf_inverse, leaf_basis, leaf_lift, node_inverse, node_basis, node_lift
):
    row_count = lax.axis_size("row")
    col_count = lax.axis_size("col")
    devices = row_count * col_count
    col_levels = col_count.bit_length() - 1
    levels = col_levels + row_count.bit_length() - 1
    leaf_rows, width = right_sides.shape
    rank = leaf_basis.shape[3]
    capacity = 2 * leaf_rows // min(devices, leaf_rows // 8)
    block = (devices, 2 * capacity + EXTRA, LANES)
    sizes = dict(devices=devices, capacity=capacity)
    def exchange(blocks):
        return lax.all_to_all(blocks, ("row", "col"), split_axis=0, concat_axis=0, tiled=True)

    def partner_of(shard, height):
        if height < col_levels:
            return from_partner(shard, "col", height)
        return from_partner(shard, "row", height - col_levels)

    send, slot, real, basis = call(
        functools.partial(pack_kernel, **sizes),
        [
            (shape(block, BF16), "vmem"),
            (shape((leaf_rows // LANES, LANES)), "vmem"),
            (shape(leaf_inverse.shape[2:], BF16), "vmem"),
            (shape(leaf_basis.shape[1:], BF16), "vmem"),
        ],
        [(tree_order.reshape(1, leaf_rows), "hbm"), (right_sides, "hbm")]
        + [(leaf_inverse, "hbm"), (leaf_basis, "hbm")],
        [
            shape((1, leaf_rows), jnp.int32),
            shape(right_sides.shape, BF16),
            shape((devices * capacity, leaf_rows), BF16),
            4,
        ],
    )
    slots = devices * capacity
    total = slots // LANES
    gathers = {
        levels - 3: ("sol", (0, total // 2), False),
        levels - 2: ("sol", (total // 2, total), False),
        levels - 1: ("lift", (0, 3 * total // 8), True),
        levels: ("lift", (3 * total // 8, total), True),
    }

    def load(after, weights, picks, turned=0, stores=(), gather=("", (0, 0), False), height=0):
        shapes = [
            jax.eval_shape(
                lambda w, pick=pick: w[tuple(slice(0, rank) if isinstance(p, tuple) else p for p in pick)], w
            )
            for w, pick in zip(weights, picks)
        ]
        plain = len(weights) - turned
        outs = [shape(one.shape, one.dtype) for one in shapes[:plain]]
        outs += [shape((2, one.shape[2], one.shape[1]), one.dtype) for one in shapes[plain:]]
        rows_of, groups, kept = gather
        rows = (groups[1] - groups[0]) * LANES
        taken = {
            "": [],
            "sol": [shape((rows, width))],
            "lift": [shape((rows, 2 * rank), BF16)],
        }[rows_of]
        given = {"": [], "sol": [(place, "vmem"), (parts, "vmem")], "lift": [(place, "vmem"), (leaf_lift, "hbm")]}
        work = [shape((rows, leaf_rows), BF16)] if rows_of else []
        work += [shape(leaf_lift.shape[1:], BF16)] if rows_of == "lift" else []
        work += [] if kept else taken
        return call(
            functools.partial(
                load_kernel,
                picks=picks,
                turned=turned,
                stores=len(stores),
                rows_of=rows_of,
                groups=groups,
                kept=kept,
                levels=levels,
                height=height,
            ),
            [(out, "vmem") for out in outs]
            + [(shape(one.shape), "hbm") for one in stores]
            + [(one, "vmem" if kept else "hbm") for one in taken]
            + ([(shape((shapes[0].shape[1], LANES)), "vmem")] if height else []),
            [(after, "vmem" if height else "any")]
            + [(weight, "hbm") for weight in weights]
            + [(one, "any") for one in stores]
            + given[rows_of],
            [shape(one.shape, one.dtype) for one in shapes[plain:]]
            + work
            + [len(weights) + len(stores) + 2 * bool(rows_of)],
            vmem=14 if rows_of else 6,
        )

    place = parts = None
    got = exchange(send)
    half = shape((rank, LANES))
    placed, place, imag, basis = call(
        functools.partial(place_kernel, **sizes),
        [
            (shape((leaf_rows, width), BF16), "vmem"),
            (shape((slots // LANES * EXTRA, LANES)), "vmem"),
            (shape(leaf_inverse.shape[2:], BF16), "vmem"),
            (shape((2, rank, leaf_rows), BF16), "vmem"),
        ],
        [(got, "vmem"), (leaf_inverse, "hbm"), (basis, "vmem")],
        [shape((leaf_rows, slots), BF16), shape((slots, width), BF16), 1],
    )
    parts, lowest = call(
        leaf_kernel,
        [(shape((leaf_rows, 2 * width), BF16), "vmem"), (shape(node_inverse.shape[2:], BF16), "vmem")],
        [(placed, "vmem"), (real, "vmem"), (imag, "vmem"), (node_inverse, "hbm")],
        [1],
    )
    own, other = call(
        coef_kernel,
        [(half, "vmem"), (half, "vmem")],
        [(parts, "vmem"), (basis, "vmem")],
    )
    leaf_own, leaf_other = own, other
    whole = shape((2 * rank, LANES))
    sols, stored, coefs, gathered = [], [], [], []
    no_gather = ("", (0, 0), False)
    for height in range(1, levels):
        partner = partner_of(other if height == 1 else code, height - 1)
        pick = (0, height - 1)
        first = height == 1
        loaded = load(
            own,
            (node_basis,) if first else (node_inverse, node_basis),
            (pick,) if first else (pick, pick),
            1,
            sols[-1:],
            gathers.get(height, no_gather),
            0 if first else height,
        )
        (inverse, basis, *kept) = (lowest, *loaded) if first else loaded
        early = own if first else kept.pop()
        stored += kept[: len(sols[-1:])]
        gathered += kept[len(sols[-1:]) :]
        sol, own, code = call(
            functools.partial(node_kernel, height=height),
            [(whole, "vmem"), (half, "vmem"), (shape((rank + TAIL, LANES), jnp.int16), "vmem")],
            [
                (early, "vmem"),
                (partner, "vmem"),
                (inverse, "vmem"),
                (basis, "vmem"),
            ],
            vmem=8,
        )
        sols.append(sol)
        coefs.append(own)
    partner = partner_of(code, levels - 1)
    loaded = load(
        own,
        (node_inverse, *(node_lift for _ in coefs), *stored, gathered[0]),
        (
            (0, levels - 1, slice(None), ("half", levels - 1)),
            (0, 0),
            *((0, k, slice(None), ("half", k)) for k in range(1, levels - 1)),
            (),
            *((("half", k),) for k in range(1, levels - 2)),
            (),
        ),
        gather=gathers[levels],
        height=levels,
    )
    *loaded, early = loaded
    inverse, lifts, sols = loaded[0], loaded[1:levels], [*loaded[levels:-2], sols[-1]]
    gathered.append(loaded[-1])
    mine, other = call(
        functools.partial(descent_kernel, levels=levels),
        [
            (half, "vmem"),
            (half, "vmem"),
        ],
        [(early, "vmem"), (partner, "vmem"), (inverse, "vmem")]
        + [(lift, "vmem") for lift in lifts]
        + [(sol, "vmem") for sol in sols]
        + [(coef, "vmem") for coef in coefs],
        vmem=8,
    )
    other_sent = other
    other = partner_of(other_sent, 0)
    bases = [loaded[-2], *load(other_sent, gathered[1:2], ((),))]
    (back,) = call(
        functools.partial(finish_kernel, **sizes),
        [(shape(block, jnp.int16), "vmem")],
        [
            (mine, "vmem"),
            (other, "vmem"),
            (leaf_own, "vmem"),
            (leaf_other, "vmem"),
            (gathered[2], "vmem"),
            (gathered[3], "vmem"),
        ]
        + [(one, "vmem") for one in bases],
    )
    returned = exchange(back)
    (result,) = call(
        functools.partial(unpack_kernel, **sizes),
        [(shape((leaf_rows, width)), "hbm")],
        [(returned, "vmem"), (slot, "vmem")],
        [shape((leaf_rows, width)), PIECES],
    )
    return result


def solution(mesh):
    in_specs = (
        P(("row", "col"), None),
        P(("row", "col")),
        P(("row", "col"), None, None, None),
        P(("row", "col"), None, None, None),
        P(("row", "col"), None, None, None),
        P(("row", "col"), None, None, None, None),
        P(("row", "col"), None, None, None, None),
        P(("row", "col"), None, None, None, None),
    )
    out_specs = P(("row", "col"), None)
    return jax.shard_map(
        per_device, mesh=mesh, in_specs=in_specs, out_specs=out_specs, check_vma=False
    )
```

```python
import functools

import jax
import jax.numpy as jnp
from jax import lax
from jax.experimental import pallas as pl
from jax.experimental.pallas import tpu as pltpu
from jax.sharding import PartitionSpec as P

LANES = 128
EXTRA = 8
CODE_BASE = 32
SCALE_STEPS = 64
HEADROOM = 1.002
ROUNDER = 1.5 * 2.0**23
TAIL = 16
STEP = 256
PIECES = 4
NODE_STEP = 128
FINISH_PIECES = 8
BF16 = jnp.bfloat16
F32 = jnp.float32
F8 = jnp.float8_e4m3fn


def whole_matmul(a, b):
    return lax.dot_general(a, b, (((1,), (0,)), ((), ())), preferred_element_type=F32)


def matmul(a, b, step=STEP):
    pieces = [whole_matmul(a[at : at + step], b) for at in range(0, a.shape[0], step)]
    return pieces[0] if len(pieces) == 1 else jnp.concatenate(pieces, axis=0)


def matmul_nt(a, b):
    return lax.dot_general(a, b, (((1,), (1,)), ((), ())), preferred_element_type=F32)


def tree_bits(levels):
    index = lax.axis_index("row") * lax.axis_size("col") + lax.axis_index("col")
    return [index >> height & 1 for height in range(levels)]


def iota(shape, dim):
    return lax.broadcasted_iota(jnp.int32, shape, dim)


def rotated(x):
    if x.shape[1] == LANES:
        turned = pltpu.roll(x, LANES // 2, 1)
        return jnp.where(iota(x.shape, 1) < LANES // 2, -turned, turned)
    return jnp.concatenate([-x[:, LANES:], x[:, :LANES]], axis=1)


def swapped(first, second):
    low = iota(first.shape, 1) < LANES // 2
    return (
        jnp.where(low, first, pltpu.roll(second, LANES // 2, 1)),
        jnp.where(low, pltpu.roll(first, LANES // 2, 1), second),
    )


def two_parts(x):
    high = x.astype(BF16)
    low = (x - high.astype(F32)).astype(BF16)
    return jnp.concatenate([high, low], axis=1)


def folded(both):
    width = both.shape[1] // 2
    return both[:, :width] + both[:, width:]


def apply_complex(real, imag, x, step=STEP):
    both = jnp.concatenate([two_parts(x), two_parts(rotated(x))], axis=0)
    return folded(matmul(jnp.concatenate([real, imag], axis=1), both, step))


def unit_of(code):
    return jnp.exp2(code * (1.0 / SCALE_STEPS) - 15.0) * HEADROOM


def inverse_unit_of(code):
    return jnp.exp2(15.0 - code * (1.0 / SCALE_STEPS)) * (1.0 / HEADROOM)


def rounded(x):
    return (x + ROUNDER) - ROUNDER


def to_int16(x):
    return x.astype(jnp.int32).astype(jnp.int16)


def from_int16(x):
    return x.astype(jnp.int32).astype(F32)


def encoded(x):
    code = scale_code(x)
    level = rounded(x * inverse_unit_of(code))
    return to_int16(jnp.concatenate([level, jnp.broadcast_to(code, (TAIL, LANES))], axis=0))


def decoded(levels):
    values = from_int16(levels)
    return values[:-TAIL] * unit_of(values[-TAIL : 1 - TAIL])


def scale_code(x):
    largest = jnp.max(jnp.abs(x), axis=0, keepdims=True)
    return jnp.ceil(jnp.log2(jnp.maximum(largest, 2.0**-110)) * SCALE_STEPS)


def fetch(source, target, sem):
    copy = pltpu.make_async_copy(source, target, sem)
    copy.start()
    return copy


def wide_one_hot(columns, blocks):
    lane = iota((LANES, LANES), 1).astype(F32)
    one, zero = jnp.ones((), BF16), jnp.zeros((), BF16)
    names = []
    for entry in columns:
        block = jnp.floor(entry * (1.0 / LANES))
        names.append(jnp.where(lane == entry - block * LANES, block, -1.0))
    names = jnp.concatenate(names, axis=0).astype(BF16)
    return jnp.concatenate([jnp.where(names == jnp.array(g, BF16), one, zero) for g in range(blocks)], axis=1)


def row_blocks(x):
    return jnp.concatenate([x[:, at : at + LANES] for at in range(0, x.shape[1], LANES)], axis=0)


def ranks(hits):
    rows, width = hits.shape
    upper = (iota((LANES, LANES), 0) < iota((LANES, LANES), 1)).astype(F32).astype(BF16)
    pieces = jnp.concatenate(
        [hits[:, at : at + LANES] for at in range(0, width, LANES)], axis=0
    ).astype(BF16)
    inside = matmul(pieces, upper)
    totals = matmul(pieces, jnp.ones((LANES, LANES), BF16))
    ahead = jnp.zeros((rows, LANES), F32)
    parts = []
    for k in range(width // LANES):
        parts.append(inside[k * rows : (k + 1) * rows] + ahead)
        ahead = ahead + totals[k * rows : (k + 1) * rows]
    return jnp.concatenate(parts, axis=1)


def pack_kernel(
    order_hbm, rows_hbm, inverse_hbm, basis_hbm, send_ref, slot_ref, real_ref, basis_ref,
    order_ref, rows_ref, chosen_ref, sem, *,
    devices, capacity,
):
    order_copy = fetch(order_hbm, order_ref, sem.at[0])
    rows_copy = fetch(rows_hbm, rows_ref, sem.at[1])
    basis_copy = fetch(basis_hbm.at[0], basis_ref, sem.at[2])
    real_copy = fetch(inverse_hbm.at[0, 0], real_ref, sem.at[3])
    leaf_rows = rows_ref.shape[0]
    order_copy.wait()
    order = order_ref[...]
    target = order // leaf_rows
    position = order - target * leaf_rows
    hits = (iota((devices, leaf_rows), 0) == target).astype(F32)
    rank = jnp.sum(hits * ranks(hits), axis=0, keepdims=True).astype(jnp.int32)
    slot_ref[...] = row_blocks((target * capacity + rank).astype(F32))
    group = LANES // capacity
    lane = rank + lax.rem(lax.axis_index("row") * lax.axis_size("col") + lax.axis_index("col"), group) * capacity
    high = position // CODE_BASE
    low = position - high * CODE_BASE
    codes = jnp.concatenate([hits * (high + 1).astype(F32), hits * low.astype(F32)], axis=0)
    places = (iota((LANES, leaf_rows), 0) == lane).astype(F32).astype(BF16)
    spread = matmul_nt(codes.astype(BF16), places)
    extra = (devices, EXTRA, LANES)
    send_ref[:, 2 * capacity :, :] = jnp.where(
        iota(extra, 1) < EXTRA // 2,
        jnp.broadcast_to(spread[:devices].reshape(devices, 1, LANES), extra),
        jnp.broadcast_to(spread[devices:].reshape(devices, 1, LANES), extra),
    ).astype(BF16)
    in_slot = (iota((capacity, leaf_rows), 0) == rank).astype(F32).astype(BF16)
    hits = hits.astype(BF16)
    for t in range(devices):
        chosen_ref[t * capacity : (t + 1) * capacity, :] = in_slot * hits[t : t + 1, :]
    rows_copy.wait()
    count = devices // PIECES
    for piece in range(PIECES):
        blocks = pl.ds(piece * count, count)
        sent = matmul(chosen_ref[pl.ds(piece * count * capacity, count * capacity), :], rows_ref[...])
        sent = sent.astype(BF16)
        send_ref[blocks, :capacity, :] = sent[:, :LANES].reshape(count, capacity, LANES)
        send_ref[blocks, capacity : 2 * capacity, :] = sent[:, LANES:].reshape(count, capacity, LANES)
    basis_copy.wait()
    real_copy.wait()


def codes_of(got_ref, devices, capacity):
    group = LANES // capacity
    extra = got_ref[:, 2 * capacity :, :].astype(F32)
    return [sum(extra[k + g] for g in range(group)) for k in range(0, devices, group)]


def load_kernel(after_ref, *refs, picks, turned, stores, rows_of, groups, kept, levels, height):
    refs = list(refs)

    def take(count):
        taken = refs[:count]
        del refs[:count]
        return taken

    count = len(picks)
    plain = count - turned
    gathers = 1 if rows_of else 0
    sources, stored, given = take(count), take(stores), take(2 * gathers)
    targets, held, gathered, early = take(count), take(stores), take(gathers), take(height > 0)
    scratch, chosen, landed = take(turned), take(gathers), take(rows_of == "lift")
    work, (sem,) = take(gathers and not kept), refs
    landing = targets[:plain] + scratch
    if landed:
        lift_copy = fetch(given[1].at[0], landed[0], sem.at[count + stores])

    bits = tree_bits(levels) if any(isinstance(one, tuple) for pick in picks for one in pick) else []

    def part(pick, rows):
        return tuple(
            pl.ds(pl.multiple_of(bits[one[1]] * rows, rows), rows) if isinstance(one, tuple) else one
            for one in pick
        )

    copies = [
        fetch(source.at[part(pick, target.shape[-2])], target, sem.at[k])
        for k, (source, target, pick) in enumerate(zip(sources, landing, picks))
    ]
    copies += [fetch(stored[k], held[k], sem.at[count + k]) for k in range(stores)]
    if rows_of:
        out_ref = gathered[0] if kept else work[0]
        (chosen_ref,) = chosen
        chosen_ref[...] = wide_one_hot(place_columns(given[0], groups), chosen_ref.shape[1] // LANES)
        if landed:
            lift_copy.wait()
            width = landed[0].shape[2]
            for part in range(2):
                columns = slice(part * width, (part + 1) * width)
                out_ref[:, columns] = matmul(chosen_ref[...], landed[0][part]).astype(BF16)
        else:
            out_ref[...] = folded(matmul(chosen_ref[...], given[1][...]))
        if not kept:
            copies.append(fetch(out_ref, gathered[0], sem.at[count + stores + 1]))
    if early:
        copies[0].wait()
        early[0][...] = half_product(targets[0], tree_bits(height)[-1], after_ref[...])
    for k in range(turned):
        copies[plain + k].wait()
        for part in range(2):
            targets[plain + k][part] = jnp.transpose(scratch[k][part])
    for k, copy in enumerate(copies):
        if not plain <= k < count and not (early and k == 0):
            copy.wait()


def half_product(inverse_ref, upper, half):
    rank = half.shape[0]
    columns = pl.ds(pl.multiple_of(upper * rank, rank), rank)
    return apply_complex(inverse_ref[0, :, columns], inverse_ref[1, :, columns], half, NODE_STEP)


def place_columns(place_ref, groups):
    turned = jnp.transpose(place_ref[...])
    return [
        (turned[:, k * EXTRA : k * EXTRA + 1] - 1.0) * CODE_BASE
        + turned[:, k * EXTRA + EXTRA // 2 : k * EXTRA + EXTRA // 2 + 1]
        for k in range(*groups)
    ]


def place_kernel(
    got_ref, inverse_hbm, basis_ref, placed_ref, place_ref, imag_ref, turned_ref, chosen_ref, rows_ref, sem, *,
    devices, capacity,
):
    imag_copy = fetch(inverse_hbm.at[0, 1], imag_ref, sem.at[0])
    leaf_rows = placed_ref.shape[0]
    codes = codes_of(got_ref, devices, capacity)
    place_ref[...] = jnp.concatenate(codes, axis=0)
    code = iota((CODE_BASE, LANES), 0).astype(F32)
    is_low = jnp.concatenate(
        [(code == one[EXTRA // 2 : EXTRA // 2 + 1]).astype(F32) for one in codes], axis=1
    ).astype(BF16)
    is_high = jnp.concatenate([(code == one[:1] - 1.0).astype(F32) for one in codes], axis=1).astype(BF16)
    for h in range(leaf_rows // CODE_BASE):
        chosen_ref[h * CODE_BASE : (h + 1) * CODE_BASE, :] = is_low * is_high[h : h + 1, :]
    slots = devices * capacity
    rows_ref[:, :LANES] = got_ref[:, :capacity, :].reshape(slots, LANES)
    rows_ref[:, LANES:] = got_ref[:, capacity : 2 * capacity, :].reshape(slots, LANES)
    placed_ref[...] = matmul(chosen_ref[...], rows_ref[...]).astype(BF16)
    for part in range(2):
        turned_ref[part] = jnp.transpose(basis_ref[part])
    imag_copy.wait()


def leaf_kernel(placed_ref, real_ref, imag_ref, inverse_hbm, parts_ref, inverse_ref, sem):
    copy = fetch(inverse_hbm.at[0, 0], inverse_ref, sem.at[0])
    placed = placed_ref[...]
    parts_ref[...] = two_parts(matmul(real_ref[...], placed) + matmul(imag_ref[...], rotated(placed)))
    copy.wait()


def coef_kernel(parts_ref, basis_ref, own_ref, other_ref):
    width = parts_ref.shape[1] // 2
    parts = parts_ref[...]
    turned = jnp.concatenate([rotated(parts[:, :width]), rotated(parts[:, width:])], axis=1)
    coef = folded(matmul(basis_ref[0], parts) + matmul(basis_ref[1], turned))
    first, second = swapped(coef[:, :LANES], coef[:, LANES:])
    odd = tree_bits(1)[0] == 1
    own_ref[...] = jnp.where(odd, second, first)
    other_ref[...] = jnp.where(odd, first, second)


def node_rhs(upper, own, partner):
    is_upper = upper == 1
    return jnp.concatenate(
        [jnp.where(is_upper, partner, own), jnp.where(is_upper, own, partner)], axis=0
    )


def node_kernel(own_ref, partner_ref, inverse_ref, basis_ref, sol_ref, coef_ref, code_ref, *, height):
    bit = tree_bits(height)[-1]
    if height == 1:
        rhs = node_rhs(bit, own_ref[...], partner_ref[...])
        sol = apply_complex(inverse_ref[0], inverse_ref[1], rhs, NODE_STEP)
    else:
        sol = own_ref[...] + half_product(inverse_ref, 1 - bit, decoded(partner_ref[...]))
    sol_ref[...] = sol
    coef = apply_complex(basis_ref[0], basis_ref[1], sol, NODE_STEP)
    coef_ref[...] = coef
    code_ref[...] = encoded(coef)


def descent_kernel(own_ref, partner_ref, inverse_ref, *refs, levels):
    below = levels - 1
    bits = tree_bits(levels)
    lifts, sols, coefs = refs[:below], refs[below : 2 * below], refs[2 * below : 3 * below]
    mine_ref, other_ref = refs[3 * below :]
    rank = own_ref.shape[0]
    down = own_ref[...] + half_product(inverse_ref, 1 - bits[below], decoded(partner_ref[...]))
    for k in range(below - 1, -1, -1):
        gap = coefs[k][...] - down
        if k == below - 1:
            sol = sols[k][pl.ds(pl.multiple_of(bits[k] * rank, rank), rank), :]
        else:
            sol = sols[k][...]
        down = sol - apply_complex(lifts[k][0], lifts[k][1], gap)
    swap = bits[0] == 1
    mine_ref[...] = jnp.where(swap, down[rank:], down[:rank])
    other_ref[...] = jnp.where(swap, down[:rank], down[rank:])


def rows_of(refs, rows):
    parts, at = [], 0
    for ref in refs:
        first, last = max(rows.start - at, 0), min(rows.stop - at, ref.shape[0])
        if first < last:
            parts.append(ref[first:last, :])
        at += ref.shape[0]
    return parts[0] if len(parts) == 1 else jnp.concatenate(parts, axis=0)


def finish_kernel(
    mine_ref, others_ref, own_ref, other_ref, *refs, devices, capacity
):
    *pieces, send_ref = refs
    moved, pieces = pieces[:2], pieces[2:]
    swap = tree_bits(1)[0] == 1
    mine = own_ref[...] - mine_ref[...]
    other = other_ref[...] - others_ref[...]
    first, second = swapped(jnp.where(swap, other, mine), jnp.where(swap, mine, other))
    gap = jnp.concatenate([first, second], axis=1)
    rank, width = gap.shape
    parts = jnp.concatenate([two_parts(gap), two_parts(rotated(gap))], axis=0)
    count = devices // FINISH_PIECES
    for at in range(0, devices, count):
        rows = slice(at * capacity, (at + count) * capacity)
        sol = rows_of(pieces, rows) - folded(matmul(rows_of(moved, rows), parts, NODE_STEP))
        code = scale_code(sol)
        level = to_int16(rounded(sol * inverse_unit_of(code)))
        blocks = slice(at, at + count)
        send_ref[blocks, :capacity, :] = level[:, :LANES].reshape(count, capacity, LANES)
        send_ref[blocks, capacity : 2 * capacity, :] = level[:, LANES:].reshape(count, capacity, LANES)
        extra = (EXTRA, LANES)
        extra = jnp.where(
            iota(extra, 0) < EXTRA // 2,
            jnp.broadcast_to(code[:, :LANES], extra),
            jnp.broadcast_to(code[:, LANES:], extra),
        )
        send_ref[blocks, 2 * capacity :, :] = jnp.broadcast_to(
            to_int16(extra).reshape(1, EXTRA, LANES), (count, EXTRA, LANES)
        )


def unpack_kernel(got_ref, slot_ref, out_hbm, out_ref, sem, *, devices, capacity):
    slots = devices * capacity
    turned = jnp.transpose(slot_ref[...])
    chosen = wide_one_hot([turned[:, k : k + 1] for k in range(turned.shape[1])], slots // LANES)
    extra = from_int16(got_ref[:, 2 * capacity :, :])
    unit = unit_of(extra)
    unit = jnp.concatenate([unit[:, :1, :], unit[:, EXTRA // 2 : EXTRA // 2 + 1, :]], axis=2)
    largest = jnp.max(unit, axis=0)
    inverse = 1.0 / largest
    highs, lows = [], []
    for half in range(2):
        lanes = slice(half * LANES, (half + 1) * LANES)
        level = from_int16(got_ref[:, half * capacity : (half + 1) * capacity, :])
        value = (level * unit[:, :, lanes]).reshape(slots, LANES)
        high = value.astype(BF16)
        highs.append(high)
        lows.append(((value - high.astype(F32)) * inverse[:, lanes]).astype(F8))
    high, low = jnp.concatenate(highs, axis=1), jnp.concatenate(lows, axis=1)
    count = out_ref.shape[0] // PIECES
    copies = []
    for piece in range(PIECES):
        rows = pl.ds(piece * count, count)
        some = chosen[piece * count : (piece + 1) * count]
        out_ref[rows, :] = whole_matmul(some, high) + whole_matmul(some.astype(F8), low) * largest
        copies.append(fetch(out_ref.at[rows], out_hbm.at[rows], sem.at[piece]))
    for copy in copies:
        copy.wait()


def call(kernel, outs, operands, scratch=(), vmem=24):
    specs = {
        "vmem": pl.BlockSpec(memory_space=pltpu.VMEM),
        "hbm": pl.BlockSpec(memory_space=pl.ANY),
        "any": pl.BlockSpec(memory_space=pl.ANY),
    }
    results = pl.pallas_call(
        kernel,
        out_shape=[pltpu.HBM(out.shape, out.dtype) if space == "hbm" else out for out, space in outs],
        in_specs=[specs[space] for _, space in operands],
        out_specs=[specs[space] for _, space in outs],
        scratch_shapes=[
            pltpu.SemaphoreType.DMA((one,)) if isinstance(one, int) else pltpu.VMEM(one.shape, one.dtype)
            for one in scratch
        ],
        compiler_params=pltpu.CompilerParams(vmem_limit_bytes=vmem * 2**20),
    )(
        *[
            pltpu.with_memory_space_constraint(array, pltpu.HBM) if space == "hbm" else array
            for array, space in operands
        ]
    )
    return results


def shape(dims, dtype=F32):
    return jax.ShapeDtypeStruct(dims, dtype)


def from_partner(shard, axis, apart):
    return lax.ppermute(shard, axis, [(i, i ^ 1 << apart) for i in range(lax.axis_size(axis))])


def per_device(
    right_sides, tree_order, leaf_inverse, leaf_basis, leaf_lift, node_inverse, node_basis, node_lift
):
    row_count = lax.axis_size("row")
    col_count = lax.axis_size("col")
    devices = row_count * col_count
    col_levels = col_count.bit_length() - 1
    levels = col_levels + row_count.bit_length() - 1
    leaf_rows, width = right_sides.shape
    rank = leaf_basis.shape[3]
    capacity = 2 * leaf_rows // min(devices, leaf_rows // 8)
    block = (devices, 2 * capacity + EXTRA, LANES)
    sizes = dict(devices=devices, capacity=capacity)
    def exchange(blocks):
        return lax.all_to_all(blocks, ("row", "col"), split_axis=0, concat_axis=0, tiled=True)

    def partner_of(shard, height):
        if height < col_levels:
            return from_partner(shard, "col", height)
        return from_partner(shard, "row", height - col_levels)

    send, slot, real, basis = call(
        functools.partial(pack_kernel, **sizes),
        [
            (shape(block, BF16), "vmem"),
            (shape((leaf_rows // LANES, LANES)), "vmem"),
            (shape(leaf_inverse.shape[2:], BF16), "vmem"),
            (shape(leaf_basis.shape[1:], BF16), "vmem"),
        ],
        [(tree_order.reshape(1, leaf_rows), "hbm"), (right_sides, "hbm")]
        + [(leaf_inverse, "hbm"), (leaf_basis, "hbm")],
        [
            shape((1, leaf_rows), jnp.int32),
            shape(right_sides.shape, BF16),
            shape((devices * capacity, leaf_rows), BF16),
            4,
        ],
    )
    slots = devices * capacity
    total = slots // LANES
    gathers = {
        levels - 3: ("sol", (0, total // 2), True),
        levels - 2: ("sol", (total // 2, total), True),
        levels - 1: ("lift", (0, 3 * total // 8), True),
        levels: ("lift", (3 * total // 8, total), True),
    }

    def load(after, weights, picks, turned=0, stores=(), gather=("", (0, 0), False), height=0):
        shapes = [
            jax.eval_shape(
                lambda w, pick=pick: w[tuple(slice(0, rank) if isinstance(p, tuple) else p for p in pick)], w
            )
            for w, pick in zip(weights, picks)
        ]
        plain = len(weights) - turned
        outs = [shape(one.shape, one.dtype) for one in shapes[:plain]]
        outs += [shape((2, one.shape[2], one.shape[1]), one.dtype) for one in shapes[plain:]]
        rows_of, groups, kept = gather
        rows = (groups[1] - groups[0]) * LANES
        taken = {
            "": [],
            "sol": [shape((rows, width))],
            "lift": [shape((rows, 2 * rank), BF16)],
        }[rows_of]
        given = {"": [], "sol": [(place, "vmem"), (parts, "vmem")], "lift": [(place, "vmem"), (leaf_lift, "hbm")]}
        work = [shape((rows, leaf_rows), BF16)] if rows_of else []
        work += [shape(leaf_lift.shape[1:], BF16)] if rows_of == "lift" else []
        work += [] if kept else taken
        return call(
            functools.partial(
                load_kernel,
                picks=picks,
                turned=turned,
                stores=len(stores),
                rows_of=rows_of,
                groups=groups,
                kept=kept,
                levels=levels,
                height=height,
            ),
            [(out, "vmem") for out in outs]
            + [(shape(one.shape), "hbm") for one in stores]
            + [(one, "vmem" if kept else "hbm") for one in taken]
            + ([(shape((shapes[0].shape[1], LANES)), "vmem")] if height else []),
            [(after, "vmem" if height else "any")]
            + [(weight, "hbm") for weight in weights]
            + [(one, "any") for one in stores]
            + given[rows_of],
            [shape(one.shape, one.dtype) for one in shapes[plain:]]
            + work
            + [len(weights) + len(stores) + 2 * bool(rows_of)],
            vmem=14 if rows_of else 6,
        )

    place = parts = None
    got = exchange(send)
    half = shape((rank, LANES))
    placed, place, imag, basis = call(
        functools.partial(place_kernel, **sizes),
        [
            (shape((leaf_rows, width), BF16), "vmem"),
            (shape((slots // LANES * EXTRA, LANES)), "vmem"),
            (shape(leaf_inverse.shape[2:], BF16), "vmem"),
            (shape((2, rank, leaf_rows), BF16), "vmem"),
        ],
        [(got, "vmem"), (leaf_inverse, "hbm"), (basis, "vmem")],
        [shape((leaf_rows, slots), BF16), shape((slots, width), BF16), 1],
    )
    parts, lowest = call(
        leaf_kernel,
        [(shape((leaf_rows, 2 * width), BF16), "vmem"), (shape(node_inverse.shape[2:], BF16), "vmem")],
        [(placed, "vmem"), (real, "vmem"), (imag, "vmem"), (node_inverse, "hbm")],
        [1],
    )
    own, other = call(
        coef_kernel,
        [(half, "vmem"), (half, "vmem")],
        [(parts, "vmem"), (basis, "vmem")],
    )
    leaf_own, leaf_other = own, other
    whole = shape((2 * rank, LANES))
    sols, stored, coefs, gathered = [], [], [], []
    no_gather = ("", (0, 0), False)
    for height in range(1, levels):
        partner = partner_of(other if height == 1 else code, height - 1)
        pick = (0, height - 1)
        first = height == 1
        loaded = load(
            own,
            (node_basis,) if first else (node_inverse, node_basis),
            (pick,) if first else (pick, pick),
            1,
            sols[-1:],
            gathers.get(height, no_gather),
            0 if first else height,
        )
        (inverse, basis, *kept) = (lowest, *loaded) if first else loaded
        early = own if first else kept.pop()
        stored += kept[: len(sols[-1:])]
        gathered += kept[len(sols[-1:]) :]
        sol, own, code = call(
            functools.partial(node_kernel, height=height),
            [(whole, "vmem"), (half, "vmem"), (shape((rank + TAIL, LANES), jnp.int16), "vmem")],
            [
                (early, "vmem"),
                (partner, "vmem"),
                (inverse, "vmem"),
                (basis, "vmem"),
            ],
            vmem=8,
        )
        sols.append(sol)
        coefs.append(own)
    partner = partner_of(code, levels - 1)
    loaded = load(
        own,
        (node_inverse, *(node_lift for _ in coefs), *stored),
        (
            (0, levels - 1, slice(None), ("half", levels - 1)),
            (0, 0),
            *((0, k, slice(None), ("half", k)) for k in range(1, levels - 1)),
            (),
            *((("half", k),) for k in range(1, levels - 2)),
        ),
        gather=gathers[levels],
        height=levels,
    )
    *loaded, early = loaded
    inverse, lifts, sols = loaded[0], loaded[1:levels], [*loaded[levels:-1], sols[-1]]
    gathered.append(loaded[-1])
    mine, other = call(
        functools.partial(descent_kernel, levels=levels),
        [
            (half, "vmem"),
            (half, "vmem"),
        ],
        [(early, "vmem"), (partner, "vmem"), (inverse, "vmem")]
        + [(lift, "vmem") for lift in lifts]
        + [(sol, "vmem") for sol in sols]
        + [(coef, "vmem") for coef in coefs],
        vmem=8,
    )
    other = partner_of(other, 0)
    bases = gathered[:2]
    (back,) = call(
        functools.partial(finish_kernel, **sizes),
        [(shape(block, jnp.int16), "vmem")],
        [
            (mine, "vmem"),
            (other, "vmem"),
            (leaf_own, "vmem"),
            (leaf_other, "vmem"),
            (gathered[2], "vmem"),
            (gathered[3], "vmem"),
        ]
        + [(one, "vmem") for one in bases],
    )
    returned = exchange(back)
    (result,) = call(
        functools.partial(unpack_kernel, **sizes),
        [(shape((leaf_rows, width)), "hbm")],
        [(returned, "vmem"), (slot, "vmem")],
        [shape((leaf_rows, width)), PIECES],
    )
    return result


def solution(mesh):
    in_specs = (
        P(("row", "col"), None),
        P(("row", "col")),
        P(("row", "col"), None, None, None),
        P(("row", "col"), None, None, None),
        P(("row", "col"), None, None, None),
        P(("row", "col"), None, None, None, None),
        P(("row", "col"), None, None, None, None),
        P(("row", "col"), None, None, None, None),
    )
    out_specs = P(("row", "col"), None)
    return jax.shard_map(
        per_device, mesh=mesh, in_specs=in_specs, out_specs=out_specs, check_vma=False
    )
```

```python
import functools

import jax
import jax.numpy as jnp
from jax import lax
from jax.experimental import pallas as pl
from jax.experimental.pallas import tpu as pltpu
from jax.sharding import PartitionSpec as P

LANES = 128
EXTRA = 8
CODE_BASE = 32
SCALE_STEPS = 64
HEADROOM = 1.002
ROUNDER = 1.5 * 2.0**23
TAIL = 16
STEP = 256
PIECES = 8
NODE_STEP = 128
FINISH_PIECES = 8
BF16 = jnp.bfloat16
F32 = jnp.float32
F8 = jnp.float8_e4m3fn


def whole_matmul(a, b):
    return lax.dot_general(a, b, (((1,), (0,)), ((), ())), preferred_element_type=F32)


def matmul(a, b, step=STEP):
    pieces = [whole_matmul(a[at : at + step], b) for at in range(0, a.shape[0], step)]
    return pieces[0] if len(pieces) == 1 else jnp.concatenate(pieces, axis=0)


def matmul_nt(a, b):
    return lax.dot_general(a, b, (((1,), (1,)), ((), ())), preferred_element_type=F32)


def tree_bits(levels):
    index = lax.axis_index("row") * lax.axis_size("col") + lax.axis_index("col")
    return [index >> height & 1 for height in range(levels)]


def iota(shape, dim):
    return lax.broadcasted_iota(jnp.int32, shape, dim)


def rotated(x):
    if x.shape[1] == LANES:
        turned = pltpu.roll(x, LANES // 2, 1)
        return jnp.where(iota(x.shape, 1) < LANES // 2, -turned, turned)
    return jnp.concatenate([-x[:, LANES:], x[:, :LANES]], axis=1)


def swapped(first, second):
    low = iota(first.shape, 1) < LANES // 2
    return (
        jnp.where(low, first, pltpu.roll(second, LANES // 2, 1)),
        jnp.where(low, pltpu.roll(first, LANES // 2, 1), second),
    )


def two_parts(x):
    high = x.astype(BF16)
    low = (x - high.astype(F32)).astype(BF16)
    return jnp.concatenate([high, low], axis=1)


def folded(both):
    width = both.shape[1] // 2
    return both[:, :width] + both[:, width:]


def apply_complex(real, imag, x, step=STEP):
    both = jnp.concatenate([two_parts(x), two_parts(rotated(x))], axis=0)
    return folded(matmul(jnp.concatenate([real, imag], axis=1), both, step))


def unit_of(code):
    return jnp.exp2(code * (1.0 / SCALE_STEPS) - 15.0) * HEADROOM


def inverse_unit_of(code):
    return jnp.exp2(15.0 - code * (1.0 / SCALE_STEPS)) * (1.0 / HEADROOM)


def rounded(x):
    return (x + ROUNDER) - ROUNDER


def to_int16(x):
    return x.astype(jnp.int32).astype(jnp.int16)


def from_int16(x):
    return x.astype(jnp.int32).astype(F32)


def encoded(x):
    code = scale_code(x)
    level = rounded(x * inverse_unit_of(code))
    return to_int16(jnp.concatenate([level, jnp.broadcast_to(code, (TAIL, LANES))], axis=0))


def decoded(levels):
    values = from_int16(levels)
    return values[:-TAIL] * unit_of(values[-TAIL : 1 - TAIL])


def scale_code(x):
    largest = jnp.max(jnp.abs(x), axis=0, keepdims=True)
    return jnp.ceil(jnp.log2(jnp.maximum(largest, 2.0**-110)) * SCALE_STEPS)


def fetch(source, target, sem):
    copy = pltpu.make_async_copy(source, target, sem)
    copy.start()
    return copy


def wide_one_hot(columns, blocks):
    lane = iota((LANES, LANES), 1).astype(F32)
    one, zero = jnp.ones((), BF16), jnp.zeros((), BF16)
    names = []
    for entry in columns:
        block = jnp.floor(entry * (1.0 / LANES))
        names.append(jnp.where(lane == entry - block * LANES, block, -1.0))
    names = jnp.concatenate(names, axis=0).astype(BF16)
    return jnp.concatenate([jnp.where(names == jnp.array(g, BF16), one, zero) for g in range(blocks)], axis=1)


def row_blocks(x):
    return jnp.concatenate([x[:, at : at + LANES] for at in range(0, x.shape[1], LANES)], axis=0)


def ranks(hits):
    rows, width = hits.shape
    upper = (iota((LANES, LANES), 0) < iota((LANES, LANES), 1)).astype(F32).astype(BF16)
    pieces = jnp.concatenate(
        [hits[:, at : at + LANES] for at in range(0, width, LANES)], axis=0
    ).astype(BF16)
    inside = matmul(pieces, upper)
    totals = matmul(pieces, jnp.ones((LANES, LANES), BF16))
    ahead = jnp.zeros((rows, LANES), F32)
    parts = []
    for k in range(width // LANES):
        parts.append(inside[k * rows : (k + 1) * rows] + ahead)
        ahead = ahead + totals[k * rows : (k + 1) * rows]
    return jnp.concatenate(parts, axis=1)


def pack_kernel(
    order_hbm, rows_hbm, inverse_hbm, basis_hbm, send_ref, slot_ref, real_ref, basis_ref,
    order_ref, rows_ref, chosen_ref, sem, *,
    devices, capacity,
):
    order_copy = fetch(order_hbm, order_ref, sem.at[0])
    rows_copy = fetch(rows_hbm, rows_ref, sem.at[1])
    basis_copy = fetch(basis_hbm.at[0], basis_ref, sem.at[2])
    real_copy = fetch(inverse_hbm.at[0, 0], real_ref, sem.at[3])
    leaf_rows = rows_ref.shape[0]
    order_copy.wait()
    order = order_ref[...]
    target = order // leaf_rows
    position = order - target * leaf_rows
    hits = (iota((devices, leaf_rows), 0) == target).astype(F32)
    rank = jnp.sum(hits * ranks(hits), axis=0, keepdims=True).astype(jnp.int32)
    slot_ref[...] = row_blocks((target * capacity + rank).astype(F32))
    group = LANES // capacity
    lane = rank + lax.rem(lax.axis_index("row") * lax.axis_size("col") + lax.axis_index("col"), group) * capacity
    high = position // CODE_BASE
    low = position - high * CODE_BASE
    codes = jnp.concatenate([hits * (high + 1).astype(F32), hits * low.astype(F32)], axis=0)
    places = (iota((LANES, leaf_rows), 0) == lane).astype(F32).astype(BF16)
    spread = matmul_nt(codes.astype(BF16), places)
    extra = (devices, EXTRA, LANES)
    send_ref[:, 2 * capacity :, :] = jnp.where(
        iota(extra, 1) < EXTRA // 2,
        jnp.broadcast_to(spread[:devices].reshape(devices, 1, LANES), extra),
        jnp.broadcast_to(spread[devices:].reshape(devices, 1, LANES), extra),
    ).astype(BF16)
    in_slot = (iota((capacity, leaf_rows), 0) == rank).astype(F32).astype(BF16)
    hits = hits.astype(BF16)
    for t in range(devices):
        chosen_ref[t * capacity : (t + 1) * capacity, :] = in_slot * hits[t : t + 1, :]
    rows_copy.wait()
    count = devices // PIECES
    for piece in range(PIECES):
        blocks = pl.ds(piece * count, count)
        sent = matmul(chosen_ref[pl.ds(piece * count * capacity, count * capacity), :], rows_ref[...])
        sent = sent.astype(BF16)
        send_ref[blocks, :capacity, :] = sent[:, :LANES].reshape(count, capacity, LANES)
        send_ref[blocks, capacity : 2 * capacity, :] = sent[:, LANES:].reshape(count, capacity, LANES)
    basis_copy.wait()
    real_copy.wait()


def codes_of(got_ref, devices, capacity):
    group = LANES // capacity
    extra = got_ref[:, 2 * capacity :, :].astype(F32)
    return [sum(extra[k + g] for g in range(group)) for k in range(0, devices, group)]


def load_kernel(after_ref, *refs, picks, turned, stores, rows_of, groups, kept, levels, height):
    refs = list(refs)

    def take(count):
        taken = refs[:count]
        del refs[:count]
        return taken

    count = len(picks)
    plain = count - turned
    gathers = 1 if rows_of else 0
    sources, stored, given = take(count), take(stores), take(2 * gathers)
    targets, held, gathered, early = take(count), take(stores), take(gathers), take(height > 0)
    scratch, chosen, landed = take(turned), take(gathers), take(rows_of == "lift")
    work, (sem,) = take(gathers and not kept), refs
    landing = targets[:plain] + scratch
    if landed:
        lift_copy = fetch(given[1].at[0], landed[0], sem.at[count + stores])

    bits = tree_bits(levels) if any(isinstance(one, tuple) for pick in picks for one in pick) else []

    def part(pick, rows):
        return tuple(
            pl.ds(pl.multiple_of(bits[one[1]] * rows, rows), rows) if isinstance(one, tuple) else one
            for one in pick
        )

    copies = [
        fetch(source.at[part(pick, target.shape[-2])], target, sem.at[k])
        for k, (source, target, pick) in enumerate(zip(sources, landing, picks))
    ]
    copies += [fetch(stored[k], held[k], sem.at[count + k]) for k in range(stores)]
    if rows_of:
        out_ref = gathered[0] if kept else work[0]
        (chosen_ref,) = chosen
        chosen_ref[...] = wide_one_hot(place_columns(given[0], groups), chosen_ref.shape[1] // LANES)
        if landed:
            lift_copy.wait()
            width = landed[0].shape[2]
            for part in range(2):
                columns = slice(part * width, (part + 1) * width)
                out_ref[:, columns] = matmul(chosen_ref[...], landed[0][part]).astype(BF16)
        else:
            out_ref[...] = folded(matmul(chosen_ref[...], given[1][...]))
        if not kept:
            copies.append(fetch(out_ref, gathered[0], sem.at[count + stores + 1]))
    if early:
        copies[0].wait()
        early[0][...] = half_product(targets[0], tree_bits(height)[-1], after_ref[...])
    for k in range(turned):
        copies[plain + k].wait()
        for part in range(2):
            targets[plain + k][part] = jnp.transpose(scratch[k][part])
    for k, copy in enumerate(copies):
        if not plain <= k < count and not (early and k == 0):
            copy.wait()


def half_product(inverse_ref, upper, half):
    rank = half.shape[0]
    columns = pl.ds(pl.multiple_of(upper * rank, rank), rank)
    return apply_complex(inverse_ref[0, :, columns], inverse_ref[1, :, columns], half, NODE_STEP)


def place_columns(place_ref, groups):
    turned = jnp.transpose(place_ref[...])
    return [
        (turned[:, k * EXTRA : k * EXTRA + 1] - 1.0) * CODE_BASE
        + turned[:, k * EXTRA + EXTRA // 2 : k * EXTRA + EXTRA // 2 + 1]
        for k in range(*groups)
    ]


def place_kernel(
    got_ref, inverse_hbm, basis_ref, placed_ref, place_ref, imag_ref, turned_ref, chosen_ref, rows_ref, sem, *,
    devices, capacity,
):
    imag_copy = fetch(inverse_hbm.at[0, 1], imag_ref, sem.at[0])
    leaf_rows = placed_ref.shape[0]
    codes = codes_of(got_ref, devices, capacity)
    place_ref[...] = jnp.concatenate(codes, axis=0)
    code = iota((CODE_BASE, LANES), 0).astype(F32)
    is_low = jnp.concatenate(
        [(code == one[EXTRA // 2 : EXTRA // 2 + 1]).astype(F32) for one in codes], axis=1
    ).astype(BF16)
    is_high = jnp.concatenate([(code == one[:1] - 1.0).astype(F32) for one in codes], axis=1).astype(BF16)
    for h in range(leaf_rows // CODE_BASE):
        chosen_ref[h * CODE_BASE : (h + 1) * CODE_BASE, :] = is_low * is_high[h : h + 1, :]
    slots = devices * capacity
    rows_ref[:, :LANES] = got_ref[:, :capacity, :].reshape(slots, LANES)
    rows_ref[:, LANES:] = got_ref[:, capacity : 2 * capacity, :].reshape(slots, LANES)
    placed_ref[...] = matmul(chosen_ref[...], rows_ref[...]).astype(BF16)
    for part in range(2):
        turned_ref[part] = jnp.transpose(basis_ref[part])
    imag_copy.wait()


def leaf_kernel(placed_ref, real_ref, imag_ref, inverse_hbm, parts_ref, inverse_ref, sem):
    copy = fetch(inverse_hbm.at[0, 0], inverse_ref, sem.at[0])
    placed = placed_ref[...]
    parts_ref[...] = two_parts(matmul(real_ref[...], placed) + matmul(imag_ref[...], rotated(placed)))
    copy.wait()


def coef_kernel(parts_ref, basis_ref, own_ref, other_ref):
    width = parts_ref.shape[1] // 2
    parts = parts_ref[...]
    turned = jnp.concatenate([rotated(parts[:, :width]), rotated(parts[:, width:])], axis=1)
    coef = folded(matmul(basis_ref[0], parts) + matmul(basis_ref[1], turned))
    first, second = swapped(coef[:, :LANES], coef[:, LANES:])
    odd = tree_bits(1)[0] == 1
    own_ref[...] = jnp.where(odd, second, first)
    other_ref[...] = jnp.where(odd, first, second)


def node_rhs(upper, own, partner):
    is_upper = upper == 1
    return jnp.concatenate(
        [jnp.where(is_upper, partner, own), jnp.where(is_upper, own, partner)], axis=0
    )


def node_kernel(own_ref, partner_ref, inverse_ref, basis_ref, sol_ref, coef_ref, code_ref, *, height):
    bit = tree_bits(height)[-1]
    if height == 1:
        rhs = node_rhs(bit, own_ref[...], partner_ref[...])
        sol = apply_complex(inverse_ref[0], inverse_ref[1], rhs, NODE_STEP)
    else:
        sol = own_ref[...] + half_product(inverse_ref, 1 - bit, decoded(partner_ref[...]))
    sol_ref[...] = sol
    coef = apply_complex(basis_ref[0], basis_ref[1], sol, NODE_STEP)
    coef_ref[...] = coef
    code_ref[...] = encoded(coef)


def descent_kernel(own_ref, partner_ref, inverse_ref, *refs, levels):
    below = levels - 1
    bits = tree_bits(levels)
    lifts, sols, coefs = refs[:below], refs[below : 2 * below], refs[2 * below : 3 * below]
    mine_ref, other_ref = refs[3 * below :]
    rank = own_ref.shape[0]
    down = own_ref[...] + half_product(inverse_ref, 1 - bits[below], decoded(partner_ref[...]))
    for k in range(below - 1, -1, -1):
        gap = coefs[k][...] - down
        if k == below - 1:
            sol = sols[k][pl.ds(pl.multiple_of(bits[k] * rank, rank), rank), :]
        else:
            sol = sols[k][...]
        down = sol - apply_complex(lifts[k][0], lifts[k][1], gap)
    swap = bits[0] == 1
    mine_ref[...] = jnp.where(swap, down[rank:], down[:rank])
    other_ref[...] = jnp.where(swap, down[:rank], down[rank:])


def rows_of(refs, rows):
    parts, at = [], 0
    for ref in refs:
        first, last = max(rows.start - at, 0), min(rows.stop - at, ref.shape[0])
        if first < last:
            parts.append(ref[first:last, :])
        at += ref.shape[0]
    return parts[0] if len(parts) == 1 else jnp.concatenate(parts, axis=0)


def finish_kernel(
    mine_ref, others_ref, own_ref, other_ref, *refs, devices, capacity
):
    *pieces, send_ref = refs
    moved, pieces = pieces[:2], pieces[2:]
    swap = tree_bits(1)[0] == 1
    mine = own_ref[...] - mine_ref[...]
    other = other_ref[...] - others_ref[...]
    first, second = swapped(jnp.where(swap, other, mine), jnp.where(swap, mine, other))
    gap = jnp.concatenate([first, second], axis=1)
    rank, width = gap.shape
    parts = jnp.concatenate([two_parts(gap), two_parts(rotated(gap))], axis=0)
    count = devices // FINISH_PIECES
    for at in range(0, devices, count):
        rows = slice(at * capacity, (at + count) * capacity)
        sol = rows_of(pieces, rows) - folded(matmul(rows_of(moved, rows), parts, NODE_STEP))
        code = scale_code(sol)
        level = to_int16(rounded(sol * inverse_unit_of(code)))
        blocks = slice(at, at + count)
        send_ref[blocks, :capacity, :] = level[:, :LANES].reshape(count, capacity, LANES)
        send_ref[blocks, capacity : 2 * capacity, :] = level[:, LANES:].reshape(count, capacity, LANES)
        extra = (EXTRA, LANES)
        extra = jnp.where(
            iota(extra, 0) < EXTRA // 2,
            jnp.broadcast_to(code[:, :LANES], extra),
            jnp.broadcast_to(code[:, LANES:], extra),
        )
        send_ref[blocks, 2 * capacity :, :] = jnp.broadcast_to(
            to_int16(extra).reshape(1, EXTRA, LANES), (count, EXTRA, LANES)
        )


def unpack_kernel(got_ref, slot_ref, out_hbm, out_ref, sem, *, devices, capacity):
    slots = devices * capacity
    turned = jnp.transpose(slot_ref[...])
    chosen = wide_one_hot([turned[:, k : k + 1] for k in range(turned.shape[1])], slots // LANES)
    extra = from_int16(got_ref[:, 2 * capacity :, :])
    unit = unit_of(extra)
    unit = jnp.concatenate([unit[:, :1, :], unit[:, EXTRA // 2 : EXTRA // 2 + 1, :]], axis=2)
    largest = jnp.max(unit, axis=0)
    inverse = 1.0 / largest
    highs, lows = [], []
    for half in range(2):
        lanes = slice(half * LANES, (half + 1) * LANES)
        level = from_int16(got_ref[:, half * capacity : (half + 1) * capacity, :])
        value = (level * unit[:, :, lanes]).reshape(slots, LANES)
        high = value.astype(BF16)
        highs.append(high)
        lows.append(((value - high.astype(F32)) * inverse[:, lanes]).astype(F8))
    high, low = jnp.concatenate(highs, axis=1), jnp.concatenate(lows, axis=1)
    count = out_ref.shape[0] // PIECES
    copies = []
    for piece in range(PIECES):
        rows = pl.ds(piece * count, count)
        some = chosen[piece * count : (piece + 1) * count]
        out_ref[rows, :] = whole_matmul(some, high) + whole_matmul(some.astype(F8), low) * largest
        copies.append(fetch(out_ref.at[rows], out_hbm.at[rows], sem.at[piece]))
    for copy in copies:
        copy.wait()


def call(kernel, outs, operands, scratch=(), vmem=24):
    specs = {
        "vmem": pl.BlockSpec(memory_space=pltpu.VMEM),
        "hbm": pl.BlockSpec(memory_space=pl.ANY),
        "any": pl.BlockSpec(memory_space=pl.ANY),
    }
    results = pl.pallas_call(
        kernel,
        out_shape=[pltpu.HBM(out.shape, out.dtype) if space == "hbm" else out for out, space in outs],
        in_specs=[specs[space] for _, space in operands],
        out_specs=[specs[space] for _, space in outs],
        scratch_shapes=[
            pltpu.SemaphoreType.DMA((one,)) if isinstance(one, int) else pltpu.VMEM(one.shape, one.dtype)
            for one in scratch
        ],
        compiler_params=pltpu.CompilerParams(vmem_limit_bytes=vmem * 2**20),
    )(
        *[
            pltpu.with_memory_space_constraint(array, pltpu.HBM) if space == "hbm" else array
            for array, space in operands
        ]
    )
    return results


def shape(dims, dtype=F32):
    return jax.ShapeDtypeStruct(dims, dtype)


def from_partner(shard, axis, apart):
    return lax.ppermute(shard, axis, [(i, i ^ 1 << apart) for i in range(lax.axis_size(axis))])


def per_device(
    right_sides, tree_order, leaf_inverse, leaf_basis, leaf_lift, node_inverse, node_basis, node_lift
):
    row_count = lax.axis_size("row")
    col_count = lax.axis_size("col")
    devices = row_count * col_count
    col_levels = col_count.bit_length() - 1
    levels = col_levels + row_count.bit_length() - 1
    leaf_rows, width = right_sides.shape
    rank = leaf_basis.shape[3]
    capacity = 2 * leaf_rows // min(devices, leaf_rows // 8)
    block = (devices, 2 * capacity + EXTRA, LANES)
    sizes = dict(devices=devices, capacity=capacity)
    def exchange(blocks):
        return lax.all_to_all(blocks, ("row", "col"), split_axis=0, concat_axis=0, tiled=True)

    def partner_of(shard, height):
        if height < col_levels:
            return from_partner(shard, "col", height)
        return from_partner(shard, "row", height - col_levels)

    send, slot, real, basis = call(
        functools.partial(pack_kernel, **sizes),
        [
            (shape(block, BF16), "vmem"),
            (shape((leaf_rows // LANES, LANES)), "vmem"),
            (shape(leaf_inverse.shape[2:], BF16), "vmem"),
            (shape(leaf_basis.shape[1:], BF16), "vmem"),
        ],
        [(tree_order.reshape(1, leaf_rows), "hbm"), (right_sides, "hbm")]
        + [(leaf_inverse, "hbm"), (leaf_basis, "hbm")],
        [
            shape((1, leaf_rows), jnp.int32),
            shape(right_sides.shape, BF16),
            shape((devices * capacity, leaf_rows), BF16),
            4,
        ],
    )
    slots = devices * capacity
    total = slots // LANES
    gathers = {
        levels - 3: ("sol", (0, total // 2), True),
        levels - 2: ("sol", (total // 2, total), True),
        levels - 1: ("lift", (0, 3 * total // 8), True),
        levels: ("lift", (3 * total // 8, total), True),
    }

    def load(after, weights, picks, turned=0, stores=(), gather=("", (0, 0), False), height=0):
        shapes = [
            jax.eval_shape(
                lambda w, pick=pick: w[tuple(slice(0, rank) if isinstance(p, tuple) else p for p in pick)], w
            )
            for w, pick in zip(weights, picks)
        ]
        plain = len(weights) - turned
        outs = [shape(one.shape, one.dtype) for one in shapes[:plain]]
        outs += [shape((2, one.shape[2], one.shape[1]), one.dtype) for one in shapes[plain:]]
        rows_of, groups, kept = gather
        rows = (groups[1] - groups[0]) * LANES
        taken = {
            "": [],
            "sol": [shape((rows, width))],
            "lift": [shape((rows, 2 * rank), BF16)],
        }[rows_of]
        given = {"": [], "sol": [(place, "vmem"), (parts, "vmem")], "lift": [(place, "vmem"), (leaf_lift, "hbm")]}
        work = [shape((rows, leaf_rows), BF16)] if rows_of else []
        work += [shape(leaf_lift.shape[1:], BF16)] if rows_of == "lift" else []
        work += [] if kept else taken
        return call(
            functools.partial(
                load_kernel,
                picks=picks,
                turned=turned,
                stores=len(stores),
                rows_of=rows_of,
                groups=groups,
                kept=kept,
                levels=levels,
                height=height,
            ),
            [(out, "vmem") for out in outs]
            + [(shape(one.shape), "hbm") for one in stores]
            + [(one, "vmem" if kept else "hbm") for one in taken]
            + ([(shape((shapes[0].shape[1], LANES)), "vmem")] if height else []),
            [(after, "vmem" if height else "any")]
            + [(weight, "hbm") for weight in weights]
            + [(one, "any") for one in stores]
            + given[rows_of],
            [shape(one.shape, one.dtype) for one in shapes[plain:]]
            + work
            + [len(weights) + len(stores) + 2 * bool(rows_of)],
            vmem=14 if rows_of else 6,
        )

    place = parts = None
    got = exchange(send)
    half = shape((rank, LANES))
    placed, place, imag, basis = call(
        functools.partial(place_kernel, **sizes),
        [
            (shape((leaf_rows, width), BF16), "vmem"),
            (shape((slots // LANES * EXTRA, LANES)), "vmem"),
            (shape(leaf_inverse.shape[2:], BF16), "vmem"),
            (shape((2, rank, leaf_rows), BF16), "vmem"),
        ],
        [(got, "vmem"), (leaf_inverse, "hbm"), (basis, "vmem")],
        [shape((leaf_rows, slots), BF16), shape((slots, width), BF16), 1],
    )
    parts, lowest = call(
        leaf_kernel,
        [(shape((leaf_rows, 2 * width), BF16), "vmem"), (shape(node_inverse.shape[2:], BF16), "vmem")],
        [(placed, "vmem"), (real, "vmem"), (imag, "vmem"), (node_inverse, "hbm")],
        [1],
    )
    own, other = call(
        coef_kernel,
        [(half, "vmem"), (half, "vmem")],
        [(parts, "vmem"), (basis, "vmem")],
    )
    leaf_own, leaf_other = own, other
    whole = shape((2 * rank, LANES))
    sols, stored, coefs, gathered = [], [], [], []
    no_gather = ("", (0, 0), False)
    for height in range(1, levels):
        partner = partner_of(other if height == 1 else code, height - 1)
        pick = (0, height - 1)
        first = height == 1
        loaded = load(
            own,
            (node_basis,) if first else (node_inverse, node_basis),
            (pick,) if first else (pick, pick),
            1,
            sols[-1:],
            gathers.get(height, no_gather),
            0 if first else height,
        )
        (inverse, basis, *kept) = (lowest, *loaded) if first else loaded
        early = own if first else kept.pop()
        stored += kept[: len(sols[-1:])]
        gathered += kept[len(sols[-1:]) :]
        sol, own, code = call(
            functools.partial(node_kernel, height=height),
            [(whole, "vmem"), (half, "vmem"), (shape((rank + TAIL, LANES), jnp.int16), "vmem")],
            [
                (early, "vmem"),
                (partner, "vmem"),
                (inverse, "vmem"),
                (basis, "vmem"),
            ],
            vmem=8,
        )
        sols.append(sol)
        coefs.append(own)
    partner = partner_of(code, levels - 1)
    loaded = load(
        own,
        (node_inverse, *(node_lift for _ in coefs), *stored),
        (
            (0, levels - 1, slice(None), ("half", levels - 1)),
            (0, 0),
            *((0, k, slice(None), ("half", k)) for k in range(1, levels - 1)),
            (),
            *((("half", k),) for k in range(1, levels - 2)),
        ),
        gather=gathers[levels],
        height=levels,
    )
    *loaded, early = loaded
    inverse, lifts, sols = loaded[0], loaded[1:levels], [*loaded[levels:-1], sols[-1]]
    gathered.append(loaded[-1])
    mine, other = call(
        functools.partial(descent_kernel, levels=levels),
        [
            (half, "vmem"),
            (half, "vmem"),
        ],
        [(early, "vmem"), (partner, "vmem"), (inverse, "vmem")]
        + [(lift, "vmem") for lift in lifts]
        + [(sol, "vmem") for sol in sols]
        + [(coef, "vmem") for coef in coefs],
        vmem=8,
    )
    other = partner_of(other, 0)
    bases = gathered[:2]
    (back,) = call(
        functools.partial(finish_kernel, **sizes),
        [(shape(block, jnp.int16), "vmem")],
        [
            (mine, "vmem"),
            (other, "vmem"),
            (leaf_own, "vmem"),
            (leaf_other, "vmem"),
            (gathered[2], "vmem"),
            (gathered[3], "vmem"),
        ]
        + [(one, "vmem") for one in bases],
    )
    returned = exchange(back)
    (result,) = call(
        functools.partial(unpack_kernel, **sizes),
        [(shape((leaf_rows, width)), "hbm")],
        [(returned, "vmem"), (slot, "vmem")],
        [shape((leaf_rows, width)), PIECES],
    )
    return result


def solution(mesh):
    in_specs = (
        P(("row", "col"), None),
        P(("row", "col")),
        P(("row", "col"), None, None, None),
        P(("row", "col"), None, None, None),
        P(("row", "col"), None, None, None),
        P(("row", "col"), None, None, None, None),
        P(("row", "col"), None, None, None, None),
        P(("row", "col"), None, None, None, None),
    )
    out_specs = P(("row", "col"), None)
    return jax.shard_map(
        per_device, mesh=mesh, in_specs=in_specs, out_specs=out_specs, check_vma=False
    )
```
